1024 devices in a mesh: gx: 64 (over z, y), gy: 8 (over x), gz: 2 (over core).
Axes of the slice: x: 8, y: 8, z: 8, core: 2. Of those that a mesh axis runs over, the one named last changes fastest.
Arguments:
- fine_rhs: float32 [32768, 8, 64], P(('gx', 'gy', 'gz')), may hold values from -15 to 15
- fine_coef: bfloat16 [32768, 8, 64], P(('gx', 'gy', 'gz')), may hold values from 0.25 to 2
- coarse_rhs: float32 [512, 128, 256], P('gx', 'gy', 'gz'), may hold values from -15 to 15
- coarse_coef: bfloat16 [512, 128, 256], P('gx', 'gy', 'gz'), may hold values from 0.25 to 2
- patch_count: int32 [1024], P(('gx', 'gy', 'gz')), may hold values from 1 to 32, as said below
- patch_target: int32 [32768], P(('gx', 'gy', 'gz')), may hold values from 0 to 4095, as said below
Outputs:
- fine_solution: float32 [32768, 8, 64], P(('gx', 'gy', 'gz'))
- coarse_solution: float32 [512, 128, 256], P('gx', 'gy', 'gz')
- deep_solution: float32 [64, 16, 32], P('gx', 'gy', 'gz')
The draws below stay inside these ranges and needn't reach their ends.
Inputs may be any that keep to these rules, and one draw needn't show every extreme that they name: A device's live patches fill its slots 0 to patch_count - 1; in every gx slab some device has all 32 slots live. `patch_target`: A target is owner * 256 + local block, owner being the gy+gz index of a device in the holder's gx slab. The targets of all slots of one gx slab differ. At most 2 slots of one device name one owner, and a device with all slots live names every owner exactly 2 times.
All inputs are finite; a program needn't handle non-finite values.
Results may differ from the reference program's by a relative error of at most 0.0003.
Values may be sent and summed in bfloat16 or wider, within the bound.
No kernel may reach another device: no remote copies, remote signals or barrier semaphores. Data moves between devices by JAX's collectives and lax.ppermute only.
A program may use at most 128 MiB of HBM per device.

```python
import math
import jax
import jax.numpy as jnp
from jax import lax

CX = 8
CY = 16
CZ = 128
PS = 8
CAP = 2
DEEP = 3
B = 4
SLOTS = 32
BLOCKS_DEV = 256
PATCHES = 32768
X = 512
Y = 128
Z = 256
N_GY = 8
N_GZ = 2
DEVICES = 1024


def draw_patch_count(key, part):
    groups = N_GY * N_GZ
    key_first, key_second, key_pick = jax.random.split(key, 3)
    draw_first = jax.random.randint(key_first, (DEVICES,), 0, SLOTS + 1)
    draw_second = jax.random.randint(key_second, (DEVICES,), 0, SLOTS + 1)
    counts = jnp.maximum(1, draw_first * draw_second // SLOTS)
    picked = jax.random.randint(key_pick, (DEVICES // groups,), 0, groups)
    device_ids = lax.iota(jnp.int32, DEVICES)
    full_mask = device_ids % groups == jnp.repeat(picked, groups)
    return jnp.where(full_mask, SLOTS, counts).astype(jnp.int32)


def draw_patch_target(key, part):
    groups = N_GY * N_GZ
    slab_count = DEVICES // groups
    key_owner, key_block = jax.random.split(key)
    owner_scores = jax.random.randint(key_owner, (DEVICES, groups), 0, 1 << 20) * groups + lax.iota(jnp.int32, groups)[None, :]
    owner_perm = jnp.argsort(owner_scores, axis=1, stable=True).astype(jnp.int32)
    block_scores = jax.random.randint(key_block, (slab_count * groups, BLOCKS_DEV), 0, 1 << 16) * BLOCKS_DEV + lax.iota(jnp.int32, BLOCKS_DEV)[None, :]
    block_perm = jnp.argsort(block_scores, axis=1, stable=True).astype(jnp.int32)
    slot_ids = lax.iota(jnp.int32, SLOTS)
    owners = owner_perm[:, slot_ids % groups]
    rounds = slot_ids // groups
    device_ids = lax.iota(jnp.int32, DEVICES)
    row_ids = (device_ids // groups)[:, None] * groups + owners
    col_ids = (device_ids % groups)[:, None] * CAP + rounds[None, :]
    local_blocks = block_perm[row_ids, col_ids]
    return (owners * BLOCKS_DEV + local_blocks).reshape(DEVICES * SLOTS).astype(jnp.int32)


def block_levels(own_key, shape, shards, low, high):
    def one(dim, blocks):
        draws = jax.random.uniform(jax.random.fold_in(jax.random.fold_in(own_key, 6), dim), (blocks,), jnp.float32, low / len(shards), high / len(shards))
        return jnp.repeat(jnp.exp(draws), shape[dim] // blocks).reshape((-1,) + (1,) * (len(shape) - dim - 1))

    level = one(*shards[0])
    for cut in shards[1:]:
        level = level * one(*cut)
    return level


def centred(own_key, shape, scale, reach, shards=(), kind=jnp.bfloat16):
    loudness = block_levels(own_key, shape, shards, -0.22, 0.18) if shards else 1.0
    values = jax.random.normal(own_key, shape, jnp.float32) * scale * loudness
    return jnp.minimum(jnp.maximum(values, -reach), reach).astype(kind)


def setup_inputs(seed: int = 0) -> dict:
    arg_keys = jax.random.split(jax.random.key(seed), 7)
    return {
        "fine_rhs": centred(arg_keys[0], (PATCHES, PS, PS * PS), 3.0, 15.0, ((0, 1024),), jnp.float32),
        "fine_coef": jnp.clip(jnp.exp(math.log(2.0) - 2.0794415 * jax.random.uniform(arg_keys[1], (PATCHES, PS, PS * PS), jnp.float32) ** block_levels(arg_keys[1], (PATCHES, PS, PS * PS), ((0, 1024),), -0.2, 0.2)), 0.25, 2.0).astype(jnp.bfloat16),
        "coarse_rhs": centred(arg_keys[2], (X, Y, Z), 3.0, 15.0, ((0, 64), (1, 8), (2, 2)), jnp.float32),
        "coarse_coef": jnp.clip(jnp.exp(math.log(2.0) - 2.0794415 * jax.random.uniform(arg_keys[3], (X, Y, Z), jnp.float32) ** block_levels(arg_keys[3], (X, Y, Z), ((0, 64), (1, 8), (2, 2)), -0.2, 0.2)), 0.25, 2.0).astype(jnp.bfloat16),
        "patch_count": draw_patch_count(jax.random.fold_in(arg_keys[6], 71), 0),
        "patch_target": draw_patch_target(jax.random.fold_in(arg_keys[6], 71), 0),
    }


DAMPING = 6.0 / 7.0


def grid_sides(padded):
    return (padded[:-2, 1:-1, 1:-1], padded[2:, 1:-1, 1:-1], padded[1:-1, :-2, 1:-1],
            padded[1:-1, 2:, 1:-1], padded[1:-1, 1:-1, :-2], padded[1:-1, 1:-1, 2:])


def combine_sides(weights, side_values):
    summed = weights[0] * side_values[0]
    for number in range(1, 6):
        summed = summed + weights[number] * side_values[number]
    return summed


def face_weights(conduct):
    side_values = grid_sides(jnp.pad(conduct, 1))
    weights = tuple(0.5 * (conduct + neighbour) for neighbour in side_values)
    diagonal = weights[0]
    for number in range(1, 6):
        diagonal = diagonal + weights[number]
    return weights, diagonal


def smooth_grid(source, conduct, last_level):
    weights, diagonal = face_weights(conduct)
    first_pass = DAMPING * source / diagonal
    second_pass = first_pass + DAMPING * (source - diagonal * first_pass + combine_sides(weights, grid_sides(jnp.pad(first_pass, 1)))) / diagonal
    if last_level:
        return second_pass, second_pass
    residue = source - diagonal * second_pass + combine_sides(weights, grid_sides(jnp.pad(second_pass, 1)))
    return second_pass, residue


def patch_smooth(source, conduct):
    return smooth_grid(source, conduct, False)


def halve_sum(values):
    return values.reshape(values.shape[0] // 2, 2, values.shape[1] // 2, 2, values.shape[2] // 2, 2).sum(axis=(1, 3, 5)) * 0.5


def eighth_sum(values):
    return values.reshape(values.shape[0] // 2, 2, values.shape[1] // 2, 2, values.shape[2] // 2, 2).sum(axis=(1, 3, 5)) * 0.125


def device_patches(inputs):
    source, conduct, live_count = inputs
    source = source.reshape(SLOTS, PS, PS, PS)
    conduct = conduct.astype(jnp.float32).reshape(SLOTS, PS, PS, PS)
    second_pass, residue = jax.vmap(patch_smooth)(source, conduct)
    alive_rows = lax.iota(jnp.int32, SLOTS) < live_count
    solved = jnp.where(alive_rows[:, None, None, None], second_pass, 0.0).reshape(SLOTS, PS, PS * PS)
    reduced = residue.reshape(SLOTS, B, 2, B, 2, B, 2).sum(axis=(2, 4, 6)) * 0.5
    return solved, reduced


def reference(fine_rhs, fine_coef, coarse_rhs, coarse_coef, patch_count, patch_target):
    groups = N_GY * N_GZ
    solved, reduced = lax.map(device_patches, (fine_rhs.reshape(DEVICES, SLOTS, PS, PS * PS), fine_coef.reshape(DEVICES, SLOTS, PS, PS * PS), patch_count))
    blocks_x = CX // B
    blocks_y = CY // B
    blocks_z = CZ // B
    slot_ids = lax.iota(jnp.int32, PATCHES)
    device_ids = slot_ids // SLOTS
    slab_ids = device_ids // groups
    owner_ids = patch_target // BLOCKS_DEV
    local_block = patch_target % BLOCKS_DEV
    index_x = slab_ids * blocks_x + local_block // (blocks_y * blocks_z)
    index_y = (owner_ids // N_GZ) * blocks_y + (local_block // blocks_z) % blocks_y
    index_z = (owner_ids % N_GZ) * blocks_z + local_block % blocks_z
    alive_rows = (slot_ids % SLOTS) < patch_count[device_ids]
    index_x = jnp.where(alive_rows, index_x, X // B).astype(jnp.int32)
    blocks = jnp.zeros((X // B, Y // B, Z // B, B, B, B), jnp.float32)
    blocks = blocks.at[index_x, index_y, index_z].set(reduced.reshape(PATCHES, B, B, B), mode="drop")
    covered = jnp.zeros((X // B, Y // B, Z // B), jnp.float32).at[index_x, index_y, index_z].set(1.0, mode="drop")
    placed_grid = blocks.transpose(0, 3, 1, 4, 2, 5).reshape(X, Y, Z)
    covered_grid = jnp.broadcast_to(covered[:, None, :, None, :, None], (X // B, B, Y // B, B, Z // B, B)).reshape(X, Y, Z)
    source = jnp.where(covered_grid > 0.5, placed_grid, coarse_rhs)
    conduct = coarse_coef.astype(jnp.float32)
    coarse_solution, residue = smooth_grid(source, conduct, False)
    deep_solution = coarse_solution
    for level_number in range(1, DEEP + 1):
        source = halve_sum(residue)
        conduct = eighth_sum(conduct)
        deep_solution, residue = smooth_grid(source, conduct, level_number == DEEP)
    return solved.reshape(PATCHES, PS, PS * PS), coarse_solution, deep_solution
```

```python
import functools

import jax
import jax.numpy as jnp
from jax import lax
from jax.experimental import pallas as pl
from jax.experimental.pallas import tpu as pltpu
from jax.sharding import PartitionSpec as P

DAMPING = 6.0 / 7.0
REST = 1.0 - DAMPING
PRECISE = lax.Precision.HIGHEST
F32 = jnp.float32
CORES = 2
VMEM_BYTES = 40 * 1024 * 1024


def iota(shape, dim):
    return lax.broadcasted_iota(jnp.int32, shape, dim)


def dot(a, b):
    return jnp.dot(a, b, precision=PRECISE, preferred_element_type=F32)


def after(values, axis):
    return pltpu.roll(values, values.shape[axis] - 1, axis)


def before(values, axis):
    return pltpu.roll(values, 1, axis)


def fine_kernel(count_ref, target_ref, rhs_ref, coef_ref, solved_ref, send_ref):
    live = count_ref[0]
    half = rhs_ref.shape[0] // 2
    source = jnp.concatenate([rhs_ref[:half], rhs_ref[half:]], axis=2)
    k = coef_ref[...].astype(F32) * 0.5
    h = jnp.concatenate([k[:half], k[half:]], axis=2)
    shape = h.shape
    x, lane = iota(shape, 1), iota(shape, 2)
    y, z = (lane >> 3) & 7, lane & 7

    def wrapped(values, amount):
        return pltpu.roll(values, amount % 128, 2)

    hx = jnp.where(x < 7, after(h, 1), 0.0)
    hy = jnp.where(y < 7, wrapped(h, -8), 0.0)
    hz = jnp.where(z < 7, wrapped(h, -1), 0.0)
    diagonal = 6.0 * h + hx + hy + hz
    diagonal += jnp.where(x > 0, before(h, 1), 0.0)
    diagonal += jnp.where(y > 0, wrapped(h, 8), 0.0)
    diagonal += jnp.where(z > 0, wrapped(h, 1), 0.0)
    wx = jnp.where(x < 7, h + hx, 0.0)
    wy = jnp.where(y < 7, h + hy, 0.0)
    wz = jnp.where(z < 7, h + hz, 0.0)

    def sides(u):
        total = wx * after(u, 1) + before(wx * u, 1)
        total += wy * wrapped(u, -8) + wrapped(wy * u, 8)
        return total + wz * wrapped(u, -1) + wrapped(wz * u, 1)

    scale = DAMPING / diagonal
    first = source * scale
    second = first + scale * (REST * source + sides(first))
    residue = source - diagonal * second + sides(second)
    slot = iota((half, 8, 64), 0)
    solved_ref[:half] = jnp.where(slot < live, second[:, :, :64], 0.0)
    solved_ref[half:] = jnp.where(slot + half < live, second[:, :, 64:], 0.0)

    square = (128, 128)
    row, col = iota(square, 0), iota(square, 1)
    iz, ix, iy = col >> 4, (col >> 2) & 3, col & 3
    match = (((row >> 4) & 3) == iy) & (((row >> 1) & 3) == iz)
    keep = ((row >> 1) & 3) == ix
    cells = residue.reshape(square)
    parts = []
    for number in range(2):
        gather = jnp.where(match & ((row >> 6) == number), 0.5, 0.0)
        parts.append(jnp.where(keep, dot(cells, gather), 0.0))

    wide = (32, 256)
    spread = jnp.where(iota(wide, 0) == (iota(wide, 1) >> 3), 1.0, 0.0)
    names = jnp.broadcast_to(target_ref[...].astype(F32), (8, 32))
    name = (dot(names, spread)[:1] + 0.5).astype(jnp.int32)
    row, col = iota(wide, 0), iota(wide, 1)
    name = jnp.broadcast_to(name, wide)
    own = jnp.sum(jnp.where(col == row * 8, name, 0).astype(F32), axis=1, keepdims=True)
    own = own.astype(jnp.int32)
    earlier = ((own >> 8) == (name >> 8)) & (row < (col >> 3))
    rank = jnp.sum(jnp.where(earlier, 1.0, 0.0), axis=0, keepdims=True).astype(jnp.int32)
    place = (name >> 8) * 2 + rank
    chosen = (place == row) & ((col >> 3) < live)
    picked = jnp.where(chosen, 1.0, 0.0)
    tag = jnp.where(chosen & ((col & 7) == 0), (name & 255) + 1, 0).astype(F32)
    tag = jnp.sum(tag, axis=1, keepdims=True)
    packed = dot(picked[:, :128], parts[0]) + dot(picked[:, 128:], parts[1])
    send_ref[...] = jnp.where(iota(packed.shape, 1) < 64, packed, tag)


def place_kernel(got_ref, rhs_ref, coef_ref, out_ref):
    got = got_ref[...]
    four = jnp.concatenate([got, got, got, got], axis=0)
    square = (128, 128)
    row, col = iota(square, 0), iota(square, 1)
    slices = jnp.where((col >> 4) == (row >> 5), four, 0.0)
    cell = (((row >> 4) & 3) << 2) + (row & 3)
    select = jnp.where(((col & 15) == cell) & (col < 64), 1.0, 0.0)
    turned = (((1,), (1,)), ((), ()))
    left = lax.dot_general(select, slices, turned, precision=PRECISE, preferred_element_type=F32)
    only = jnp.where(iota((8, 128), 1) == 64, 1.0, 0.0)
    tags = lax.dot_general(only, four, turned, precision=PRECISE, preferred_element_type=F32)
    tags = (tags[:1] + 0.5).astype(jnp.int32) - 1
    tags = jnp.broadcast_to(tags, square)
    here = ((tags >> 7) == (row >> 6)) & (((tags >> 5) & 3) == ((row >> 2) & 3))
    down = (four[:, 64:65] + 0.5).astype(jnp.int32) - 1
    right = jnp.where(((down & 31) == (col >> 2)) & ((col & 3) == (row >> 5)), 1.0, 0.0)
    placed = dot(jnp.where(here, left, 0.0), right)
    covered = jnp.dot(
        jnp.where(here, 1.0, 0.0).astype(jnp.bfloat16),
        right.astype(jnp.bfloat16),
        preferred_element_type=F32,
    )
    shape = rhs_ref.shape
    out_ref[0] = jnp.where(covered.reshape(shape) > 0.5, placed.reshape(shape), rhs_ref[...])
    out_ref[1] = coef_ref[...].astype(F32) * 0.5


def pair_matrix(size):
    shape = (size, 128)
    return jnp.where((iota(shape, 0) >> 1) == iota(shape, 1), 1.0, 0.0)


def prepare(h, inside, depth):
    mid = h[1:-1]
    lane = iota(mid.shape, 2)
    hy = after(mid, 1)
    hz = jnp.where(lane < depth - 1, after(mid, 2), 0.0)
    diagonal = 6.0 * mid + h[:-2] + h[2:] + hy + before(mid, 1) + hz
    diagonal += jnp.where(lane > 0, before(mid, 2), 0.0)
    scale = jnp.where(inside & (lane < depth), DAMPING / diagonal, 0.0)
    wx = h[:-1] + h[1:]
    wy = mid + hy
    wz = jnp.where(lane < depth - 1, mid + hz, 0.0)
    return diagonal, scale, wx, wy, wz


def neighbours(u, wx, wy, wz):
    mid = u[1:-1]
    total = wx[1:] * u[2:] + wx[:-1] * u[:-2]
    total += wy * after(mid, 1) + before(wy * mid, 1)
    return total + wz * after(mid, 2) + before(wz * mid, 2)


def within(shape, start, first_layer, first_row, sizes):
    x = iota(shape, 0) + (start[0] + first_layer)
    y = iota(shape, 1) + (start[1] + first_row)
    return (x >= 0) & (x < sizes[0]) & (y >= 0) & (y < sizes[1])


def coarser(values, matrix, scale, rows_ref):
    layers, rows, depth = values.shape
    values = values.reshape(layers // 2, 2, rows, depth)
    values = values[:, 0] + values[:, 1]
    flat = dot(values.reshape(layers // 2 * rows, depth), matrix) * scale
    count = flat.shape[0]
    rows_ref[:count] = flat
    total = rows_ref[pl.ds(0, count // 2, stride=2), :] + rows_ref[pl.ds(1, count // 2, stride=2), :]
    return total.reshape(layers // 2, rows // 2, 128)


def base_kernel(
    sizes, pos_ref, full_ref, side_ref, out_ref, pay_ref,
    s_ref, h_ref, wx_ref, wy_ref, wz_ref, diag_ref, scale_ref, first_ref, second_ref,
    res_ref, rows_ref,
):
    gx, gy, core = pos_ref[0], pos_ref[1], pos_ref[2]
    for number in range(2):
        lanes = slice(128 * number, 128 * number + 128)
        s_ref[0:6, :, lanes] = side_ref[0, number, 0:6]
        s_ref[6:14, :, lanes] = full_ref[number, 0]
        s_ref[14:20, :, lanes] = side_ref[1, number, 0:6]
        h_ref[0:7, :, lanes] = side_ref[0, number, 6:13]
        h_ref[7:15, :, lanes] = full_ref[number, 1]
        h_ref[15:22, :, lanes] = side_ref[1, number, 6:13]
    shape = (32, 256)
    lane = iota(shape, 1)
    y = iota(shape, 0) + (gy * 16 - 8)
    rows_in = (y >= 0) & (y < sizes[1])

    def weigh(layer, _):
        h = h_ref[layer + 1]
        below, above = h_ref[layer], h_ref[layer + 2]
        hy = after(h, 0)
        hz = jnp.where(lane < 255, after(h, 1), 0.0)
        diagonal = 6.0 * h + below + above + hy + before(h, 0) + hz
        diagonal += jnp.where(lane > 0, before(h, 1), 0.0)
        x = gx * 8 + layer - 6
        inside = rows_in & (x >= 0) & (x < sizes[0])
        scale = jnp.where(inside, DAMPING / diagonal, 0.0)
        diag_ref[layer] = diagonal
        scale_ref[layer] = scale
        wx_ref[layer] = h + above
        wy_ref[layer] = h + hy
        wz_ref[layer] = jnp.where(lane < 255, h + hz, 0.0)
        first_ref[layer] = s_ref[layer] * scale
        return 0

    lax.fori_loop(0, 20, weigh, 0)

    def sides(ref, layer):
        u, wy, wz = ref[layer], wy_ref[layer], wz_ref[layer]
        total = wx_ref[layer] * ref[layer + 1] + wx_ref[layer - 1] * ref[layer - 1]
        total += wy * after(u, 0) + before(wy * u, 0)
        return u, total + wz * after(u, 1) + before(wz * u, 1)

    def correct(layer, _):
        u, total = sides(first_ref, layer)
        second_ref[layer] = u + scale_ref[layer] * (REST * s_ref[layer] + total)
        return 0

    lax.fori_loop(1, 19, correct, 0)

    def leave(layer, _):
        u, total = sides(second_ref, layer)
        res_ref[layer - 2] = s_ref[layer] - diag_ref[layer] * u + total
        return 0

    lax.fori_loop(2, 18, leave, 0)
    own = second_ref[6:14, 8:24, :]
    out_ref[...] = jnp.where(core == 0, own[:, :, :128], own[:, :, 128:])

    zoom = pair_matrix(256)
    source = coarser(res_ref[...], zoom, 0.5, rows_ref)
    h = coarser(h_ref[1:21], zoom, 0.125, rows_ref)
    inside = within(source.shape, (gx * 4, gy * 8), -2, -4, (sizes[0] // 2, sizes[1] // 2))
    diagonal, scale, wx, wy, wz = prepare(h, inside, 128)
    first = source * scale
    total = neighbours(first, wx[1:-1], wy[1:-1], wz[1:-1])
    second = first[1:-1] + scale[1:-1] * (REST * source[1:-1] + total)
    total = neighbours(second, wx[2:-2], wy[2:-2], wz[2:-2])
    residue = source[2:-2] - diagonal[2:-2] * second[1:-1] + total

    zoom = pair_matrix(128)
    source = coarser(residue, zoom, 0.5, rows_ref)
    h = coarser(h[1:-1], zoom, 0.125, rows_ref)
    _, scale, _, _, _ = prepare(h, jnp.full(source.shape, True), 64)
    pay_ref[0:2] = source[:, 2:6]
    pay_ref[2:4] = (source * scale)[:, 2:6]
    pay_ref[4:6] = h[1:3, 2:6]


def deep_kernel(sizes, pos_ref, mid_ref, side_ref, out_ref, win_ref, rows_ref):
    gx, gy, core = pos_ref[0], pos_ref[1], pos_ref[2]
    win_ref[...] = jnp.zeros(win_ref.shape, F32)
    for number in range(3):
        for part in range(3):
            blocks = [
                side_ref[0, 1, part], side_ref[0, 0, part], mid_ref[part],
                side_ref[1, 0, part], side_ref[1, 1, part],
            ]
            for place, block in enumerate(blocks):
                win_ref[number, 2 * place : 2 * place + 2, 4 * part : 4 * part + 4] = block[
                    2 * number : 2 * number + 2
                ]
    source, first, h = win_ref[0], win_ref[1], win_ref[2]
    shape = (8, 16, 128)
    inside = within(shape, (gx * 2, gy * 4), -3, -4, (sizes[0] // 4, sizes[1] // 4))
    inside &= iota(shape, 1) < 12
    diagonal, scale, wx, wy, wz = prepare(h, inside, 64)
    total = neighbours(first, wx, wy, wz)
    second = first[1:-1] + scale * (REST * source[1:-1] + total)
    total = neighbours(second, wx[1:-1], wy[1:-1], wz[1:-1])
    residue = source[2:-2] - diagonal[1:-1] * second[1:-1] + total

    zoom = pair_matrix(128)
    source = coarser(residue, zoom, 0.5, rows_ref)
    h = coarser(h, zoom, 0.125, rows_ref)
    inside = within(source.shape, (gx, gy * 2), -1, -2, (sizes[0] // 8, sizes[1] // 8))
    inside &= iota(source.shape, 1) < 6
    _, scale, wx, wy, wz = prepare(h, inside, 32)
    first = source * scale
    total = neighbours(first, wx[1:-1], wy[1:-1], wz[1:-1])
    second = first[1:-1] + scale[1:-1] * (REST * source[1:-1] + total)
    second = second[:, 2:4]
    out_ref[...] = jnp.where(core == 0, second[:, :, :16], second[:, :, 16:32])


def call(kernel, out_shape, in_specs=None, scratch=(), flops=100_000):
    specs = {} if in_specs is None else {"in_specs": in_specs}
    return pl.pallas_call(
        kernel,
        out_shape=out_shape,
        scratch_shapes=list(scratch),
        compiler_params=pltpu.CompilerParams(vmem_limit_bytes=VMEM_BYTES),
        cost_estimate=pl.CostEstimate(flops=flops, bytes_accessed=flops, transcendentals=0),
        **specs,
    )


def split_send(values, axis, step):
    count = lax.axis_size(axis)
    pairs = []
    for place in range(count):
        if place + step < count:
            pairs.append((place * CORES, (place + step) * CORES))
        if place - step >= 0:
            pairs.append((place * CORES + 1, (place - step) * CORES + 1))
    return lax.ppermute(values, (axis, "gz"), pairs)


def shared(values):
    return lax.all_gather(values, "gz")


def per_device(fine_rhs, fine_coef, coarse_rhs, coarse_coef, patch_count, patch_target):
    core = lax.axis_index("gz")
    pos = jnp.stack([lax.axis_index("gx"), lax.axis_index("gy"), core])
    sizes = (
        lax.axis_size("gx") * coarse_rhs.shape[0],
        lax.axis_size("gy") * coarse_rhs.shape[1],
    )
    vmem = pl.BlockSpec(memory_space=pltpu.VMEM)
    smem = pl.BlockSpec(memory_space=pltpu.SMEM)
    struct = jax.ShapeDtypeStruct
    fine_solution, send = call(
        fine_kernel,
        (struct(fine_rhs.shape, F32), struct((32, 128), F32)),
        [smem, vmem, vmem, vmem],
    )(patch_count, patch_target.reshape(1, 32), fine_rhs, fine_coef)
    got = lax.all_to_all(send.reshape(16, 2, 128), ("gy", "gz"), 0, 0).reshape(32, 128)
    both = call(place_kernel, struct((2, 8, 16, 128), F32), [vmem, vmem, vmem])(
        got, coarse_rhs, coarse_coef
    )
    chip = shared(both)
    rows = jnp.where(core == 0, chip[:, :, :, 8:], chip[:, :, :, :8])
    halo = shared(split_send(rows, "gy", 1))
    full = jnp.concatenate([halo[0], chip, halo[1]], axis=3)
    high = jnp.concatenate([full[:, 0, 2:], full[:, 1, 1:]], axis=1)
    low = jnp.concatenate([full[:, 0, :6], full[:, 1, :7]], axis=1)
    side = shared(split_send(jnp.where(core == 0, high, low), "gx", 1))
    grid = (32, 256)
    coarse_solution, pay = call(
        functools.partial(base_kernel, sizes),
        (struct((8, 16, 128), F32), struct((6, 4, 128), F32)),
        [smem, vmem, vmem],
        [pltpu.VMEM((20, *grid), F32), pltpu.VMEM((22, *grid), F32)]
        + [pltpu.VMEM((20, *grid), F32)] * 7
        + [pltpu.VMEM((16, *grid), F32), pltpu.VMEM((320, 128), F32)],
        flops=5_000_000,
    )(pos, full, side)
    halo = shared(split_send(pay, "gy", 1))
    mid = jnp.stack([halo[0], pay, halo[1]])
    sides = shared(jnp.stack([split_send(mid, "gx", 1), split_send(mid, "gx", 2)]))
    deep_solution = call(
        functools.partial(deep_kernel, sizes),
        struct((1, 2, 16), F32),
        [smem, vmem, vmem],
        [pltpu.VMEM((3, 10, 16, 128), F32), pltpu.VMEM((320, 128), F32)],
    )(pos, mid, sides)
    return (fine_solution, coarse_solution, deep_solution)


def solution(mesh):
    return jax.shard_map(
        per_device,
        mesh=mesh,
        in_specs=(
            P(("gx", "gy", "gz"), None, None),
            P(("gx", "gy", "gz"), None, None),
            P("gx", "gy", "gz"),
            P("gx", "gy", "gz"),
            P(("gx", "gy", "gz")),
            P(("gx", "gy", "gz")),
        ),
        out_specs=(P(("gx", "gy", "gz"), None, None), P("gx", "gy", "gz"), P("gx", "gy", "gz")),
        check_vma=False,
    )
```

```python
import functools

import jax
import jax.numpy as jnp
from jax import lax
from jax.experimental import pallas as pl
from jax.experimental.pallas import tpu as pltpu
from jax.sharding import PartitionSpec as P

DAMPING = 6.0 / 7.0
REST = 1.0 - DAMPING
PRECISE = lax.Precision.HIGHEST
F32 = jnp.float32
CORES = 2
VMEM_BYTES = 40 * 1024 * 1024


def iota(shape, dim):
    return lax.broadcasted_iota(jnp.int32, shape, dim)


def dot(a, b):
    return jnp.dot(a, b, precision=PRECISE, preferred_element_type=F32)


def after(values, axis):
    return pltpu.roll(values, values.shape[axis] - 1, axis)


def before(values, axis):
    return pltpu.roll(values, 1, axis)


def inverse(values):
    guess = pl.reciprocal(values, approx=True)
    return guess * (2.0 - values * guess)


def fine_kernel(
    count_ref, target_hbm, rhs_hbm, coef_hbm, solved_ref, send_ref, target_ref, rhs_ref, coef_ref, sems
):
    live = count_ref[0]
    loads = [
        pltpu.make_async_copy(coef_hbm, coef_ref, sems.at[0]),
        pltpu.make_async_copy(rhs_hbm, rhs_ref, sems.at[1]),
        pltpu.make_async_copy(target_hbm, target_ref, sems.at[2]),
    ]
    for load in loads:
        load.start()
    half = rhs_ref.shape[0] // 2
    loads[0].wait()
    k = coef_ref[...].astype(F32) * 0.5
    h = jnp.concatenate([k[:half], k[half:]], axis=2)
    shape = h.shape
    x, lane = iota(shape, 1), iota(shape, 2)
    y, z = (lane >> 3) & 7, lane & 7

    def wrapped(values, amount):
        return pltpu.roll(values, amount % 128, 2)

    hx = jnp.where(x < 7, after(h, 1), 0.0)
    hy = jnp.where(y < 7, wrapped(h, -8), 0.0)
    hz = jnp.where(z < 7, wrapped(h, -1), 0.0)
    diagonal = 6.0 * h + hx + hy + hz
    diagonal += jnp.where(x > 0, before(h, 1), 0.0)
    diagonal += jnp.where(y > 0, wrapped(h, 8), 0.0)
    diagonal += jnp.where(z > 0, wrapped(h, 1), 0.0)
    wx = jnp.where(x < 7, h + hx, 0.0)
    wy = jnp.where(y < 7, h + hy, 0.0)
    wz = jnp.where(z < 7, h + hz, 0.0)

    def sides(u):
        total = wx * after(u, 1) + before(wx * u, 1)
        total += wy * wrapped(u, -8) + wrapped(wy * u, 8)
        return total + wz * wrapped(u, -1) + wrapped(wz * u, 1)

    scale = DAMPING * inverse(diagonal)
    loads[1].wait()
    source = jnp.concatenate([rhs_ref[:half], rhs_ref[half:]], axis=2)
    first = source * scale
    second = first + scale * (REST * source + sides(first))
    residue = source - diagonal * second + sides(second)
    solved_ref[...] = second

    loads[2].wait()
    square = (128, 128)
    row, col = iota(square, 0), iota(square, 1)
    iz, ix, iy = (col >> 4) & 3, (col >> 2) & 3, col & 3
    match = (((row >> 4) & 3) == iy) & (((row >> 1) & 3) == iz)
    keep = ((row >> 1) & 3) == ix
    cells = residue.reshape(square)
    parts = []
    for number in range(2):
        gather = jnp.where(match & ((row >> 6) == number), 0.5, 0.0)
        parts.append(jnp.where(keep, dot(cells, gather), 0.0))

    wide = (32, 256)
    spread = jnp.where(iota(wide, 0) == (iota(wide, 1) >> 3), 1.0, 0.0)
    names = jnp.broadcast_to(target_ref[...].astype(F32), (8, 32))
    name = (dot(names, spread)[:1] + 0.5).astype(jnp.int32)
    names = jnp.broadcast_to(name, wide)
    row, col = iota(wide, 0), iota(wide, 1)
    own = jnp.sum(jnp.where(col == row * 8, names, 0).astype(F32), axis=1, keepdims=True)
    own = own.astype(jnp.int32)
    earlier = ((own >> 8) == (names >> 8)) & (row < (col >> 3))
    rank = jnp.sum(jnp.where(earlier, 1.0, 0.0), axis=0, keepdims=True).astype(jnp.int32)
    wide = (128, 256)
    row, col = iota(wide, 0), iota(wide, 1)
    chip = (row >> 4) + ((row >> 1) & 3) - 1
    owner = chip * 2 + (row & 1)
    wanted = ((row & 7) < 6) & (chip >= 0) & (chip < 8) & ((col >> 3) < live)
    chosen = wanted & (owner == (name >> 8))
    packed, tags = [], []
    for number in range(2):
        mine = chosen & (rank == number)
        picked = jnp.where(mine, 1.0, 0.0)
        packed.append(dot(picked[:, :128], parts[0]) + dot(picked[:, 128:], parts[1]))
        tag = jnp.where(mine & ((col & 7) == 0), (name & 255) + 1, 0).astype(F32)
        tags.append(jnp.sum(tag, axis=1, keepdims=True))
    row, col = iota(square, 0), iota(square, 1)
    place = (row & 7) * 2
    tags = jnp.where(col == place, tags[0], 0.0) + jnp.where(col == place + 1, tags[1], 0.0)
    lift = jnp.where(((row & 7) == 6) & ((row >> 3) == (col >> 3)), 1.0, 0.0)
    send_ref[...] = jnp.where(col < 64, packed[0], packed[1]) + dot(lift, tags)


def store_kernel(count_ref, second_ref, solved_ref):
    live = count_ref[0]
    second = second_ref[...]
    half = second.shape[0]
    slot = iota((half, 8, 64), 0)
    solved_ref[:half] = jnp.where(slot < live, second[:, :, :64], 0.0)
    solved_ref[half:] = jnp.where(slot + half < live, second[:, :, 64:], 0.0)


def place_kernel(pos_ref, got_ref, chip_ref, full_ref, pay_ref):
    tags = got_ref[pl.ds(6, 16, stride=8), :]
    square = (128, 128)
    row, col = iota(square, 0), iota(square, 1)
    rank = (row >> 4) & 1
    mask = (col >> 4) == rank * 4 + (row >> 5)
    turned = (((1,), (1,)), ((), ()))
    tall = jnp.concatenate([tags] * 8, axis=0)
    ones = jnp.ones((8, 128), F32)

    def place(number, first_row, rows):
        got = got_ref[pl.ds(number, 16, stride=8), :]
        slices = jnp.where(mask, jnp.concatenate([got] * 8, axis=0), 0.0)
        shape = (8 * rows, 128)
        shift = rows.bit_length() - 1
        r, c = iota(shape, 0), iota(shape, 1)
        x, y = r >> shift, (r & (rows - 1)) + first_row
        select = jnp.where((c & 15) == (x & 3) * 4 + (y & 3), 1.0, 0.0)
        left = lax.dot_general(
            select, slices, turned, precision=PRECISE, preferred_element_type=F32
        )
        named = jnp.where(col == 2 * number + rank, tall, 0.0)
        across = lax.dot_general(
            ones, named, turned, precision=PRECISE, preferred_element_type=F32
        )
        across = (across[:1] + 0.5).astype(jnp.int32) - 1
        here = ((across >> 7) == (x >> 2)) & (((across >> 5) & 3) == (y >> 2))
        down = (jnp.sum(named, axis=1, keepdims=True) + 0.5).astype(jnp.int32) - 1
        right = jnp.where(((down & 31) == (col >> 2)) & ((col & 3) == (row >> 5)), 1.0, 0.0)
        placed = dot(jnp.where(here, left, 0.0), right)
        covered = jnp.dot(
            jnp.where(here, 1.0, 0.0).astype(jnp.bfloat16),
            right.astype(jnp.bfloat16),
            preferred_element_type=F32,
        )
        return placed.reshape(8, rows, 128), covered.reshape(8, rows, 128) > 0.5

    core = pos_ref[2]
    for number in range(2):
        for part, (first_row, rows, start) in enumerate(((8, 8, 0), (0, 16, 8), (0, 8, 24))):
            placed, covered = place(2 * part + number, first_row, rows)
            lines = slice(start, start + rows)
            full_ref[number, 0, :, lines] = jnp.where(covered, placed, chip_ref[number, 0, :, lines])
        full_ref[number, 1] = chip_ref[number, 1]

    @pl.when(core == 0)
    def _():
        for number in range(2):
            pay_ref[number, 0:6] = full_ref[number, 0, 2:8]
            pay_ref[number, 6:13] = full_ref[number, 1, 1:8]

    @pl.when(core != 0)
    def _():
        for number in range(2):
            pay_ref[number, 0:6] = full_ref[number, 0, 0:6]
            pay_ref[number, 6:13] = full_ref[number, 1, 0:7]


def pair_matrix(size):
    shape = (size, 128)
    return jnp.where((iota(shape, 0) >> 1) == iota(shape, 1), 1.0, 0.0)


def prepare(h, inside, depth):
    mid = h[1:-1]
    lane = iota(mid.shape, 2)
    hy = after(mid, 1)
    hz = jnp.where(lane < depth - 1, after(mid, 2), 0.0)
    diagonal = 6.0 * mid + h[:-2] + h[2:] + hy + before(mid, 1) + hz
    diagonal += jnp.where(lane > 0, before(mid, 2), 0.0)
    scale = jnp.where(inside & (lane < depth), DAMPING * inverse(diagonal), 0.0)
    wx = h[:-1] + h[1:]
    wy = mid + hy
    wz = jnp.where(lane < depth - 1, mid + hz, 0.0)
    return diagonal, scale, wx, wy, wz


def neighbours(u, wx, wy, wz):
    mid = u[1:-1]
    total = wx[1:] * u[2:] + wx[:-1] * u[:-2]
    total += wy * after(mid, 1) + before(wy * mid, 1)
    return total + wz * after(mid, 2) + before(wz * mid, 2)


def within(shape, start, first_layer, first_row, sizes):
    x = iota(shape, 0) + (start[0] + first_layer)
    y = iota(shape, 1) + (start[1] + first_row)
    return (x >= 0) & (x < sizes[0]) & (y >= 0) & (y < sizes[1])


def coarser(values, matrix, scale, rows_ref):
    layers, rows, depth = values.shape
    values = values.reshape(layers // 2, 2, rows, depth)
    values = values[:, 0] + values[:, 1]
    flat = dot(values.reshape(layers // 2 * rows, depth), matrix) * scale
    count = flat.shape[0]
    rows_ref[:count] = flat
    total = rows_ref[pl.ds(0, count // 2, stride=2), :] + rows_ref[pl.ds(1, count // 2, stride=2), :]
    return total.reshape(layers // 2, rows // 2, 128)


def base_kernel(
    sizes, pos_ref, full_ref, side_ref, out_ref, pay_ref,
    s_ref, h_ref, wx_ref, wy_ref, wz_ref, diag_ref, scale_ref, first_ref, second_ref,
    res_ref, rows_ref,
):
    gx, gy, core = pos_ref[0], pos_ref[1], pos_ref[2]
    for number in range(2):
        lanes = slice(128 * number, 128 * number + 128)
        s_ref[0:6, :, lanes] = side_ref[0, number, 0:6]
        s_ref[6:14, :, lanes] = full_ref[number, 0]
        s_ref[14:20, :, lanes] = side_ref[1, number, 0:6]
        h_ref[0:7, :, lanes] = side_ref[0, number, 6:13]
        h_ref[7:15, :, lanes] = full_ref[number, 1]
        h_ref[15:22, :, lanes] = side_ref[1, number, 6:13]
    shape = (32, 256)
    lane = iota(shape, 1)
    y = iota(shape, 0) + (gy * 16 - 8)
    rows_in = (y >= 0) & (y < sizes[1])

    def weigh(layer, _):
        h = h_ref[layer + 1]
        below, above = h_ref[layer], h_ref[layer + 2]
        hy = after(h, 0)
        hz = jnp.where(lane < 255, after(h, 1), 0.0)
        diagonal = 6.0 * h + below + above + hy + before(h, 0) + hz
        diagonal += jnp.where(lane > 0, before(h, 1), 0.0)
        x = gx * 8 + layer - 6
        inside = rows_in & (x >= 0) & (x < sizes[0])
        scale = jnp.where(inside, DAMPING * inverse(diagonal), 0.0)
        diag_ref[layer] = diagonal
        scale_ref[layer] = scale
        wx_ref[layer] = h + above
        wy_ref[layer] = h + hy
        wz_ref[layer] = jnp.where(lane < 255, h + hz, 0.0)
        first_ref[layer] = s_ref[layer] * scale
        return 0

    lax.fori_loop(0, 20, weigh, 0)

    def sides(ref, layer):
        u, wy, wz = ref[layer], wy_ref[layer], wz_ref[layer]
        total = wx_ref[layer] * ref[layer + 1] + wx_ref[layer - 1] * ref[layer - 1]
        total += wy * after(u, 0) + before(wy * u, 0)
        return u, total + wz * after(u, 1) + before(wz * u, 1)

    def correct(layer, _):
        u, total = sides(first_ref, layer)
        second_ref[layer] = u + scale_ref[layer] * (REST * s_ref[layer] + total)
        return 0

    lax.fori_loop(1, 19, correct, 0)

    def leave(layer, _):
        u, total = sides(second_ref, layer)
        res_ref[layer - 2] = s_ref[layer] - diag_ref[layer] * u + total
        return 0

    lax.fori_loop(2, 18, leave, 0)
    own = second_ref[6:14, 8:24, :]
    out_ref[...] = jnp.where(core == 0, own[:, :, :128], own[:, :, 128:])

    zoom = pair_matrix(256)
    source = coarser(res_ref[...], zoom, 0.5, rows_ref)
    h = coarser(h_ref[1:21], zoom, 0.125, rows_ref)
    inside = within(source.shape, (gx * 4, gy * 8), -2, -4, (sizes[0] // 2, sizes[1] // 2))
    diagonal, scale, wx, wy, wz = prepare(h, inside, 128)
    first = source * scale
    total = neighbours(first, wx[1:-1], wy[1:-1], wz[1:-1])
    second = first[1:-1] + scale[1:-1] * (REST * source[1:-1] + total)
    total = neighbours(second, wx[2:-2], wy[2:-2], wz[2:-2])
    residue = source[2:-2] - diagonal[2:-2] * second[1:-1] + total

    zoom = pair_matrix(128)
    source = coarser(residue, zoom, 0.5, rows_ref)
    h = coarser(h[1:-1], zoom, 0.125, rows_ref)
    _, scale, _, _, _ = prepare(h, jnp.full(source.shape, True), 64)
    pay_ref[0:2] = source[:, 2:6]
    pay_ref[2:4] = (source * scale)[:, 2:6]
    pay_ref[4:6] = h[1:3, 2:6]


def deep_kernel(sizes, pos_ref, mid_ref, side_ref, out_ref, win_ref, rows_ref):
    gx, gy, core = pos_ref[0], pos_ref[1], pos_ref[2]
    win_ref[...] = jnp.zeros(win_ref.shape, F32)
    for number in range(3):
        for part in range(3):
            blocks = [
                side_ref[0, 1, part], side_ref[0, 0, part], mid_ref[part],
                side_ref[1, 0, part], side_ref[1, 1, part],
            ]
            for place, block in enumerate(blocks):
                win_ref[number, 2 * place : 2 * place + 2, 4 * part : 4 * part + 4] = block[
                    2 * number : 2 * number + 2
                ]
    source, first, h = win_ref[0], win_ref[1], win_ref[2]
    shape = (8, 16, 128)
    inside = within(shape, (gx * 2, gy * 4), -3, -4, (sizes[0] // 4, sizes[1] // 4))
    inside &= iota(shape, 1) < 12
    diagonal, scale, wx, wy, wz = prepare(h, inside, 64)
    total = neighbours(first, wx, wy, wz)
    second = first[1:-1] + scale * (REST * source[1:-1] + total)
    total = neighbours(second, wx[1:-1], wy[1:-1], wz[1:-1])
    residue = source[2:-2] - diagonal[1:-1] * second[1:-1] + total

    zoom = pair_matrix(128)
    source = coarser(residue, zoom, 0.5, rows_ref)
    h = coarser(h, zoom, 0.125, rows_ref)
    inside = within(source.shape, (gx, gy * 2), -1, -2, (sizes[0] // 8, sizes[1] // 8))
    inside &= iota(source.shape, 1) < 6
    _, scale, wx, wy, wz = prepare(h, inside, 32)
    first = source * scale
    total = neighbours(first, wx[1:-1], wy[1:-1], wz[1:-1])
    second = first[1:-1] + scale[1:-1] * (REST * source[1:-1] + total)
    second = second[:, 2:4]
    out_ref[...] = jnp.where(core == 0, second[:, :, :16], second[:, :, 16:32])


def call(kernel, out_shape, in_specs=None, scratch=(), flops=100_000):
    specs = {} if in_specs is None else {"in_specs": in_specs}
    return pl.pallas_call(
        kernel,
        out_shape=out_shape,
        scratch_shapes=list(scratch),
        compiler_params=pltpu.CompilerParams(vmem_limit_bytes=VMEM_BYTES),
        cost_estimate=pl.CostEstimate(flops=flops, bytes_accessed=flops, transcendentals=0),
        **specs,
    )


def split_send(values, axis, step):
    count = lax.axis_size(axis)
    pairs = []
    for place in range(count):
        if place + step < count:
            pairs.append((place * CORES, (place + step) * CORES))
        if place - step >= 0:
            pairs.append((place * CORES + 1, (place - step) * CORES + 1))
    return lax.ppermute(values, (axis, "gz"), pairs)


def exchanged(up, down, axis):
    count = lax.axis_size(axis)
    pairs = [(place, place + 1) for place in range(count - 1)]
    back = [(target, source) for source, target in pairs]
    return lax.ppermute(up, axis, pairs), lax.ppermute(down, axis, back)


def shared(values):
    return lax.all_gather(values, "gz")


def per_device(fine_rhs, fine_coef, coarse_rhs, coarse_coef, patch_count, patch_target):
    core = lax.axis_index("gz")
    pos = jnp.stack([lax.axis_index("gx"), lax.axis_index("gy"), core])
    sizes = (
        lax.axis_size("gx") * coarse_rhs.shape[0],
        lax.axis_size("gy") * coarse_rhs.shape[1],
    )
    vmem = pl.BlockSpec(memory_space=pltpu.VMEM)
    smem = pl.BlockSpec(memory_space=pltpu.SMEM)
    struct = jax.ShapeDtypeStruct
    anywhere = pl.BlockSpec(memory_space=pl.ANY)
    second, send = call(
        fine_kernel,
        (struct((16, 8, 128), F32), struct((128, 128), F32)),
        [smem, anywhere, anywhere, anywhere],
        [
            pltpu.VMEM((1, 32), jnp.int32),
            pltpu.VMEM(fine_rhs.shape, F32),
            pltpu.VMEM(fine_coef.shape, fine_coef.dtype),
            pltpu.SemaphoreType.DMA((3,)),
        ],
    )(patch_count, patch_target.reshape(1, 32), fine_rhs, fine_coef)
    got = lax.all_to_all(send.reshape(16, 8, 128), ("gy", "gz"), 0, 0).reshape(128, 128)
    fine_solution = call(store_kernel, struct(fine_rhs.shape, F32), [smem, vmem])(
        patch_count, second
    )
    own = jnp.stack([coarse_rhs, coarse_coef.astype(F32) * 0.5])
    below, above = exchanged(own[:, :, 8:], own[:, :, :8], "gy")
    chip = shared(jnp.concatenate([below, own, above], axis=2))
    full, pay = call(
        place_kernel,
        (struct((2, 2, 8, 32, 128), F32), struct((2, 13, 32, 128), F32)),
        [smem, vmem, vmem],
    )(pos, got, chip)
    side = shared(split_send(pay, "gx", 1))
    grid = (32, 256)
    coarse_solution, pay = call(
        functools.partial(base_kernel, sizes),
        (struct((8, 16, 128), F32), struct((6, 4, 128), F32)),
        [smem, vmem, vmem],
        [pltpu.VMEM((20, *grid), F32), pltpu.VMEM((22, *grid), F32)]
        + [pltpu.VMEM((20, *grid), F32)] * 7
        + [pltpu.VMEM((16, *grid), F32), pltpu.VMEM((320, 128), F32)],
        flops=5_000_000,
    )(pos, full, side)
    halo = shared(split_send(pay, "gy", 1))
    mid = jnp.stack([halo[0], pay, halo[1]])
    sides = shared(jnp.stack([split_send(mid, "gx", 1), split_send(mid, "gx", 2)]))
    deep_solution = call(
        functools.partial(deep_kernel, sizes),
        struct((1, 2, 16), F32),
        [smem, vmem, vmem],
        [pltpu.VMEM((3, 10, 16, 128), F32), pltpu.VMEM((320, 128), F32)],
    )(pos, mid, sides)
    return (fine_solution, coarse_solution, deep_solution)


def solution(mesh):
    return jax.shard_map(
        per_device,
        mesh=mesh,
        in_specs=(
            P(("gx", "gy", "gz"), None, None),
            P(("gx", "gy", "gz"), None, None),
            P("gx", "gy", "gz"),
            P("gx", "gy", "gz"),
            P(("gx", "gy", "gz")),
            P(("gx", "gy", "gz")),
        ),
        out_specs=(P(("gx", "gy", "gz"), None, None), P("gx", "gy", "gz"), P("gx", "gy", "gz")),
        check_vma=False,
    )
```

```python
import functools

import jax
import jax.numpy as jnp
from jax import lax
from jax.experimental import pallas as pl
from jax.experimental.pallas import tpu as pltpu
from jax.sharding import PartitionSpec as P

DAMPING = 6.0 / 7.0
REST = 1.0 - DAMPING
F32 = jnp.float32
BF16 = jnp.bfloat16
CORES = 2
VMEM_BYTES = 40 * 1024 * 1024
MOST_VMEM = 60 * 1024 * 1024


def iota(shape, dim):
    return lax.broadcasted_iota(jnp.int32, shape, dim)


def split(values):
    high = values.astype(BF16)
    return high, (values - high.astype(F32)).astype(BF16)


def small(a, b):
    return jnp.dot(a.astype(BF16), b.astype(BF16), preferred_element_type=F32)


def dot(a, picks):
    high, low = split(a)
    return small(high, picks) + small(low, picks)


def pick(picks, a):
    high, low = split(a)
    return small(picks, high) + small(picks, low)


def turned(a, b):
    return lax.dot_general(
        a.astype(BF16), b, (((1,), (1,)), ((), ())), preferred_element_type=F32
    )


def after(values, axis):
    return pltpu.roll(values, values.shape[axis] - 1, axis)


def before(values, axis):
    return pltpu.roll(values, 1, axis)


def inverse(values):
    guess = pl.reciprocal(values, approx=True)
    return guess * (2.0 - values * guess)


def fine_kernel(
    count_ref, target_hbm, rhs_hbm, coef_hbm, grid_hbm, cond_hbm, solved_hbm, send_ref, low_ref, high_ref,
    target_ref, rhs_ref, coef_ref, grid_ref, cond_ref, solved_ref, sems
):
    live = count_ref[0]
    loads = [
        pltpu.make_async_copy(coef_hbm, coef_ref, sems.at[0]),
        pltpu.make_async_copy(rhs_hbm, rhs_ref, sems.at[1]),
        pltpu.make_async_copy(target_hbm, target_ref, sems.at[2]),
        pltpu.make_async_copy(grid_hbm, grid_ref, sems.at[3]),
        pltpu.make_async_copy(cond_hbm, cond_ref, sems.at[4]),
    ]
    for load in loads:
        load.start()
    half = rhs_ref.shape[0] // 2
    loads[0].wait()
    k = coef_ref[...].astype(F32) * 0.5
    h = jnp.concatenate([k[:half], k[half:]], axis=2)
    shape = h.shape
    x, lane = iota(shape, 1), iota(shape, 2)
    y, z = (lane >> 3) & 7, lane & 7

    def wrapped(values, amount):
        return pltpu.roll(values, amount % 128, 2)

    hx = jnp.where(x < 7, after(h, 1), 0.0)
    hy = jnp.where(y < 7, wrapped(h, -8), 0.0)
    hz = jnp.where(z < 7, wrapped(h, -1), 0.0)
    diagonal = 6.0 * h + hx + hy + hz
    diagonal += jnp.where(x > 0, before(h, 1), 0.0)
    diagonal += jnp.where(y > 0, wrapped(h, 8), 0.0)
    diagonal += jnp.where(z > 0, wrapped(h, 1), 0.0)
    wx = jnp.where(x < 7, h + hx, 0.0)
    wy = jnp.where(y < 7, h + hy, 0.0)
    wz = jnp.where(z < 7, h + hz, 0.0)

    def sides(u):
        total = wx * after(u, 1) + before(wx * u, 1)
        total += wy * wrapped(u, -8) + wrapped(wy * u, 8)
        return total + wz * wrapped(u, -1) + wrapped(wz * u, 1)

    scale = DAMPING * inverse(diagonal)
    loads[1].wait()
    source = jnp.concatenate([rhs_ref[:half], rhs_ref[half:]], axis=2)
    first = source * scale
    second = first + scale * (REST * source + sides(first))
    residue = source - diagonal * second + sides(second)
    slot = iota((half, 8, 64), 0)
    solved_ref[:half] = jnp.where(slot < live, second[:, :, :64], 0.0)
    solved_ref[half:] = jnp.where(slot + half < live, second[:, :, 64:], 0.0)
    store = pltpu.make_async_copy(solved_ref, solved_hbm, sems.at[5])
    store.start()

    loads[2].wait()
    square = (128, 128)
    row, col = iota(square, 0), iota(square, 1)
    iz, ix, iy = (col >> 4) & 3, (col >> 2) & 3, col & 3
    match = (((row >> 4) & 3) == iy) & (((row >> 1) & 3) == iz)
    keep = ((row >> 1) & 3) == ix
    cells = residue.reshape(square)
    parts = []
    for number in range(2):
        gather = jnp.where(match & ((row >> 6) == number), 0.5, 0.0)
        parts.append(jnp.where(keep, dot(cells, gather), 0.0))

    wide = (32, 256)
    spread = jnp.where(iota(wide, 0) == (iota(wide, 1) >> 3), 1.0, 0.0)
    names = jnp.broadcast_to(target_ref[...].astype(F32), (8, 32))
    name = (dot(names, spread)[:1] + 0.5).astype(jnp.int32)
    names = jnp.broadcast_to(name, wide)
    row, col = iota(wide, 0), iota(wide, 1)
    own = jnp.sum(jnp.where(col == row * 8, names, 0).astype(F32), axis=1, keepdims=True)
    own = own.astype(jnp.int32)
    earlier = ((own >> 8) == (names >> 8)) & (row < (col >> 3))
    rank = jnp.sum(jnp.where(earlier, 1.0, 0.0), axis=0, keepdims=True).astype(jnp.int32)
    wide = (128, 256)
    row, col = iota(wide, 0), iota(wide, 1)
    chip = (row >> 4) + ((row >> 1) & 3) - 1
    owner = chip * 2 + (row & 1)
    wanted = ((row & 7) < 6) & (chip >= 0) & (chip < 8) & ((col >> 3) < live)
    chosen = wanted & (owner == (name >> 8))
    packed, tags = [], []
    for number in range(2):
        mine = chosen & (rank == number)
        picked = jnp.where(mine, 1.0, 0.0)
        packed.append(pick(picked[:, :128], parts[0]) + pick(picked[:, 128:], parts[1]))
        tag = jnp.where(mine & ((col & 7) == 0), (name & 255) + 1, 0).astype(F32)
        tags.append(jnp.sum(tag, axis=1, keepdims=True))
    row, col = iota(square, 0), iota(square, 1)
    place = (row & 7) * 2
    tags = jnp.where(col == place, tags[0], 0.0) + jnp.where(col == place + 1, tags[1], 0.0)
    lift = jnp.where(((row & 7) == 6) & ((row >> 3) == (col >> 3)), 1.0, 0.0)
    send_ref[...] = jnp.where(col < 64, packed[0], packed[1]) + small(lift, tags)
    loads[3].wait()
    loads[4].wait()
    k = cond_ref[...].astype(F32) * 0.5
    low_ref[0] = grid_ref[:, 0:8]
    low_ref[1] = k[:, 0:8]
    high_ref[0] = grid_ref[:, 8:16]
    high_ref[1] = k[:, 8:16]
    store.wait()


def place_kernel(pos_ref, got_ref, chip_ref, source_ref, pay_ref, sems):
    first = jnp.where(pos_ref[2] == 0, 1, 0)
    copies = [
        pltpu.make_async_copy(
            chip_ref.at[number, 1, pl.ds(first, 7)], pay_ref.at[number, pl.ds(6, 7)], sems.at[number]
        )
        for number in range(2)
    ]
    for copy in copies:
        copy.start()
    square = (128, 128)
    row, col = iota(square, 0), iota(square, 1)
    slot = (row >> 4) & 1
    tags = jnp.concatenate([got_ref[pl.ds(6, 16, stride=8), :]] * 8, axis=0)
    tags = jnp.where((col & 1) == slot, tags, 0.0).astype(BF16)
    some = (16, 128)
    across = turned(jnp.where((iota(some, 1) >> 1) == iota(some, 0), 1.0, 0.0), tags)
    across = (across + 0.5).astype(jnp.int32) - 1
    wide = (128, 768)
    spread = jnp.where((iota(wide, 0) >> 1) == (iota(wide, 1) >> 7), 1.0, 0.0)
    down = (small(tags, spread) + 0.5).astype(jnp.int32) - 1
    lane = iota(wide, 1)
    right = ((down & 31) == ((lane & 127) >> 2)) & ((lane & 3) == (iota(wide, 0) >> 5))
    right = jnp.where(right, 1.0, 0.0).astype(BF16)
    mask = (col >> 4) == slot * 4 + (row >> 5)
    some = (32, 128)
    cell = (iota(some, 0) >> 3) * 4 + (iota(some, 0) & 3)
    select = jnp.where((iota(some, 1) & 15) == cell, 1.0, 0.0)
    half = iota((8, 128), 0) >> 2

    def place(owner, tiles):
        got = got_ref[pl.ds(owner, 16, stride=8), :]
        slices = jnp.where(mask, jnp.concatenate([got] * 8, axis=0), 0.0)
        high, low = split(slices)
        left = turned(select, high) + turned(select, low)
        name = jnp.broadcast_to(across[owner : owner + 1], (8, 128))
        here = {
            (x, t): ((name >> 7) == x) & (((name >> 5) & 3) == 2 * t + half)
            for x in range(2)
            for t in tiles
        }
        places = [(x, t) for x in range(8) for t in tiles]
        values = jnp.concatenate(
            [jnp.where(here[x >> 2, t], left[8 * (x & 3) : 8 * (x & 3) + 8], 0.0) for x, t in places],
            axis=0,
        )
        marks = jnp.concatenate(
            [jnp.where(here[x >> 2, t], 1.0, 0.0) for x, t in places if x % 4 == 0], axis=0
        )
        put = right[:, 128 * owner : 128 * owner + 128]
        placed = dot(values, put).reshape(8, 8 * len(tiles), 128)
        covered = small(marks, put).reshape(2, 8 * len(tiles), 128) > 0.5
        return placed, covered

    for number in range(2):
        for part, (tiles, start) in enumerate((((1,), 0), ((0, 1), 8), ((0,), 24))):
            placed, covered = place(2 * part + number, tiles)
            lines = slice(start, start + 8 * len(tiles))
            old = chip_ref[number, 0, :, lines]
            for x in range(2):
                four = slice(4 * x, 4 * x + 4)
                source_ref[number, four, lines] = jnp.where(covered[x], placed[four], old[four])
    for number in range(2):
        pay_ref[number, 0:6] = source_ref[number, pl.ds(2 * first, 6)]
    for copy in copies:
        copy.wait()


def pair_matrix(size):
    shape = (size, 128)
    return jnp.where((iota(shape, 0) >> 1) == iota(shape, 1), 1.0, 0.0)


def prepare(h, inside, depth):
    mid = h[1:-1]
    lane = iota(mid.shape, 2)
    hy = after(mid, 1)
    hz = jnp.where(lane < depth - 1, after(mid, 2), 0.0)
    diagonal = 6.0 * mid + h[:-2] + h[2:] + hy + before(mid, 1) + hz
    diagonal += jnp.where(lane > 0, before(mid, 2), 0.0)
    scale = jnp.where(inside & (lane < depth), DAMPING * inverse(diagonal), 0.0)
    wx = h[:-1] + h[1:]
    wy = mid + hy
    wz = jnp.where(lane < depth - 1, mid + hz, 0.0)
    return diagonal, scale, wx, wy, wz


def neighbours(u, wx, wy, wz):
    mid = u[1:-1]
    total = wx[1:] * u[2:] + wx[:-1] * u[:-2]
    total += wy * after(mid, 1) + before(wy * mid, 1)
    return total + wz * after(mid, 2) + before(wz * mid, 2)


def within(shape, start, first_layer, first_row, sizes):
    x = iota(shape, 0) + (start[0] + first_layer)
    y = iota(shape, 1) + (start[1] + first_row)
    return (x >= 0) & (x < sizes[0]) & (y >= 0) & (y < sizes[1])


def coarser(values, matrix, scale, rows_ref):
    layers, rows, depth = values.shape
    values = values.reshape(layers // 2, 2, rows, depth)
    values = values[:, 0] + values[:, 1]
    flat = dot(values.reshape(layers // 2 * rows, depth), matrix) * scale
    count = flat.shape[0]
    rows_ref[:count] = flat
    total = rows_ref[pl.ds(0, count // 2, stride=2), :] + rows_ref[pl.ds(1, count // 2, stride=2), :]
    return total.reshape(layers // 2, rows // 2, 128)


def base_kernel(
    sizes, pos_ref, source_ref, chip_ref, side_ref, out_ref, pay_ref,
    s_ref, h_ref, wx_ref, wy_ref, wz_ref, diag_ref, scale_ref, first_ref, second_ref,
    res_ref, rows_ref,
):
    gx, gy, core = pos_ref[0], pos_ref[1], pos_ref[2]
    for number in range(2):
        lanes = slice(128 * number, 128 * number + 128)
        s_ref[0:6, :, lanes] = side_ref[0, number, 0:6]
        s_ref[6:14, :, lanes] = source_ref[number]
        s_ref[14:20, :, lanes] = side_ref[1, number, 0:6]
        h_ref[0:7, :, lanes] = side_ref[0, number, 6:13]
        h_ref[7:15, :, lanes] = chip_ref[number, 1]
        h_ref[15:22, :, lanes] = side_ref[1, number, 6:13]
    shape = (32, 256)
    lane = iota(shape, 1)
    y = iota(shape, 0) + (gy * 16 - 8)
    rows_in = (y >= 0) & (y < sizes[1])

    def weigh(layer, _):
        h = h_ref[layer + 1]
        below, above = h_ref[layer], h_ref[layer + 2]
        hy = after(h, 0)
        hz = jnp.where(lane < 255, after(h, 1), 0.0)
        diagonal = 6.0 * h + below + above + hy + before(h, 0) + hz
        diagonal += jnp.where(lane > 0, before(h, 1), 0.0)
        x = gx * 8 + layer - 6
        inside = rows_in & (x >= 0) & (x < sizes[0])
        scale = jnp.where(inside, DAMPING * inverse(diagonal), 0.0)
        diag_ref[layer] = diagonal
        scale_ref[layer] = scale
        wx_ref[layer] = h + above
        wy_ref[layer] = h + hy
        wz_ref[layer] = jnp.where(lane < 255, h + hz, 0.0)
        first_ref[layer] = s_ref[layer] * scale
        return 0

    lax.fori_loop(0, 20, weigh, 0, unroll=True)

    def sides(ref, layer):
        u, wy, wz = ref[layer], wy_ref[layer], wz_ref[layer]
        total = wx_ref[layer] * ref[layer + 1] + wx_ref[layer - 1] * ref[layer - 1]
        total += wy * after(u, 0) + before(wy * u, 0)
        return u, total + wz * after(u, 1) + before(wz * u, 1)

    def correct(layer, _):
        u, total = sides(first_ref, layer)
        second_ref[layer] = u + scale_ref[layer] * (REST * s_ref[layer] + total)
        return 0

    lax.fori_loop(1, 19, correct, 0, unroll=True)

    def leave(layer, _):
        u, total = sides(second_ref, layer)
        res_ref[layer - 2] = s_ref[layer] - diag_ref[layer] * u + total
        return 0

    lax.fori_loop(2, 18, leave, 0, unroll=True)
    own = second_ref[6:14, 8:24, :]
    out_ref[...] = jnp.where(core == 0, own[:, :, :128], own[:, :, 128:])

    zoom = pair_matrix(256)
    source = coarser(res_ref[...], zoom, 0.5, rows_ref)
    h = coarser(h_ref[1:21], zoom, 0.125, rows_ref)
    inside = within(source.shape, (gx * 4, gy * 8), -2, -4, (sizes[0] // 2, sizes[1] // 2))
    diagonal, scale, wx, wy, wz = prepare(h, inside, 128)
    first = source * scale
    total = neighbours(first, wx[1:-1], wy[1:-1], wz[1:-1])
    second = first[1:-1] + scale[1:-1] * (REST * source[1:-1] + total)
    total = neighbours(second, wx[2:-2], wy[2:-2], wz[2:-2])
    residue = source[2:-2] - diagonal[2:-2] * second[1:-1] + total

    zoom = pair_matrix(128)
    source = coarser(residue, zoom, 0.5, rows_ref)
    h = coarser(h[1:-1], zoom, 0.125, rows_ref)
    _, scale, _, _, _ = prepare(h, jnp.full(source.shape, True), 64)
    pay_ref[0:2] = source[:, 2:6]
    pay_ref[2:4] = (source * scale)[:, 2:6]
    pay_ref[4:6] = h[1:3, 2:6]


def deep_kernel(sizes, pos_ref, mid_ref, side_ref, out_ref, win_ref, rows_ref):
    gx, gy, core = pos_ref[0], pos_ref[1], pos_ref[2]
    win_ref[...] = jnp.zeros(win_ref.shape, F32)
    for number in range(3):
        for part in range(3):
            blocks = [
                side_ref[0, 1, part], side_ref[0, 0, part], mid_ref[part],
                side_ref[1, 0, part], side_ref[1, 1, part],
            ]
            for place, block in enumerate(blocks):
                win_ref[number, 2 * place : 2 * place + 2, 4 * part : 4 * part + 4] = block[
                    2 * number : 2 * number + 2
                ]
    source, first, h = win_ref[0], win_ref[1], win_ref[2]
    shape = (8, 16, 128)
    inside = within(shape, (gx * 2, gy * 4), -3, -4, (sizes[0] // 4, sizes[1] // 4))
    inside &= iota(shape, 1) < 12
    diagonal, scale, wx, wy, wz = prepare(h, inside, 64)
    total = neighbours(first, wx, wy, wz)
    second = first[1:-1] + scale * (REST * source[1:-1] + total)
    total = neighbours(second, wx[1:-1], wy[1:-1], wz[1:-1])
    residue = source[2:-2] - diagonal[1:-1] * second[1:-1] + total

    zoom = pair_matrix(128)
    source = coarser(residue, zoom, 0.5, rows_ref)
    h = coarser(h, zoom, 0.125, rows_ref)
    inside = within(source.shape, (gx, gy * 2), -1, -2, (sizes[0] // 8, sizes[1] // 8))
    inside &= iota(source.shape, 1) < 6
    _, scale, wx, wy, wz = prepare(h, inside, 32)
    first = source * scale
    total = neighbours(first, wx[1:-1], wy[1:-1], wz[1:-1])
    second = first[1:-1] + scale[1:-1] * (REST * source[1:-1] + total)
    second = second[:, 2:4]
    out_ref[...] = jnp.where(core == 0, second[:, :, :16], second[:, :, 16:32])


def call(kernel, out_shape, in_specs, scratch=(), flops=100_000, outs=None, vmem=VMEM_BYTES):
    specs = {} if outs is None else {"out_specs": outs}
    return pl.pallas_call(
        kernel,
        out_shape=out_shape,
        scratch_shapes=list(scratch),
        compiler_params=pltpu.CompilerParams(vmem_limit_bytes=vmem),
        cost_estimate=pl.CostEstimate(flops=flops, bytes_accessed=flops, transcendentals=0),
        in_specs=in_specs,
        **specs,
    )


def split_send(values, axis, step):
    count = lax.axis_size(axis)
    pairs = []
    for place in range(count):
        if place + step < count:
            pairs.append((place * CORES, (place + step) * CORES))
        if place - step >= 0:
            pairs.append((place * CORES + 1, (place - step) * CORES + 1))
    return lax.ppermute(values, (axis, "gz"), pairs)


def exchanged(up, down, axis):
    count = lax.axis_size(axis)
    pairs = [(place, place + 1) for place in range(count - 1)]
    back = [(target, source) for source, target in pairs]
    return lax.ppermute(up, axis, pairs), lax.ppermute(down, axis, back)


def shared(values):
    return lax.all_gather(values, "gz")


def per_device(fine_rhs, fine_coef, coarse_rhs, coarse_coef, patch_count, patch_target):
    core = lax.axis_index("gz")
    pos = jnp.stack([lax.axis_index("gx"), lax.axis_index("gy"), core])
    sizes = (
        lax.axis_size("gx") * coarse_rhs.shape[0],
        lax.axis_size("gy") * coarse_rhs.shape[1],
    )
    vmem = pl.BlockSpec(memory_space=pltpu.VMEM)
    smem = pl.BlockSpec(memory_space=pltpu.SMEM)
    struct = jax.ShapeDtypeStruct
    hbm = pl.BlockSpec(memory_space=pltpu.HBM)
    edge = struct((2, 8, 8, 128), F32)
    fine_solution, send, low, high = call(
        fine_kernel,
        (struct(fine_rhs.shape, F32), struct((128, 128), F32), edge, edge),
        [smem, hbm, hbm, hbm, hbm, hbm],
        [
            pltpu.VMEM((1, 32), jnp.int32),
            pltpu.VMEM(fine_rhs.shape, F32),
            pltpu.VMEM(fine_coef.shape, fine_coef.dtype),
            pltpu.VMEM(coarse_rhs.shape, F32),
            pltpu.VMEM(coarse_coef.shape, coarse_coef.dtype),
            pltpu.VMEM(fine_rhs.shape, F32),
            pltpu.SemaphoreType.DMA((6,)),
        ],
        outs=[hbm, vmem, vmem, vmem],
        vmem=MOST_VMEM,
    )(patch_count, patch_target.reshape(1, 32), fine_rhs, fine_coef, coarse_rhs, coarse_coef)
    got = lax.all_to_all(send.reshape(16, 8, 128), ("gy", "gz"), 0, 0).reshape(128, 128)
    below, above = exchanged(high, low, "gy")
    chip = shared(jnp.concatenate([below, low, high, above], axis=2))
    source, pay = call(
        place_kernel,
        (struct((2, 8, 32, 128), F32), struct((2, 13, 32, 128), F32)),
        [smem, vmem, vmem],
        [pltpu.SemaphoreType.DMA((2,))],
        outs=[vmem] * 2,
    )(pos, got, chip)
    side = shared(split_send(pay, "gx", 1))
    grid = (32, 256)
    coarse_solution, pay = call(
        functools.partial(base_kernel, sizes),
        (struct((8, 16, 128), F32), struct((6, 4, 128), F32)),
        [smem, vmem, vmem, vmem],
        [pltpu.VMEM((20, *grid), F32), pltpu.VMEM((22, *grid), F32)]
        + [pltpu.VMEM((20, *grid), F32)] * 7
        + [pltpu.VMEM((16, *grid), F32), pltpu.VMEM((320, 128), F32)],
        flops=5_000_000,
        outs=[vmem] * 2,
    )(pos, source, chip, side)
    halo = shared(split_send(pay, "gy", 1))
    mid = jnp.stack([halo[0], pay, halo[1]])
    sides = shared(jnp.stack([split_send(mid, "gx", 1), split_send(mid, "gx", 2)]))
    deep_solution = call(
        functools.partial(deep_kernel, sizes),
        struct((1, 2, 16), F32),
        [smem, vmem, vmem],
        [pltpu.VMEM((3, 10, 16, 128), F32), pltpu.VMEM((320, 128), F32)],
    )(pos, mid, sides)
    return (fine_solution, coarse_solution, deep_solution)


def solution(mesh):
    return jax.shard_map(
        per_device,
        mesh=mesh,
        in_specs=(
            P(("gx", "gy", "gz"), None, None),
            P(("gx", "gy", "gz"), None, None),
            P("gx", "gy", "gz"),
            P("gx", "gy", "gz"),
            P(("gx", "gy", "gz")),
            P(("gx", "gy", "gz")),
        ),
        out_specs=(P(("gx", "gy", "gz"), None, None), P("gx", "gy", "gz"), P("gx", "gy", "gz")),
        check_vma=False,
    )
```

```python
import functools

import jax
import jax.numpy as jnp
from jax import lax
from jax.experimental import pallas as pl
from jax.experimental.pallas import tpu as pltpu
from jax.sharding import PartitionSpec as P

DAMPING = 6.0 / 7.0
REST = 1.0 - DAMPING
F32 = jnp.float32
BF16 = jnp.bfloat16
CORES = 2
VMEM_BYTES = 40 * 1024 * 1024
MOST_VMEM = 60 * 1024 * 1024


def iota(shape, dim):
    return lax.broadcasted_iota(jnp.int32, shape, dim)


def split(values):
    high = values.astype(BF16)
    return high, (values - high.astype(F32)).astype(BF16)


def small(a, b):
    return jnp.dot(a.astype(BF16), b.astype(BF16), preferred_element_type=F32)


def dot(a, picks):
    high, low = split(a)
    return small(high, picks) + small(low, picks)


def pick(picks, a):
    high, low = split(a)
    return small(picks, high) + small(picks, low)


def turned(a, b):
    return lax.dot_general(
        a.astype(BF16), b, (((1,), (1,)), ((), ())), preferred_element_type=F32
    )


def after(values, axis):
    return pltpu.roll(values, values.shape[axis] - 1, axis)


def before(values, axis):
    return pltpu.roll(values, 1, axis)


def inverse(values):
    guess = pl.reciprocal(values, approx=True)
    return guess * (2.0 - values * guess)


def fine_kernel(
    count_ref, target_hbm, rhs_hbm, coef_hbm, grid_hbm, cond_hbm, solved_hbm, send_ref, own_ref,
    target_ref, rhs_ref, coef_ref, grid_ref, cond_ref, solved_ref, sems
):
    live = count_ref[0]
    loads = [
        pltpu.make_async_copy(coef_hbm, coef_ref, sems.at[0]),
        pltpu.make_async_copy(rhs_hbm, rhs_ref, sems.at[1]),
        pltpu.make_async_copy(target_hbm, target_ref, sems.at[2]),
        pltpu.make_async_copy(grid_hbm, grid_ref, sems.at[3]),
        pltpu.make_async_copy(cond_hbm, cond_ref, sems.at[4]),
    ]
    for load in loads:
        load.start()
    half = rhs_ref.shape[0] // 2
    loads[0].wait()
    k = coef_ref[...].astype(F32) * 0.5
    h = jnp.concatenate([k[:half], k[half:]], axis=2)
    shape = h.shape
    x, lane = iota(shape, 1), iota(shape, 2)
    y, z = (lane >> 3) & 7, lane & 7

    def wrapped(values, amount):
        return pltpu.roll(values, amount % 128, 2)

    hx = jnp.where(x < 7, after(h, 1), 0.0)
    hy = jnp.where(y < 7, wrapped(h, -8), 0.0)
    hz = jnp.where(z < 7, wrapped(h, -1), 0.0)
    diagonal = 6.0 * h + hx + hy + hz
    diagonal += jnp.where(x > 0, before(h, 1), 0.0)
    diagonal += jnp.where(y > 0, wrapped(h, 8), 0.0)
    diagonal += jnp.where(z > 0, wrapped(h, 1), 0.0)
    wx = jnp.where(x < 7, h + hx, 0.0)
    wy = jnp.where(y < 7, h + hy, 0.0)
    wz = jnp.where(z < 7, h + hz, 0.0)

    def sides(u):
        total = wx * after(u, 1) + before(wx * u, 1)
        total += wy * wrapped(u, -8) + wrapped(wy * u, 8)
        return total + wz * wrapped(u, -1) + wrapped(wz * u, 1)

    scale = DAMPING * inverse(diagonal)
    loads[1].wait()
    source = jnp.concatenate([rhs_ref[:half], rhs_ref[half:]], axis=2)
    first = source * scale
    second = first + scale * (REST * source + sides(first))
    residue = source - diagonal * second + sides(second)
    slot = iota((half, 8, 64), 0)
    solved_ref[:half] = jnp.where(slot < live, second[:, :, :64], 0.0)
    solved_ref[half:] = jnp.where(slot + half < live, second[:, :, 64:], 0.0)
    store = pltpu.make_async_copy(solved_ref, solved_hbm, sems.at[5])
    store.start()

    loads[2].wait()
    square = (128, 128)
    row, col = iota(square, 0), iota(square, 1)
    iz, ix, iy = (col >> 4) & 3, (col >> 2) & 3, col & 3
    match = (((row >> 4) & 3) == iy) & (((row >> 1) & 3) == iz)
    keep = ((row >> 1) & 3) == ix
    cells = residue.reshape(square)
    parts = []
    for number in range(2):
        gather = jnp.where(match & ((row >> 6) == number), 0.5, 0.0)
        parts.append(jnp.where(keep, dot(cells, gather), 0.0))

    wide = (32, 256)
    spread = jnp.where(iota(wide, 0) == (iota(wide, 1) >> 3), 1.0, 0.0)
    names = jnp.broadcast_to(target_ref[...].astype(F32), (8, 32))
    name = (dot(names, spread)[:1] + 0.5).astype(jnp.int32)
    names = jnp.broadcast_to(name, wide)
    row, col = iota(wide, 0), iota(wide, 1)
    own = jnp.sum(jnp.where(col == row * 8, names, 0).astype(F32), axis=1, keepdims=True)
    own = own.astype(jnp.int32)
    earlier = ((own >> 8) == (names >> 8)) & (row < (col >> 3))
    rank = jnp.sum(jnp.where(earlier, 1.0, 0.0), axis=0, keepdims=True).astype(jnp.int32)
    wide = (128, 256)
    row, col = iota(wide, 0), iota(wide, 1)
    chip = (row >> 4) + ((row >> 1) & 3) - 1
    owner = chip * 2 + (row & 1)
    wanted = ((row & 7) < 6) & (chip >= 0) & (chip < 8) & ((col >> 3) < live)
    chosen = wanted & (owner == (name >> 8))
    packed, tags = [], []
    for number in range(2):
        mine = chosen & (rank == number)
        picked = jnp.where(mine, 1.0, 0.0)
        packed.append(pick(picked[:, :128], parts[0]) + pick(picked[:, 128:], parts[1]))
        tag = jnp.where(mine & ((col & 7) == 0), (name & 255) + 1, 0).astype(F32)
        tags.append(jnp.sum(tag, axis=1, keepdims=True))
    row, col = iota(square, 0), iota(square, 1)
    place = (row & 7) * 2
    tags = jnp.where(col == place, tags[0], 0.0) + jnp.where(col == place + 1, tags[1], 0.0)
    lift = jnp.where(((row & 7) == 6) & ((row >> 3) == (col >> 3)), 1.0, 0.0)
    send_ref[...] = jnp.where(col < 64, packed[0], packed[1]) + small(lift, tags)
    loads[3].wait()
    loads[4].wait()
    own_ref[0] = grid_ref[...]
    own_ref[1] = cond_ref[...].astype(F32) * 0.5
    store.wait()


def place_kernel(pos_ref, got_ref, chip_ref, source_ref, pay_ref):
    first = jnp.where(pos_ref[2] == 0, 2, 0)
    square = (128, 128)
    row, col = iota(square, 0), iota(square, 1)
    slot = (row >> 4) & 1
    tags = jnp.concatenate([got_ref[pl.ds(6, 16, stride=8), :]] * 8, axis=0)
    tags = jnp.where((col & 1) == slot, tags, 0.0).astype(BF16)
    some = (16, 128)
    across = turned(jnp.where((iota(some, 1) >> 1) == iota(some, 0), 1.0, 0.0), tags)
    across = (across + 0.5).astype(jnp.int32) - 1
    wide = (128, 768)
    spread = jnp.where((iota(wide, 0) >> 1) == (iota(wide, 1) >> 7), 1.0, 0.0)
    down = (small(tags, spread) + 0.5).astype(jnp.int32) - 1
    lane = iota(wide, 1)
    right = ((down & 31) == ((lane & 127) >> 2)) & ((lane & 3) == (iota(wide, 0) >> 5))
    right = jnp.where(right, 1.0, 0.0).astype(BF16)
    mask = (col >> 4) == slot * 4 + (row >> 5)
    some = (32, 128)
    cell = (iota(some, 0) >> 3) * 4 + (iota(some, 0) & 3)
    select = jnp.where((iota(some, 1) & 15) == cell, 1.0, 0.0)
    half = iota((8, 128), 0) >> 2

    def place(owner, tiles):
        got = got_ref[pl.ds(owner, 16, stride=8), :]
        slices = jnp.where(mask, jnp.concatenate([got] * 8, axis=0), 0.0)
        high, low = split(slices)
        left = turned(select, high) + turned(select, low)
        name = jnp.broadcast_to(across[owner : owner + 1], (8, 128))
        here = {
            (x, t): ((name >> 7) == x) & (((name >> 5) & 3) == 2 * t + half)
            for x in range(2)
            for t in tiles
        }
        places = [(x, t) for x in range(8) for t in tiles]
        values = jnp.concatenate(
            [jnp.where(here[x >> 2, t], left[8 * (x & 3) : 8 * (x & 3) + 8], 0.0) for x, t in places],
            axis=0,
        )
        marks = jnp.concatenate(
            [jnp.where(here[x >> 2, t], 1.0, 0.0) for x, t in places if x % 4 == 0], axis=0
        )
        put = right[:, 128 * owner : 128 * owner + 128]
        placed = dot(values, put).reshape(8, 8 * len(tiles), 128)
        covered = small(marks, put).reshape(2, 8 * len(tiles), 128) > 0.5
        return placed, covered

    for number in range(2):
        for part, (tiles, start) in enumerate((((1,), 0), ((0, 1), 8), ((0,), 24))):
            placed, covered = place(2 * part + number, tiles)
            lines = slice(start, start + 8 * len(tiles))
            old = chip_ref[number, 0, :, lines]
            for x in range(2):
                four = slice(4 * x, 4 * x + 4)
                source_ref[number, four, lines] = jnp.where(covered[x], placed[four], old[four])
    for number in range(2):
        pay_ref[number] = source_ref[number, pl.ds(first, 6)]


def pair_matrix(size):
    shape = (size, 128)
    return jnp.where((iota(shape, 0) >> 1) == iota(shape, 1), 1.0, 0.0)


def prepare(h, inside, depth):
    mid = h[1:-1]
    lane = iota(mid.shape, 2)
    hy = after(mid, 1)
    hz = jnp.where(lane < depth - 1, after(mid, 2), 0.0)
    diagonal = 6.0 * mid + h[:-2] + h[2:] + hy + before(mid, 1) + hz
    diagonal += jnp.where(lane > 0, before(mid, 2), 0.0)
    scale = jnp.where(inside & (lane < depth), DAMPING * inverse(diagonal), 0.0)
    wx = h[:-1] + h[1:]
    wy = mid + hy
    wz = jnp.where(lane < depth - 1, mid + hz, 0.0)
    return diagonal, scale, wx, wy, wz


def neighbours(u, wx, wy, wz):
    mid = u[1:-1]
    total = wx[1:] * u[2:] + wx[:-1] * u[:-2]
    total += wy * after(mid, 1) + before(wy * mid, 1)
    return total + wz * after(mid, 2) + before(wz * mid, 2)


def within(shape, start, first_layer, first_row, sizes):
    x = iota(shape, 0) + (start[0] + first_layer)
    y = iota(shape, 1) + (start[1] + first_row)
    return (x >= 0) & (x < sizes[0]) & (y >= 0) & (y < sizes[1])


def coarser(values, matrix, scale, rows_ref):
    layers, rows, depth = values.shape
    values = values.reshape(layers // 2, 2, rows, depth)
    values = values[:, 0] + values[:, 1]
    flat = dot(values.reshape(layers // 2 * rows, depth), matrix) * scale
    count = flat.shape[0]
    rows_ref[:count] = flat
    total = rows_ref[pl.ds(0, count // 2, stride=2), :] + rows_ref[pl.ds(1, count // 2, stride=2), :]
    return total.reshape(layers // 2, rows // 2, 128)


def base_kernel(
    sizes, pos_ref, source_ref, chip_ref, side_ref, out_ref, pay_ref,
    s_ref, h_ref, wx_ref, wy_ref, wz_ref, diag_ref, scale_ref, first_ref, second_ref,
    res_ref, rows_ref,
):
    gx, gy, core = pos_ref[0], pos_ref[1], pos_ref[2]
    for number in range(2):
        lanes = slice(128 * number, 128 * number + 128)
        s_ref[0:6, :, lanes] = side_ref[0, number, 0:6]
        s_ref[6:14, :, lanes] = source_ref[number]
        s_ref[14:20, :, lanes] = side_ref[1, number, 0:6]
        h_ref[0:7, :, lanes] = side_ref[0, number, 6:13]
        h_ref[7:15, :, lanes] = chip_ref[number, 1]
        h_ref[15:22, :, lanes] = side_ref[1, number, 6:13]
    shape = (32, 256)
    lane = iota(shape, 1)
    y = iota(shape, 0) + (gy * 16 - 8)
    rows_in = (y >= 0) & (y < sizes[1])

    def weigh(layer, _):
        h = h_ref[layer + 1]
        below, above = h_ref[layer], h_ref[layer + 2]
        hy = after(h, 0)
        hz = jnp.where(lane < 255, after(h, 1), 0.0)
        diagonal = 6.0 * h + below + above + hy + before(h, 0) + hz
        diagonal += jnp.where(lane > 0, before(h, 1), 0.0)
        x = gx * 8 + layer - 6
        inside = rows_in & (x >= 0) & (x < sizes[0])
        scale = jnp.where(inside, DAMPING * inverse(diagonal), 0.0)
        diag_ref[layer] = diagonal
        scale_ref[layer] = scale
        wx_ref[layer] = h + above
        wy_ref[layer] = h + hy
        wz_ref[layer] = jnp.where(lane < 255, h + hz, 0.0)
        first_ref[layer] = s_ref[layer] * scale
        return 0

    lax.fori_loop(0, 20, weigh, 0, unroll=True)

    def sides(ref, layer):
        u, wy, wz = ref[layer], wy_ref[layer], wz_ref[layer]
        total = wx_ref[layer] * ref[layer + 1] + wx_ref[layer - 1] * ref[layer - 1]
        total += wy * after(u, 0) + before(wy * u, 0)
        return u, total + wz * after(u, 1) + before(wz * u, 1)

    def correct(layer, _):
        u, total = sides(first_ref, layer)
        second_ref[layer] = u + scale_ref[layer] * (REST * s_ref[layer] + total)
        return 0

    lax.fori_loop(1, 19, correct, 0, unroll=True)

    def leave(layer, _):
        u, total = sides(second_ref, layer)
        res_ref[layer - 2] = s_ref[layer] - diag_ref[layer] * u + total
        return 0

    lax.fori_loop(2, 18, leave, 0, unroll=True)
    own = second_ref[6:14, 8:24, :]
    out_ref[...] = jnp.where(core == 0, own[:, :, :128], own[:, :, 128:])

    zoom = pair_matrix(256)
    source = coarser(res_ref[...], zoom, 0.5, rows_ref)
    h = coarser(h_ref[1:21], zoom, 0.125, rows_ref)
    inside = within(source.shape, (gx * 4, gy * 8), -2, -4, (sizes[0] // 2, sizes[1] // 2))
    diagonal, scale, wx, wy, wz = prepare(h, inside, 128)
    first = source * scale
    total = neighbours(first, wx[1:-1], wy[1:-1], wz[1:-1])
    second = first[1:-1] + scale[1:-1] * (REST * source[1:-1] + total)
    total = neighbours(second, wx[2:-2], wy[2:-2], wz[2:-2])
    residue = source[2:-2] - diagonal[2:-2] * second[1:-1] + total

    zoom = pair_matrix(128)
    source = coarser(residue, zoom, 0.5, rows_ref)
    h = coarser(h[1:-1], zoom, 0.125, rows_ref)
    _, scale, _, _, _ = prepare(h, jnp.full(source.shape, True), 64)
    pay_ref[0:2] = source[:, 2:6]
    pay_ref[2:4] = (source * scale)[:, 2:6]
    pay_ref[4:6] = h[1:3, 2:6]


def deep_kernel(sizes, pos_ref, mid_ref, side_ref, out_ref, win_ref, rows_ref):
    gx, gy, core = pos_ref[0], pos_ref[1], pos_ref[2]
    win_ref[...] = jnp.zeros(win_ref.shape, F32)
    for number in range(3):
        for part in range(3):
            blocks = [
                side_ref[0, 1, part], side_ref[0, 0, part], mid_ref[part],
                side_ref[1, 0, part], side_ref[1, 1, part],
            ]
            for place, block in enumerate(blocks):
                win_ref[number, 2 * place : 2 * place + 2, 4 * part : 4 * part + 4] = block[
                    2 * number : 2 * number + 2
                ]
    source, first, h = win_ref[0], win_ref[1], win_ref[2]
    shape = (8, 16, 128)
    inside = within(shape, (gx * 2, gy * 4), -3, -4, (sizes[0] // 4, sizes[1] // 4))
    inside &= iota(shape, 1) < 12
    diagonal, scale, wx, wy, wz = prepare(h, inside, 64)
    total = neighbours(first, wx, wy, wz)
    second = first[1:-1] + scale * (REST * source[1:-1] + total)
    total = neighbours(second, wx[1:-1], wy[1:-1], wz[1:-1])
    residue = source[2:-2] - diagonal[1:-1] * second[1:-1] + total

    zoom = pair_matrix(128)
    source = coarser(residue, zoom, 0.5, rows_ref)
    h = coarser(h, zoom, 0.125, rows_ref)
    inside = within(source.shape, (gx, gy * 2), -1, -2, (sizes[0] // 8, sizes[1] // 8))
    inside &= iota(source.shape, 1) < 6
    _, scale, wx, wy, wz = prepare(h, inside, 32)
    first = source * scale
    total = neighbours(first, wx[1:-1], wy[1:-1], wz[1:-1])
    second = first[1:-1] + scale[1:-1] * (REST * source[1:-1] + total)
    second = second[:, 2:4]
    out_ref[...] = jnp.where(core == 0, second[:, :, :16], second[:, :, 16:32])


def call(kernel, out_shape, in_specs, scratch=(), flops=100_000, outs=None, vmem=VMEM_BYTES):
    specs = {} if outs is None else {"out_specs": outs}
    return pl.pallas_call(
        kernel,
        out_shape=out_shape,
        scratch_shapes=list(scratch),
        compiler_params=pltpu.CompilerParams(vmem_limit_bytes=vmem),
        cost_estimate=pl.CostEstimate(flops=flops, bytes_accessed=flops, transcendentals=0),
        in_specs=in_specs,
        **specs,
    )


def split_send(values, axis, step):
    count = lax.axis_size(axis)
    pairs = []
    for place in range(count):
        if place + step < count:
            pairs.append((place * CORES, (place + step) * CORES))
        if place - step >= 0:
            pairs.append((place * CORES + 1, (place - step) * CORES + 1))
    return lax.ppermute(values, (axis, "gz"), pairs)


def exchanged(up, down, axis):
    count = lax.axis_size(axis)
    pairs = [(place, place + 1) for place in range(count - 1)]
    back = [(target, source) for source, target in pairs]
    return lax.ppermute(up, axis, pairs), lax.ppermute(down, axis, back)


def shared(values):
    return lax.all_gather(values, "gz")


def per_device(fine_rhs, fine_coef, coarse_rhs, coarse_coef, patch_count, patch_target):
    core = lax.axis_index("gz")
    pos = jnp.stack([lax.axis_index("gx"), lax.axis_index("gy"), core])
    sizes = (
        lax.axis_size("gx") * coarse_rhs.shape[0],
        lax.axis_size("gy") * coarse_rhs.shape[1],
    )
    vmem = pl.BlockSpec(memory_space=pltpu.VMEM)
    smem = pl.BlockSpec(memory_space=pltpu.SMEM)
    struct = jax.ShapeDtypeStruct
    hbm = pl.BlockSpec(memory_space=pltpu.HBM)
    fine_solution, send, own = call(
        fine_kernel,
        (struct(fine_rhs.shape, F32), struct((128, 128), F32), struct((2, 8, 16, 128), F32)),
        [smem, hbm, hbm, hbm, hbm, hbm],
        [
            pltpu.VMEM((1, 32), jnp.int32),
            pltpu.VMEM(fine_rhs.shape, F32),
            pltpu.VMEM(fine_coef.shape, fine_coef.dtype),
            pltpu.VMEM(coarse_rhs.shape, F32),
            pltpu.VMEM(coarse_coef.shape, coarse_coef.dtype),
            pltpu.VMEM(fine_rhs.shape, F32),
            pltpu.SemaphoreType.DMA((6,)),
        ],
        outs=[hbm, vmem, vmem],
        vmem=MOST_VMEM,
    )(patch_count, patch_target.reshape(1, 32), fine_rhs, fine_coef, coarse_rhs, coarse_coef)
    got = lax.all_to_all(send.reshape(16, 8, 128), ("gy", "gz"), 0, 0).reshape(128, 128)
    below, above = exchanged(own, own, "gy")
    chip = shared(jnp.concatenate([below[:, :, 8:], own, above[:, :, :8]], axis=2))
    edge = split_send(jnp.where(core == 0, chip[:, 1, 1:], chip[:, 1, :7]), "gx", 1)
    source, pay = call(
        place_kernel,
        (struct((2, 8, 32, 128), F32), struct((2, 6, 32, 128), F32)),
        [smem, vmem, vmem],
        outs=[vmem] * 2,
    )(pos, got, chip)
    side = shared(jnp.concatenate([split_send(pay, "gx", 1), edge], axis=1))
    grid = (32, 256)
    coarse_solution, pay = call(
        functools.partial(base_kernel, sizes),
        (struct((8, 16, 128), F32), struct((6, 4, 128), F32)),
        [smem, vmem, vmem, vmem],
        [pltpu.VMEM((20, *grid), F32), pltpu.VMEM((22, *grid), F32)]
        + [pltpu.VMEM((20, *grid), F32)] * 7
        + [pltpu.VMEM((16, *grid), F32), pltpu.VMEM((320, 128), F32)],
        flops=5_000_000,
        outs=[vmem] * 2,
    )(pos, source, chip, side)
    halo = shared(split_send(pay, "gy", 1))
    mid = jnp.stack([halo[0], pay, halo[1]])
    sides = shared(jnp.stack([split_send(mid, "gx", 1), split_send(mid, "gx", 2)]))
    deep_solution = call(
        functools.partial(deep_kernel, sizes),
        struct((1, 2, 16), F32),
        [smem, vmem, vmem],
        [pltpu.VMEM((3, 10, 16, 128), F32), pltpu.VMEM((320, 128), F32)],
    )(pos, mid, sides)
    return (fine_solution, coarse_solution, deep_solution)


def solution(mesh):
    return jax.shard_map(
        per_device,
        mesh=mesh,
        in_specs=(
            P(("gx", "gy", "gz"), None, None),
            P(("gx", "gy", "gz"), None, None),
            P("gx", "gy", "gz"),
            P("gx", "gy", "gz"),
            P(("gx", "gy", "gz")),
            P(("gx", "gy", "gz")),
        ),
        out_specs=(P(("gx", "gy", "gz"), None, None), P("gx", "gy", "gz"), P("gx", "gy", "gz")),
        check_vma=False,
    )
```

```python
import functools

import jax
import jax.numpy as jnp
from jax import lax
from jax.experimental import pallas as pl
from jax.experimental.pallas import tpu as pltpu
from jax.sharding import PartitionSpec as P

DAMPING = 6.0 / 7.0
REST = 1.0 - DAMPING
F32 = jnp.float32
BF16 = jnp.bfloat16
CORES = 2
VMEM_BYTES = 40 * 1024 * 1024
MOST_VMEM = 60 * 1024 * 1024


def iota(shape, dim):
    return lax.broadcasted_iota(jnp.int32, shape, dim)


def split(values):
    high = values.astype(BF16)
    return high, (values - high.astype(F32)).astype(BF16)


def small(a, b):
    return jnp.dot(a.astype(BF16), b.astype(BF16), preferred_element_type=F32)


def dot(a, picks):
    high, low = split(a)
    return small(high, picks) + small(low, picks)


def pick(picks, a):
    high, low = split(a)
    return small(picks, high) + small(picks, low)


def turned(a, b):
    return lax.dot_general(
        a.astype(BF16), b, (((1,), (1,)), ((), ())), preferred_element_type=F32
    )


def after(values, axis):
    return pltpu.roll(values, values.shape[axis] - 1, axis)


def before(values, axis):
    return pltpu.roll(values, 1, axis)


def inverse(values):
    guess = pl.reciprocal(values, approx=True)
    return guess * (2.0 - values * guess)


def fine_kernel(
    count_ref, target_hbm, rhs_hbm, coef_hbm, grid_hbm, cond_hbm, solved_hbm, send_ref, own_ref,
    target_ref, rhs_ref, coef_ref, grid_ref, cond_ref, solved_ref, sems
):
    live = count_ref[0]
    loads = [
        pltpu.make_async_copy(coef_hbm, coef_ref, sems.at[0]),
        pltpu.make_async_copy(rhs_hbm, rhs_ref, sems.at[1]),
        pltpu.make_async_copy(target_hbm, target_ref, sems.at[2]),
        pltpu.make_async_copy(grid_hbm, grid_ref, sems.at[3]),
        pltpu.make_async_copy(cond_hbm, cond_ref, sems.at[4]),
    ]
    for load in loads:
        load.start()
    half = rhs_ref.shape[0] // 2
    loads[0].wait()
    k = coef_ref[...].astype(F32) * 0.5
    h = jnp.concatenate([k[:half], k[half:]], axis=2)
    shape = h.shape
    x, lane = iota(shape, 1), iota(shape, 2)
    y, z = (lane >> 3) & 7, lane & 7

    def wrapped(values, amount):
        return pltpu.roll(values, amount % 128, 2)

    hx = jnp.where(x < 7, after(h, 1), 0.0)
    hy = jnp.where(y < 7, wrapped(h, -8), 0.0)
    hz = jnp.where(z < 7, wrapped(h, -1), 0.0)
    diagonal = 6.0 * h + hx + hy + hz
    diagonal += jnp.where(x > 0, before(h, 1), 0.0)
    diagonal += jnp.where(y > 0, wrapped(h, 8), 0.0)
    diagonal += jnp.where(z > 0, wrapped(h, 1), 0.0)
    wx = jnp.where(x < 7, h + hx, 0.0)
    wy = jnp.where(y < 7, h + hy, 0.0)
    wz = jnp.where(z < 7, h + hz, 0.0)

    def sides(u):
        total = wx * after(u, 1) + before(wx * u, 1)
        total += wy * wrapped(u, -8) + wrapped(wy * u, 8)
        return total + wz * wrapped(u, -1) + wrapped(wz * u, 1)

    scale = DAMPING * inverse(diagonal)
    loads[1].wait()
    source = jnp.concatenate([rhs_ref[:half], rhs_ref[half:]], axis=2)
    first = source * scale
    second = first + scale * (REST * source + sides(first))
    residue = source - diagonal * second + sides(second)
    slot = iota((half, 8, 64), 0)
    solved_ref[:half] = jnp.where(slot < live, second[:, :, :64], 0.0)
    solved_ref[half:] = jnp.where(slot + half < live, second[:, :, 64:], 0.0)
    store = pltpu.make_async_copy(solved_ref, solved_hbm, sems.at[5])
    store.start()

    loads[2].wait()
    square = (128, 128)
    row, col = iota(square, 0), iota(square, 1)
    iz, ix, iy = (col >> 4) & 3, (col >> 2) & 3, col & 3
    match = (((row >> 4) & 3) == iy) & (((row >> 1) & 3) == iz)
    keep = ((row >> 1) & 3) == ix
    cells = residue.reshape(square)
    parts = []
    for number in range(2):
        gather = jnp.where(match & ((row >> 6) == number), 0.5, 0.0)
        parts.append(jnp.where(keep, dot(cells, gather), 0.0))

    wide = (32, 256)
    spread = jnp.where(iota(wide, 0) == (iota(wide, 1) >> 3), 1.0, 0.0)
    names = jnp.broadcast_to(target_ref[...].astype(F32), (8, 32))
    name = (dot(names, spread)[:1] + 0.5).astype(jnp.int32)
    names = jnp.broadcast_to(name, wide)
    row, col = iota(wide, 0), iota(wide, 1)
    own = jnp.sum(jnp.where(col == row * 8, names, 0).astype(F32), axis=1, keepdims=True)
    own = own.astype(jnp.int32)
    earlier = ((own >> 8) == (names >> 8)) & (row < (col >> 3))
    rank = jnp.sum(jnp.where(earlier, 1.0, 0.0), axis=0, keepdims=True).astype(jnp.int32)
    wide = (128, 256)
    row, col = iota(wide, 0), iota(wide, 1)
    chip = (row >> 4) + ((row >> 1) & 3) - 1
    owner = chip * 2 + (row & 1)
    wanted = ((row & 7) < 6) & (chip >= 0) & (chip < 8) & ((col >> 3) < live)
    chosen = wanted & (owner == (name >> 8))
    packed, tags = [], []
    for number in range(2):
        mine = chosen & (rank == number)
        picked = jnp.where(mine, 1.0, 0.0)
        packed.append(pick(picked[:, :128], parts[0]) + pick(picked[:, 128:], parts[1]))
        tag = jnp.where(mine & ((col & 7) == 0), (name & 255) + 1, 0).astype(F32)
        tags.append(jnp.sum(tag, axis=1, keepdims=True))
    row, col = iota(square, 0), iota(square, 1)
    place = (row & 7) * 2
    tags = jnp.where(col == place, tags[0], 0.0) + jnp.where(col == place + 1, tags[1], 0.0)
    lift = jnp.where(((row & 7) == 6) & ((row >> 3) == (col >> 3)), 1.0, 0.0)
    send_ref[...] = jnp.where(col < 64, packed[0], packed[1]) + small(lift, tags)
    loads[3].wait()
    loads[4].wait()
    own_ref[0] = grid_ref[...]
    own_ref[1] = cond_ref[...].astype(F32) * 0.5
    store.wait()


def place_kernel(pos_ref, got_ref, chip_ref, halo_ref, source_ref, pay_ref):
    first = jnp.where(pos_ref[2] == 0, 2, 0)
    square = (128, 128)
    row, col = iota(square, 0), iota(square, 1)
    slot = (row >> 4) & 1
    tags = jnp.concatenate([got_ref[pl.ds(6, 16, stride=8), :]] * 8, axis=0)
    tags = jnp.where((col & 1) == slot, tags, 0.0).astype(BF16)
    some = (16, 128)
    across = turned(jnp.where((iota(some, 1) >> 1) == iota(some, 0), 1.0, 0.0), tags)
    across = (across + 0.5).astype(jnp.int32) - 1
    wide = (128, 768)
    spread = jnp.where((iota(wide, 0) >> 1) == (iota(wide, 1) >> 7), 1.0, 0.0)
    down = (small(tags, spread) + 0.5).astype(jnp.int32) - 1
    lane = iota(wide, 1)
    right = ((down & 31) == ((lane & 127) >> 2)) & ((lane & 3) == (iota(wide, 0) >> 5))
    right = jnp.where(right, 1.0, 0.0).astype(BF16)
    mask = (col >> 4) == slot * 4 + (row >> 5)
    some = (32, 128)
    cell = (iota(some, 0) >> 3) * 4 + (iota(some, 0) & 3)
    select = jnp.where((iota(some, 1) & 15) == cell, 1.0, 0.0)
    half = iota((8, 128), 0) >> 2

    def place(owner, tiles):
        got = got_ref[pl.ds(owner, 16, stride=8), :]
        slices = jnp.where(mask, jnp.concatenate([got] * 8, axis=0), 0.0)
        high, low = split(slices)
        left = turned(select, high) + turned(select, low)
        name = jnp.broadcast_to(across[owner : owner + 1], (8, 128))
        here = {
            (x, t): ((name >> 7) == x) & (((name >> 5) & 3) == 2 * t + half)
            for x in range(2)
            for t in tiles
        }
        places = [(x, t) for x in range(8) for t in tiles]
        values = jnp.concatenate(
            [jnp.where(here[x >> 2, t], left[8 * (x & 3) : 8 * (x & 3) + 8], 0.0) for x, t in places],
            axis=0,
        )
        marks = jnp.concatenate(
            [jnp.where(here[x >> 2, t], 1.0, 0.0) for x, t in places if x % 4 == 0], axis=0
        )
        put = right[:, 128 * owner : 128 * owner + 128]
        placed = dot(values, put).reshape(8, 8 * len(tiles), 128)
        covered = small(marks, put).reshape(2, 8 * len(tiles), 128) > 0.5
        return placed, covered

    for number in range(2):
        olds = (halo_ref[0, number, 0], chip_ref[number, 0], halo_ref[1, number, 0])
        for part, (tiles, start) in enumerate((((1,), 0), ((0, 1), 8), ((0,), 24))):
            placed, covered = place(2 * part + number, tiles)
            lines = slice(start, start + 8 * len(tiles))
            old = olds[part]
            for x in range(2):
                four = slice(4 * x, 4 * x + 4)
                source_ref[number, four, lines] = jnp.where(covered[x], placed[four], old[four])
    for number in range(2):
        pay_ref[number] = source_ref[number, pl.ds(first, 6)]


def pair_matrix(size):
    shape = (size, 128)
    return jnp.where((iota(shape, 0) >> 1) == iota(shape, 1), 1.0, 0.0)


def prepare(h, inside, depth):
    mid = h[1:-1]
    lane = iota(mid.shape, 2)
    hy = after(mid, 1)
    hz = jnp.where(lane < depth - 1, after(mid, 2), 0.0)
    diagonal = 6.0 * mid + h[:-2] + h[2:] + hy + before(mid, 1) + hz
    diagonal += jnp.where(lane > 0, before(mid, 2), 0.0)
    scale = jnp.where(inside & (lane < depth), DAMPING * inverse(diagonal), 0.0)
    wx = h[:-1] + h[1:]
    wy = mid + hy
    wz = jnp.where(lane < depth - 1, mid + hz, 0.0)
    return diagonal, scale, wx, wy, wz


def neighbours(u, wx, wy, wz):
    mid = u[1:-1]
    total = wx[1:] * u[2:] + wx[:-1] * u[:-2]
    total += wy * after(mid, 1) + before(wy * mid, 1)
    return total + wz * after(mid, 2) + before(wz * mid, 2)


def within(shape, start, first_layer, first_row, sizes):
    x = iota(shape, 0) + (start[0] + first_layer)
    y = iota(shape, 1) + (start[1] + first_row)
    return (x >= 0) & (x < sizes[0]) & (y >= 0) & (y < sizes[1])


def coarser(values, matrix, scale, rows_ref):
    layers, rows, depth = values.shape
    values = values.reshape(layers // 2, 2, rows, depth)
    values = values[:, 0] + values[:, 1]
    flat = dot(values.reshape(layers // 2 * rows, depth), matrix) * scale
    count = flat.shape[0]
    rows_ref[:count] = flat
    total = rows_ref[pl.ds(0, count // 2, stride=2), :] + rows_ref[pl.ds(1, count // 2, stride=2), :]
    return total.reshape(layers // 2, rows // 2, 128)


def base_kernel(
    sizes, pos_ref, source_ref, chip_ref, halo_ref, side_ref, out_ref, pay_ref,
    s_ref, h_ref, wx_ref, wy_ref, wz_ref, diag_ref, scale_ref, first_ref, second_ref,
    res_ref, rows_ref,
):
    gx, gy, core = pos_ref[0], pos_ref[1], pos_ref[2]
    for number in range(2):
        lanes = slice(128 * number, 128 * number + 128)
        s_ref[0:6, :, lanes] = side_ref[0, number, 0:6]
        s_ref[6:14, :, lanes] = source_ref[number]
        s_ref[14:20, :, lanes] = side_ref[1, number, 0:6]
        h_ref[0:7, :, lanes] = side_ref[0, number, 6:13]
        h_ref[7:15, 0:8, lanes] = halo_ref[0, number, 1]
        h_ref[7:15, 8:24, lanes] = chip_ref[number, 1]
        h_ref[7:15, 24:32, lanes] = halo_ref[1, number, 1]
        h_ref[15:22, :, lanes] = side_ref[1, number, 6:13]
    shape = (32, 256)
    lane = iota(shape, 1)
    y = iota(shape, 0) + (gy * 16 - 8)
    rows_in = (y >= 0) & (y < sizes[1])

    def weigh(layer, _):
        h = h_ref[layer + 1]
        below, above = h_ref[layer], h_ref[layer + 2]
        hy = after(h, 0)
        hz = jnp.where(lane < 255, after(h, 1), 0.0)
        diagonal = 6.0 * h + below + above + hy + before(h, 0) + hz
        diagonal += jnp.where(lane > 0, before(h, 1), 0.0)
        x = gx * 8 + layer - 6
        inside = rows_in & (x >= 0) & (x < sizes[0])
        scale = jnp.where(inside, DAMPING * inverse(diagonal), 0.0)
        diag_ref[layer] = diagonal
        scale_ref[layer] = scale
        wx_ref[layer] = h + above
        wy_ref[layer] = h + hy
        wz_ref[layer] = jnp.where(lane < 255, h + hz, 0.0)
        first_ref[layer] = s_ref[layer] * scale
        return 0

    lax.fori_loop(0, 20, weigh, 0, unroll=True)

    def sides(ref, layer):
        u, wy, wz = ref[layer], wy_ref[layer], wz_ref[layer]
        total = wx_ref[layer] * ref[layer + 1] + wx_ref[layer - 1] * ref[layer - 1]
        total += wy * after(u, 0) + before(wy * u, 0)
        return u, total + wz * after(u, 1) + before(wz * u, 1)

    def correct(layer, _):
        u, total = sides(first_ref, layer)
        second_ref[layer] = u + scale_ref[layer] * (REST * s_ref[layer] + total)
        return 0

    lax.fori_loop(1, 19, correct, 0, unroll=True)

    def leave(layer, _):
        u, total = sides(second_ref, layer)
        res_ref[layer - 2] = s_ref[layer] - diag_ref[layer] * u + total
        return 0

    lax.fori_loop(2, 18, leave, 0, unroll=True)
    own = second_ref[6:14, 8:24, :]
    out_ref[...] = jnp.where(core == 0, own[:, :, :128], own[:, :, 128:])

    zoom = pair_matrix(256)
    source = coarser(res_ref[...], zoom, 0.5, rows_ref)
    h = coarser(h_ref[1:21], zoom, 0.125, rows_ref)
    inside = within(source.shape, (gx * 4, gy * 8), -2, -4, (sizes[0] // 2, sizes[1] // 2))
    diagonal, scale, wx, wy, wz = prepare(h, inside, 128)
    first = source * scale
    total = neighbours(first, wx[1:-1], wy[1:-1], wz[1:-1])
    second = first[1:-1] + scale[1:-1] * (REST * source[1:-1] + total)
    total = neighbours(second, wx[2:-2], wy[2:-2], wz[2:-2])
    residue = source[2:-2] - diagonal[2:-2] * second[1:-1] + total

    zoom = pair_matrix(128)
    source = coarser(residue, zoom, 0.5, rows_ref)
    h = coarser(h[1:-1], zoom, 0.125, rows_ref)
    _, scale, _, _, _ = prepare(h, jnp.full(source.shape, True), 64)
    pay_ref[0:2] = source[:, 2:6]
    pay_ref[2:4] = (source * scale)[:, 2:6]
    pay_ref[4:6] = h[1:3, 2:6]


def deep_kernel(sizes, pos_ref, mid_ref, side_ref, out_ref, win_ref, rows_ref):
    gx, gy, core = pos_ref[0], pos_ref[1], pos_ref[2]
    win_ref[...] = jnp.zeros(win_ref.shape, F32)
    for number in range(3):
        for part in range(3):
            blocks = [
                side_ref[0, 1, part], side_ref[0, 0, part], mid_ref[part],
                side_ref[1, 0, part], side_ref[1, 1, part],
            ]
            for place, block in enumerate(blocks):
                win_ref[number, 2 * place : 2 * place + 2, 4 * part : 4 * part + 4] = block[
                    2 * number : 2 * number + 2
                ]
    source, first, h = win_ref[0], win_ref[1], win_ref[2]
    shape = (8, 16, 128)
    inside = within(shape, (gx * 2, gy * 4), -3, -4, (sizes[0] // 4, sizes[1] // 4))
    inside &= iota(shape, 1) < 12
    diagonal, scale, wx, wy, wz = prepare(h, inside, 64)
    total = neighbours(first, wx, wy, wz)
    second = first[1:-1] + scale * (REST * source[1:-1] + total)
    total = neighbours(second, wx[1:-1], wy[1:-1], wz[1:-1])
    residue = source[2:-2] - diagonal[1:-1] * second[1:-1] + total

    zoom = pair_matrix(128)
    source = coarser(residue, zoom, 0.5, rows_ref)
    h = coarser(h, zoom, 0.125, rows_ref)
    inside = within(source.shape, (gx, gy * 2), -1, -2, (sizes[0] // 8, sizes[1] // 8))
    inside &= iota(source.shape, 1) < 6
    _, scale, wx, wy, wz = prepare(h, inside, 32)
    first = source * scale
    total = neighbours(first, wx[1:-1], wy[1:-1], wz[1:-1])
    second = first[1:-1] + scale[1:-1] * (REST * source[1:-1] + total)
    second = second[:, 2:4]
    out_ref[...] = jnp.where(core == 0, second[:, :, :16], second[:, :, 16:32])


def call(kernel, out_shape, in_specs, scratch=(), flops=100_000, outs=None, vmem=VMEM_BYTES):
    specs = {} if outs is None else {"out_specs": outs}
    return pl.pallas_call(
        kernel,
        out_shape=out_shape,
        scratch_shapes=list(scratch),
        compiler_params=pltpu.CompilerParams(vmem_limit_bytes=vmem),
        cost_estimate=pl.CostEstimate(flops=flops, bytes_accessed=flops, transcendentals=0),
        in_specs=in_specs,
        **specs,
    )


def split_send(values, axis, step):
    count = lax.axis_size(axis)
    pairs = []
    for place in range(count):
        if place + step < count:
            pairs.append((place * CORES, (place + step) * CORES))
        if place - step >= 0:
            pairs.append((place * CORES + 1, (place - step) * CORES + 1))
    return lax.ppermute(values, (axis, "gz"), pairs)


def shared(values):
    return lax.all_gather(values, "gz")


def per_device(fine_rhs, fine_coef, coarse_rhs, coarse_coef, patch_count, patch_target):
    core = lax.axis_index("gz")
    pos = jnp.stack([lax.axis_index("gx"), lax.axis_index("gy"), core])
    sizes = (
        lax.axis_size("gx") * coarse_rhs.shape[0],
        lax.axis_size("gy") * coarse_rhs.shape[1],
    )
    vmem = pl.BlockSpec(memory_space=pltpu.VMEM)
    smem = pl.BlockSpec(memory_space=pltpu.SMEM)
    struct = jax.ShapeDtypeStruct
    hbm = pl.BlockSpec(memory_space=pltpu.HBM)
    fine_solution, send, own = call(
        fine_kernel,
        (struct(fine_rhs.shape, F32), struct((128, 128), F32), struct((2, 8, 16, 128), F32)),
        [smem, hbm, hbm, hbm, hbm, hbm],
        [
            pltpu.VMEM((1, 32), jnp.int32),
            pltpu.VMEM(fine_rhs.shape, F32),
            pltpu.VMEM(fine_coef.shape, fine_coef.dtype),
            pltpu.VMEM(coarse_rhs.shape, F32),
            pltpu.VMEM(coarse_coef.shape, coarse_coef.dtype),
            pltpu.VMEM(fine_rhs.shape, F32),
            pltpu.SemaphoreType.DMA((6,)),
        ],
        outs=[hbm, vmem, vmem],
        vmem=MOST_VMEM,
    )(patch_count, patch_target.reshape(1, 32), fine_rhs, fine_coef, coarse_rhs, coarse_coef)
    got = lax.all_to_all(send.reshape(16, 8, 128), ("gy", "gz"), 0, 0).reshape(128, 128)
    chip = shared(own)
    halo = shared(split_send(jnp.where(core == 0, chip[:, :, :, 8:], chip[:, :, :, :8]), "gy", 1))
    conduct = jnp.concatenate([halo[0, :, 1], chip[:, 1], halo[1, :, 1]], axis=2)
    edge = split_send(jnp.where(core == 0, conduct[:, 1:], conduct[:, :7]), "gx", 1)
    source, pay = call(
        place_kernel,
        (struct((2, 8, 32, 128), F32), struct((2, 6, 32, 128), F32)),
        [smem, vmem, vmem, vmem],
        outs=[vmem] * 2,
    )(pos, got, chip, halo)
    side = shared(jnp.concatenate([split_send(pay, "gx", 1), edge], axis=1))
    grid = (32, 256)
    coarse_solution, pay = call(
        functools.partial(base_kernel, sizes),
        (struct((8, 16, 128), F32), struct((6, 4, 128), F32)),
        [smem, vmem, vmem, vmem, vmem],
        [pltpu.VMEM((20, *grid), F32), pltpu.VMEM((22, *grid), F32)]
        + [pltpu.VMEM((20, *grid), F32)] * 7
        + [pltpu.VMEM((16, *grid), F32), pltpu.VMEM((320, 128), F32)],
        flops=5_000_000,
        outs=[vmem] * 2,
    )(pos, source, chip, halo, side)
    halo = shared(split_send(pay, "gy", 1))
    mid = jnp.stack([halo[0], pay, halo[1]])
    sides = shared(jnp.stack([split_send(mid, "gx", 1), split_send(mid, "gx", 2)]))
    deep_solution = call(
        functools.partial(deep_kernel, sizes),
        struct((1, 2, 16), F32),
        [smem, vmem, vmem],
        [pltpu.VMEM((3, 10, 16, 128), F32), pltpu.VMEM((320, 128), F32)],
    )(pos, mid, sides)
    return (fine_solution, coarse_solution, deep_solution)


def solution(mesh):
    return jax.shard_map(
        per_device,
        mesh=mesh,
        in_specs=(
            P(("gx", "gy", "gz"), None, None),
            P(("gx", "gy", "gz"), None, None),
            P("gx", "gy", "gz"),
            P("gx", "gy", "gz"),
            P(("gx", "gy", "gz")),
            P(("gx", "gy", "gz")),
        ),
        out_specs=(P(("gx", "gy", "gz"), None, None), P("gx", "gy", "gz"), P("gx", "gy", "gz")),
        check_vma=False,
    )
```

```python
import functools

import jax
import jax.numpy as jnp
from jax import lax
from jax.experimental import pallas as pl
from jax.experimental.pallas import tpu as pltpu
from jax.sharding import PartitionSpec as P

DAMPING = 6.0 / 7.0
REST = 1.0 - DAMPING
F32 = jnp.float32
BF16 = jnp.bfloat16
CORES = 2
PACK = 2048.0
VMEM_BYTES = 40 * 1024 * 1024
MOST_VMEM = 60 * 1024 * 1024


def iota(shape, dim):
    return lax.broadcasted_iota(jnp.int32, shape, dim)


def split(values):
    high = values.astype(BF16)
    return high, (values - high.astype(F32)).astype(BF16)


def small(a, b):
    return jnp.dot(a.astype(BF16), b.astype(BF16), preferred_element_type=F32)


def dot(a, picks):
    high, low = split(a)
    return small(high, picks) + small(low, picks)


def pick(picks, a):
    high, low = split(a)
    return small(picks, high) + small(picks, low)


def turned(a, b):
    return lax.dot_general(
        a.astype(BF16), b, (((1,), (1,)), ((), ())), preferred_element_type=F32
    )


def after(values, axis):
    return pltpu.roll(values, values.shape[axis] - 1, axis)


def before(values, axis):
    return pltpu.roll(values, 1, axis)


def inverse(values):
    guess = pl.reciprocal(values, approx=True)
    return guess * (2.0 - values * guess)


def fine_kernel(
    count_ref, target_hbm, rhs_hbm, coef_hbm, grid_hbm, cond_hbm, solved_hbm, send_ref, away_ref, own_ref,
    target_ref, rhs_ref, coef_ref, grid_ref, cond_ref, solved_ref, sems
):
    live = count_ref[0]
    loads = [
        pltpu.make_async_copy(coef_hbm, coef_ref, sems.at[0]),
        pltpu.make_async_copy(rhs_hbm, rhs_ref, sems.at[1]),
        pltpu.make_async_copy(target_hbm, target_ref, sems.at[2]),
        pltpu.make_async_copy(grid_hbm, grid_ref, sems.at[3]),
        pltpu.make_async_copy(cond_hbm, cond_ref, sems.at[4]),
    ]
    for load in loads:
        load.start()
    half = rhs_ref.shape[0] // 2
    loads[0].wait()
    k = coef_ref[...].astype(F32) * 0.5
    h = jnp.concatenate([k[:half], k[half:]], axis=2)
    shape = h.shape
    x, lane = iota(shape, 1), iota(shape, 2)
    y, z = (lane >> 3) & 7, lane & 7

    def wrapped(values, amount):
        return pltpu.roll(values, amount % 128, 2)

    hx = jnp.where(x < 7, after(h, 1), 0.0)
    hy = jnp.where(y < 7, wrapped(h, -8), 0.0)
    hz = jnp.where(z < 7, wrapped(h, -1), 0.0)
    diagonal = 6.0 * h + hx + hy + hz
    diagonal += jnp.where(x > 0, before(h, 1), 0.0)
    diagonal += jnp.where(y > 0, wrapped(h, 8), 0.0)
    diagonal += jnp.where(z > 0, wrapped(h, 1), 0.0)
    wx = jnp.where(x < 7, h + hx, 0.0)
    wy = jnp.where(y < 7, h + hy, 0.0)
    wz = jnp.where(z < 7, h + hz, 0.0)

    def sides(u):
        total = wx * after(u, 1) + before(wx * u, 1)
        total += wy * wrapped(u, -8) + wrapped(wy * u, 8)
        return total + wz * wrapped(u, -1) + wrapped(wz * u, 1)

    scale = DAMPING * inverse(diagonal)
    loads[1].wait()
    source = jnp.concatenate([rhs_ref[:half], rhs_ref[half:]], axis=2)
    first = source * scale
    second = first + scale * (REST * source + sides(first))
    residue = source - diagonal * second + sides(second)
    slot = iota((half, 8, 64), 0)
    solved_ref[:half] = jnp.where(slot < live, second[:, :, :64], 0.0)
    solved_ref[half:] = jnp.where(slot + half < live, second[:, :, 64:], 0.0)
    store = pltpu.make_async_copy(solved_ref, solved_hbm, sems.at[5])
    store.start()

    loads[2].wait()
    square = (128, 128)
    row, col = iota(square, 0), iota(square, 1)
    iz, ix, iy = (col >> 4) & 3, (col >> 2) & 3, col & 3
    match = (((row >> 4) & 3) == iy) & (((row >> 1) & 3) == iz)
    keep = ((row >> 1) & 3) == ix
    cells = residue.reshape(square)
    parts = []
    for number in range(2):
        gather = jnp.where(match & ((row >> 6) == number), 0.5, 0.0)
        parts.append(jnp.where(keep, dot(cells, gather), 0.0))

    wide = (32, 256)
    spread = jnp.where(iota(wide, 0) == (iota(wide, 1) >> 3), 1.0, 0.0)
    names = jnp.broadcast_to(target_ref[...].astype(F32), (8, 32))
    name = (dot(names, spread)[:1] + 0.5).astype(jnp.int32)
    names = jnp.broadcast_to(name, wide)
    row, col = iota(wide, 0), iota(wide, 1)
    own = jnp.sum(jnp.where(col == row * 8, names, 0).astype(F32), axis=1, keepdims=True)
    own = own.astype(jnp.int32)
    earlier = ((own >> 8) == (names >> 8)) & (row < (col >> 3))
    rank = jnp.sum(jnp.where(earlier, 1.0, 0.0), axis=0, keepdims=True).astype(jnp.int32)
    wide = (128, 256)
    row, col = iota(wide, 0), iota(wide, 1)
    chip = (row >> 4) + ((row >> 1) & 3) - 1
    owner = chip * 2 + (row & 1)
    wanted = ((row & 7) < 6) & (chip >= 0) & (chip < 8) & ((col >> 3) < live)
    chosen = wanted & (owner == (name >> 8))
    packed, tags = [], []
    for number in range(2):
        mine = chosen & (rank == number)
        picked = jnp.where(mine, 1.0, 0.0)
        packed.append(pick(picked[:, :128], parts[0]) + pick(picked[:, 128:], parts[1]))
        tag = jnp.where(mine & ((col & 7) == 0), (name & 255) + 1, 0).astype(F32)
        tags.append(jnp.sum(tag, axis=1, keepdims=True))
    row, col = iota(square, 0), iota(square, 1)
    place = (row & 7) * 2
    tags = jnp.where(col == place, tags[0], 0.0) + jnp.where(col == place + 1, tags[1], 0.0)
    lift = jnp.where(((row & 7) == 6) & ((row >> 3) == (col >> 3)), 1.0, 0.0)
    send_ref[...] = jnp.where(col < 64, packed[0], packed[1]) + small(lift, tags)
    loads[3].wait()
    loads[4].wait()
    for ref in (away_ref, own_ref):
        ref[0] = grid_ref[...]
        ref[1] = cond_ref[...].astype(F32) * 0.5
    store.wait()


def place_kernel(pos_ref, got_ref, chip_ref, source_ref, pay_ref):
    first = jnp.where(pos_ref[2] == 0, 2, 0)
    square = (128, 128)
    row, col = iota(square, 0), iota(square, 1)
    slot = (row >> 4) & 1
    tags = jnp.concatenate([got_ref[pl.ds(6, 16, stride=8), :]] * 8, axis=0)
    tags = jnp.where((col & 1) == slot, tags, 0.0).astype(BF16)
    some = (16, 128)
    across = turned(jnp.where((iota(some, 1) >> 1) == iota(some, 0), 1.0, 0.0), tags)
    across = (across + 0.5).astype(jnp.int32) - 1
    wide = (128, 768)
    spread = jnp.where((iota(wide, 0) >> 1) == (iota(wide, 1) >> 7), 1.0, 0.0)
    down = (small(tags, spread) + 0.5).astype(jnp.int32) - 1
    lane = iota(wide, 1)
    right = ((down & 31) == ((lane & 127) >> 2)) & ((lane & 3) == (iota(wide, 0) >> 5))
    right = jnp.where(right, 1.0, 0.0).astype(BF16)
    mask = (col >> 4) == slot * 4 + (row >> 5)
    some = (32, 128)
    cell = (iota(some, 0) >> 3) * 4 + (iota(some, 0) & 3)
    select = jnp.where((iota(some, 1) & 15) == cell, 1.0, 0.0)
    half = iota((8, 128), 0) >> 2

    def place(owner, tiles):
        got = got_ref[pl.ds(owner, 16, stride=8), :]
        slices = jnp.where(mask, jnp.concatenate([got] * 8, axis=0), 0.0)
        high, low = split(slices)
        left = turned(select, high) + turned(select, low)
        name = jnp.broadcast_to(across[owner : owner + 1], (8, 128))
        here = {
            (x, t): ((name >> 7) == x) & (((name >> 5) & 3) == 2 * t + half)
            for x in range(2)
            for t in tiles
        }
        places = [(x, t) for x in range(8) for t in tiles]
        values = jnp.concatenate(
            [jnp.where(here[x >> 2, t], left[8 * (x & 3) : 8 * (x & 3) + 8], 0.0) for x, t in places],
            axis=0,
        )
        marks = jnp.concatenate(
            [jnp.where(here[x >> 2, t], 1.0, 0.0) for x, t in places if x % 4 == 0], axis=0
        )
        put = right[:, 128 * owner : 128 * owner + 128]
        placed = dot(values, put).reshape(8, 8 * len(tiles), 128)
        covered = small(marks, put).reshape(2, 8 * len(tiles), 128) > 0.5
        return placed, covered

    for number in range(2):
        for part, (tiles, start) in enumerate((((1,), 0), ((0, 1), 8), ((0,), 24))):
            placed, covered = place(2 * part + number, tiles)
            lines = slice(start, start + 8 * len(tiles))
            old = chip_ref[number, 0, :, lines]
            for x in range(2):
                four = slice(4 * x, 4 * x + 4)
                source_ref[number, four, lines] = jnp.where(covered[x], placed[four], old[four])
    for number in range(2):
        pay_ref[number] = source_ref[number, pl.ds(first, 6)]


def pair_matrix(size):
    shape = (size, 128)
    return jnp.where((iota(shape, 0) >> 1) == iota(shape, 1), 1.0, 0.0)


def prepare(h, inside, depth):
    mid = h[1:-1]
    lane = iota(mid.shape, 2)
    hy = after(mid, 1)
    hz = jnp.where(lane < depth - 1, after(mid, 2), 0.0)
    diagonal = 6.0 * mid + h[:-2] + h[2:] + hy + before(mid, 1) + hz
    diagonal += jnp.where(lane > 0, before(mid, 2), 0.0)
    scale = jnp.where(inside & (lane < depth), DAMPING * inverse(diagonal), 0.0)
    wx = h[:-1] + h[1:]
    wy = mid + hy
    wz = jnp.where(lane < depth - 1, mid + hz, 0.0)
    return diagonal, scale, wx, wy, wz


def neighbours(u, wx, wy, wz):
    mid = u[1:-1]
    total = wx[1:] * u[2:] + wx[:-1] * u[:-2]
    total += wy * after(mid, 1) + before(wy * mid, 1)
    return total + wz * after(mid, 2) + before(wz * mid, 2)


def within(shape, start, first_layer, first_row, sizes):
    x = iota(shape, 0) + (start[0] + first_layer)
    y = iota(shape, 1) + (start[1] + first_row)
    return (x >= 0) & (x < sizes[0]) & (y >= 0) & (y < sizes[1])


def coarser(values, matrix, scale, rows_ref):
    layers, rows, depth = values.shape
    values = values.reshape(layers // 2, 2, rows, depth)
    values = values[:, 0] + values[:, 1]
    flat = dot(values.reshape(layers // 2 * rows, depth), matrix) * scale
    count = flat.shape[0]
    rows_ref[:count] = flat
    total = rows_ref[pl.ds(0, count // 2, stride=2), :] + rows_ref[pl.ds(1, count // 2, stride=2), :]
    return total.reshape(layers // 2, rows // 2, 128)


def weight_kernel(
    sizes, pos_ref, chip_ref, side_ref,
    wx_ref, wy_ref, wz_ref, diag_ref, scale_ref,
    mid_wx_ref, mid_wy_ref, mid_wz_ref, mid_diag_ref, mid_scale_ref, low_scale_ref, low_h_ref,
    h_ref, rows_ref,
):
    gx, gy = pos_ref[0], pos_ref[1]
    for number in range(2):
        lanes = slice(128 * number, 128 * number + 128)
        for place, part in ((0, 0), (15, 1)):
            both = side_ref[part, number]
            upper = jnp.floor(both * (1.0 / PACK))
            h_ref[place : place + 4, :, lanes] = upper * (1.0 / 1024.0)
            h_ref[place + 3 : place + 7, :, lanes] = (both - upper * PACK) * (1.0 / 1024.0)
        h_ref[7:15, :, lanes] = chip_ref[number, 1]
    shape = (32, 256)
    lane = iota(shape, 1)
    y = iota(shape, 0) + (gy * 16 - 8)
    rows_in = (y >= 0) & (y < sizes[1])

    def weigh(layer, _):
        h = h_ref[layer + 1]
        below, above = h_ref[layer], h_ref[layer + 2]
        hy = after(h, 0)
        hz = jnp.where(lane < 255, after(h, 1), 0.0)
        diagonal = 6.0 * h + below + above + hy + before(h, 0) + hz
        diagonal += jnp.where(lane > 0, before(h, 1), 0.0)
        x = gx * 8 + layer - 6
        inside = rows_in & (x >= 0) & (x < sizes[0])
        diag_ref[layer] = diagonal
        scale_ref[layer] = jnp.where(inside, DAMPING * inverse(diagonal), 0.0)
        wx_ref[layer] = h + above
        wy_ref[layer] = h + hy
        wz_ref[layer] = jnp.where(lane < 255, h + hz, 0.0)
        return 0

    lax.fori_loop(0, 20, weigh, 0, unroll=True)
    h = coarser(h_ref[1:21], pair_matrix(256), 0.125, rows_ref)
    inside = within((8, 16, 128), (gx * 4, gy * 8), -2, -4, (sizes[0] // 2, sizes[1] // 2))
    diagonal, scale, wx, wy, wz = prepare(h, inside, 128)
    mid_wx_ref[...] = wx
    mid_wy_ref[...] = wy
    mid_wz_ref[...] = wz
    mid_diag_ref[...] = diagonal
    mid_scale_ref[...] = scale
    h = coarser(h[1:-1], pair_matrix(128), 0.125, rows_ref)
    _, scale, _, _, _ = prepare(h, jnp.full((2, 8, 128), True), 64)
    low_scale_ref[...] = scale
    low_h_ref[...] = h[1:3]


def base_kernel(
    core_ref, source_ref, side_ref,
    wx_ref, wy_ref, wz_ref, diag_ref, scale_ref,
    mid_wx_ref, mid_wy_ref, mid_wz_ref, mid_diag_ref, mid_scale_ref, low_scale_ref, low_h_ref,
    out_ref, pay_ref, s_ref, first_ref, second_ref, res_ref, rows_ref,
):
    for number in range(2):
        lanes = slice(128 * number, 128 * number + 128)
        s_ref[0:6, :, lanes] = side_ref[0, number]
        s_ref[6:14, :, lanes] = source_ref[number]
        s_ref[14:20, :, lanes] = side_ref[1, number]

    def begin(layer, _):
        first_ref[layer] = s_ref[layer] * scale_ref[layer]
        return 0

    lax.fori_loop(0, 20, begin, 0, unroll=True)

    def sides(ref, layer):
        u, wy, wz = ref[layer], wy_ref[layer], wz_ref[layer]
        total = wx_ref[layer] * ref[layer + 1] + wx_ref[layer - 1] * ref[layer - 1]
        total += wy * after(u, 0) + before(wy * u, 0)
        return u, total + wz * after(u, 1) + before(wz * u, 1)

    def correct(layer, _):
        u, total = sides(first_ref, layer)
        second_ref[layer] = u + scale_ref[layer] * (REST * s_ref[layer] + total)
        return 0

    lax.fori_loop(1, 19, correct, 0, unroll=True)

    def leave(layer, _):
        u, total = sides(second_ref, layer)
        res_ref[layer - 2] = s_ref[layer] - diag_ref[layer] * u + total
        return 0

    lax.fori_loop(2, 18, leave, 0, unroll=True)
    own = second_ref[6:14, 8:24, :]
    out_ref[...] = jnp.where(core_ref[2] == 0, own[:, :, :128], own[:, :, 128:])

    source = coarser(res_ref[...], pair_matrix(256), 0.5, rows_ref)
    scale, wx, wy, wz = mid_scale_ref[...], mid_wx_ref[...], mid_wy_ref[...], mid_wz_ref[...]
    first = source * scale
    total = neighbours(first, wx[1:-1], wy[1:-1], wz[1:-1])
    second = first[1:-1] + scale[1:-1] * (REST * source[1:-1] + total)
    total = neighbours(second, wx[2:-2], wy[2:-2], wz[2:-2])
    residue = source[2:-2] - mid_diag_ref[2:-2] * second[1:-1] + total
    source = coarser(residue, pair_matrix(128), 0.5, rows_ref)
    pay_ref[0:2] = source[:, 2:6]
    pay_ref[2:4] = (source * low_scale_ref[...])[:, 2:6]
    pay_ref[4:6] = low_h_ref[:, 2:6]


def deep_kernel(sizes, pos_ref, mid_ref, side_ref, out_ref, win_ref, rows_ref):
    gx, gy, core = pos_ref[0], pos_ref[1], pos_ref[2]
    win_ref[...] = jnp.zeros(win_ref.shape, F32)
    for number in range(3):
        for part in range(3):
            blocks = [
                side_ref[0, 1, part], side_ref[0, 0, part], mid_ref[part],
                side_ref[1, 0, part], side_ref[1, 1, part],
            ]
            for place, block in enumerate(blocks):
                win_ref[number, 2 * place : 2 * place + 2, 4 * part : 4 * part + 4] = block[
                    2 * number : 2 * number + 2
                ]
    source, first, h = win_ref[0], win_ref[1], win_ref[2]
    shape = (8, 16, 128)
    inside = within(shape, (gx * 2, gy * 4), -3, -4, (sizes[0] // 4, sizes[1] // 4))
    inside &= iota(shape, 1) < 12
    diagonal, scale, wx, wy, wz = prepare(h, inside, 64)
    total = neighbours(first, wx, wy, wz)
    second = first[1:-1] + scale * (REST * source[1:-1] + total)
    total = neighbours(second, wx[1:-1], wy[1:-1], wz[1:-1])
    residue = source[2:-2] - diagonal[1:-1] * second[1:-1] + total

    zoom = pair_matrix(128)
    source = coarser(residue, zoom, 0.5, rows_ref)
    h = coarser(h, zoom, 0.125, rows_ref)
    inside = within(source.shape, (gx, gy * 2), -1, -2, (sizes[0] // 8, sizes[1] // 8))
    inside &= iota(source.shape, 1) < 6
    _, scale, wx, wy, wz = prepare(h, inside, 32)
    first = source * scale
    total = neighbours(first, wx[1:-1], wy[1:-1], wz[1:-1])
    second = first[1:-1] + scale[1:-1] * (REST * source[1:-1] + total)
    second = second[:, 2:4]
    out_ref[...] = jnp.where(core == 0, second[:, :, :16], second[:, :, 16:32])


def call(kernel, out_shape, in_specs, scratch=(), flops=100_000, outs=None, vmem=VMEM_BYTES):
    specs = {} if outs is None else {"out_specs": outs}
    return pl.pallas_call(
        kernel,
        out_shape=out_shape,
        scratch_shapes=list(scratch),
        compiler_params=pltpu.CompilerParams(vmem_limit_bytes=vmem),
        cost_estimate=pl.CostEstimate(flops=flops, bytes_accessed=flops, transcendentals=0),
        in_specs=in_specs,
        **specs,
    )


def split_send(values, axis, step):
    count = lax.axis_size(axis)
    pairs = []
    for place in range(count):
        if place + step < count:
            pairs.append((place * CORES, (place + step) * CORES))
        if place - step >= 0:
            pairs.append((place * CORES + 1, (place - step) * CORES + 1))
    return lax.ppermute(values, (axis, "gz"), pairs)


def exchanged(up, down, axis):
    count = lax.axis_size(axis)
    pairs = [(place, place + 1) for place in range(count - 1)]
    back = [(target, source) for source, target in pairs]
    return lax.ppermute(up, axis, pairs), lax.ppermute(down, axis, back)


def shared(values):
    return lax.all_gather(values, "gz")


def per_device(fine_rhs, fine_coef, coarse_rhs, coarse_coef, patch_count, patch_target):
    core = lax.axis_index("gz")
    pos = jnp.stack([lax.axis_index("gx"), lax.axis_index("gy"), core])
    sizes = (
        lax.axis_size("gx") * coarse_rhs.shape[0],
        lax.axis_size("gy") * coarse_rhs.shape[1],
    )
    vmem = pl.BlockSpec(memory_space=pltpu.VMEM)
    smem = pl.BlockSpec(memory_space=pltpu.SMEM)
    struct = jax.ShapeDtypeStruct
    hbm = pl.BlockSpec(memory_space=pltpu.HBM)
    own_block = struct((2, *coarse_rhs.shape), F32)
    fine_solution, send, away, own = call(
        fine_kernel,
        (struct(fine_rhs.shape, F32), struct((128, 128), F32), own_block, own_block),
        [smem, hbm, hbm, hbm, hbm, hbm],
        [
            pltpu.VMEM((1, 32), jnp.int32),
            pltpu.VMEM(fine_rhs.shape, F32),
            pltpu.VMEM(fine_coef.shape, fine_coef.dtype),
            pltpu.VMEM(coarse_rhs.shape, F32),
            pltpu.VMEM(coarse_coef.shape, coarse_coef.dtype),
            pltpu.VMEM(fine_rhs.shape, F32),
            pltpu.SemaphoreType.DMA((6,)),
        ],
        outs=[hbm, vmem, vmem, vmem],
        vmem=MOST_VMEM,
    )(patch_count, patch_target.reshape(1, 32), fine_rhs, fine_coef, coarse_rhs, coarse_coef)
    got = lax.all_to_all(send.reshape(16, 8, 128), ("gy", "gz"), 0, 0).reshape(128, 128)
    below, above = exchanged(away, away, "gy")
    chip = shared(jnp.concatenate([below[:, :, 8:], own, above[:, :, :8]], axis=2))
    edge = jnp.where(core == 0, chip[:, 1, 1:], chip[:, 1, :7])
    edge = split_send(edge[:, :4] * (1024.0 * PACK) + edge[:, 3:] * 1024.0, "gx", 1)
    source, pay = call(
        place_kernel,
        (struct((2, 8, 32, 128), F32), struct((2, 6, 32, 128), F32)),
        [smem, vmem, vmem],
        outs=[vmem] * 2,
    )(pos, got, chip)
    grid = (32, 256)
    window = struct((20, *grid), F32)
    block = struct((8, 16, 128), F32)
    low = struct((2, 8, 128), F32)
    weights = call(
        functools.partial(weight_kernel, sizes),
        (window,) * 5 + (struct((9, 16, 128), F32),) + (block,) * 4 + (low,) * 2,
        [smem, vmem, vmem],
        [pltpu.VMEM((22, *grid), F32), pltpu.VMEM((320, 128), F32)],
        flops=5_000_000,
        outs=[vmem] * 12,
    )(pos, chip, shared(edge))
    moved, last = lax.optimization_barrier((split_send(pay, "gx", 1), weights[-1]))
    side = shared(moved)
    coarse_solution, pay = call(
        base_kernel,
        (block, struct((6, 4, 128), F32)),
        [smem] + [vmem] * 14,
        [pltpu.VMEM((20, *grid), F32)] * 3
        + [pltpu.VMEM((16, *grid), F32), pltpu.VMEM((320, 128), F32)],
        flops=5_000_000,
        outs=[vmem] * 2,
    )(pos, source, side, *weights[:-1], last)
    halo = shared(split_send(pay, "gy", 1))
    mid = jnp.stack([halo[0], pay, halo[1]])
    sides = shared(jnp.stack([split_send(mid, "gx", 1), split_send(mid, "gx", 2)]))
    deep_solution = call(
        functools.partial(deep_kernel, sizes),
        struct((1, 2, 16), F32),
        [smem, vmem, vmem],
        [pltpu.VMEM((3, 10, 16, 128), F32), pltpu.VMEM((320, 128), F32)],
    )(pos, mid, sides)
    return (fine_solution, coarse_solution, deep_solution)


def solution(mesh):
    return jax.shard_map(
        per_device,
        mesh=mesh,
        in_specs=(
            P(("gx", "gy", "gz"), None, None),
            P(("gx", "gy", "gz"), None, None),
            P("gx", "gy", "gz"),
            P("gx", "gy", "gz"),
            P(("gx", "gy", "gz")),
            P(("gx", "gy", "gz")),
        ),
        out_specs=(P(("gx", "gy", "gz"), None, None), P("gx", "gy", "gz"), P("gx", "gy", "gz")),
        check_vma=False,
    )
```

```python
import functools

import jax
import jax.numpy as jnp
from jax import lax
from jax.experimental import pallas as pl
from jax.experimental.pallas import tpu as pltpu
from jax.sharding import PartitionSpec as P

DAMPING = 6.0 / 7.0
REST = 1.0 - DAMPING
F32 = jnp.float32
BF16 = jnp.bfloat16
CORES = 2
PACK = 2048.0
VMEM_BYTES = 40 * 1024 * 1024
MOST_VMEM = 60 * 1024 * 1024


def iota(shape, dim):
    return lax.broadcasted_iota(jnp.int32, shape, dim)


def split(values):
    high = values.astype(BF16)
    return high, (values - high.astype(F32)).astype(BF16)


def small(a, b):
    return jnp.dot(a.astype(BF16), b.astype(BF16), preferred_element_type=F32)


def dot(a, picks):
    high, low = split(a)
    return small(high, picks) + small(low, picks)


def pick(picks, a):
    high, low = split(a)
    return small(picks, high) + small(picks, low)


def turned(a, b):
    return lax.dot_general(
        a.astype(BF16), b, (((1,), (1,)), ((), ())), preferred_element_type=F32
    )


def after(values, axis):
    return pltpu.roll(values, values.shape[axis] - 1, axis)


def before(values, axis):
    return pltpu.roll(values, 1, axis)


def inverse(values):
    guess = pl.reciprocal(values, approx=True)
    return guess * (2.0 - values * guess)


def fine_kernel(
    count_ref, target_hbm, rhs_hbm, coef_hbm, grid_hbm, cond_hbm, second_ref, send_ref, away_ref, own_ref,
    target_ref, rhs_ref, coef_ref, grid_ref, cond_ref, sems
):
    live = count_ref[0]
    loads = [
        pltpu.make_async_copy(coef_hbm, coef_ref, sems.at[0]),
        pltpu.make_async_copy(rhs_hbm, rhs_ref, sems.at[1]),
        pltpu.make_async_copy(target_hbm, target_ref, sems.at[2]),
        pltpu.make_async_copy(grid_hbm, grid_ref, sems.at[3]),
        pltpu.make_async_copy(cond_hbm, cond_ref, sems.at[4]),
    ]
    for load in loads:
        load.start()
    half = rhs_ref.shape[0] // 2
    loads[0].wait()
    k = coef_ref[...].astype(F32) * 0.5
    h = jnp.concatenate([k[:half], k[half:]], axis=2)
    shape = h.shape
    x, lane = iota(shape, 1), iota(shape, 2)
    y, z = (lane >> 3) & 7, lane & 7

    def wrapped(values, amount):
        return pltpu.roll(values, amount % 128, 2)

    hx = jnp.where(x < 7, after(h, 1), 0.0)
    hy = jnp.where(y < 7, wrapped(h, -8), 0.0)
    hz = jnp.where(z < 7, wrapped(h, -1), 0.0)
    diagonal = 6.0 * h + hx + hy + hz
    diagonal += jnp.where(x > 0, before(h, 1), 0.0)
    diagonal += jnp.where(y > 0, wrapped(h, 8), 0.0)
    diagonal += jnp.where(z > 0, wrapped(h, 1), 0.0)
    wx = jnp.where(x < 7, h + hx, 0.0)
    wy = jnp.where(y < 7, h + hy, 0.0)
    wz = jnp.where(z < 7, h + hz, 0.0)

    def sides(u):
        total = wx * after(u, 1) + before(wx * u, 1)
        total += wy * wrapped(u, -8) + wrapped(wy * u, 8)
        return total + wz * wrapped(u, -1) + wrapped(wz * u, 1)

    scale = DAMPING * inverse(diagonal)
    loads[1].wait()
    source = jnp.concatenate([rhs_ref[:half], rhs_ref[half:]], axis=2)
    first = source * scale
    second = first + scale * (REST * source + sides(first))
    residue = source - diagonal * second + sides(second)
    second_ref[...] = second

    loads[2].wait()
    square = (128, 128)
    row, col = iota(square, 0), iota(square, 1)
    iz, ix, iy = (col >> 4) & 3, (col >> 2) & 3, col & 3
    match = (((row >> 4) & 3) == iy) & (((row >> 1) & 3) == iz)
    keep = ((row >> 1) & 3) == ix
    cells = residue.reshape(square)
    parts = []
    for number in range(2):
        gather = jnp.where(match & ((row >> 6) == number), 0.5, 0.0)
        parts.append(jnp.where(keep, dot(cells, gather), 0.0))

    wide = (32, 256)
    spread = jnp.where(iota(wide, 0) == (iota(wide, 1) >> 3), 1.0, 0.0)
    names = jnp.broadcast_to(target_ref[...].astype(F32), (8, 32))
    name = (dot(names, spread)[:1] + 0.5).astype(jnp.int32)
    names = jnp.broadcast_to(name, wide)
    row, col = iota(wide, 0), iota(wide, 1)
    own = jnp.sum(jnp.where(col == row * 8, names, 0).astype(F32), axis=1, keepdims=True)
    own = own.astype(jnp.int32)
    earlier = ((own >> 8) == (names >> 8)) & (row < (col >> 3))
    rank = jnp.sum(jnp.where(earlier, 1.0, 0.0), axis=0, keepdims=True).astype(jnp.int32)
    wide = (128, 256)
    row, col = iota(wide, 0), iota(wide, 1)
    chip = (row >> 4) + ((row >> 1) & 3) - 1
    owner = chip * 2 + (row & 1)
    wanted = ((row & 7) < 6) & (chip >= 0) & (chip < 8) & ((col >> 3) < live)
    chosen = wanted & (owner == (name >> 8))
    packed, tags = [], []
    for number in range(2):
        mine = chosen & (rank == number)
        picked = jnp.where(mine, 1.0, 0.0)
        packed.append(pick(picked[:, :128], parts[0]) + pick(picked[:, 128:], parts[1]))
        tag = jnp.where(mine & ((col & 7) == 0), (name & 255) + 1, 0).astype(F32)
        tags.append(jnp.sum(tag, axis=1, keepdims=True))
    row, col = iota(square, 0), iota(square, 1)
    place = (row & 7) * 2
    tags = jnp.where(col == place, tags[0], 0.0) + jnp.where(col == place + 1, tags[1], 0.0)
    lift = jnp.where(((row & 7) == 6) & ((row >> 3) == (col >> 3)), 1.0, 0.0)
    send_ref[...] = jnp.where(col < 64, packed[0], packed[1]) + small(lift, tags)
    loads[3].wait()
    loads[4].wait()
    for ref in (away_ref, own_ref):
        ref[0] = grid_ref[...]
        ref[1] = cond_ref[...].astype(F32) * 0.5


def store_kernel(count_ref, second_ref, solved_ref):
    live = count_ref[0]
    second = second_ref[...]
    half = second.shape[0]
    slot = iota((half, 8, 64), 0)
    solved_ref[:half] = jnp.where(slot < live, second[:, :, :64], 0.0)
    solved_ref[half:] = jnp.where(slot + half < live, second[:, :, 64:], 0.0)


def place_kernel(got_ref, chip_ref, source_ref, pay_ref):
    first = jnp.where(lax.axis_index("gz") == 0, 2, 0)
    square = (128, 128)
    row, col = iota(square, 0), iota(square, 1)
    slot = (row >> 4) & 1
    tags = jnp.concatenate([got_ref[pl.ds(6, 16, stride=8), :]] * 8, axis=0)
    tags = jnp.where((col & 1) == slot, tags, 0.0).astype(BF16)
    some = (16, 128)
    across = turned(jnp.where((iota(some, 1) >> 1) == iota(some, 0), 1.0, 0.0), tags)
    across = (across + 0.5).astype(jnp.int32) - 1
    wide = (128, 768)
    spread = jnp.where((iota(wide, 0) >> 1) == (iota(wide, 1) >> 7), 1.0, 0.0)
    down = (small(tags, spread) + 0.5).astype(jnp.int32) - 1
    lane = iota(wide, 1)
    right = ((down & 31) == ((lane & 127) >> 2)) & ((lane & 3) == (iota(wide, 0) >> 5))
    right = jnp.where(right, 1.0, 0.0).astype(BF16)
    mask = (col >> 4) == slot * 4 + (row >> 5)
    some = (32, 128)
    cell = (iota(some, 0) >> 3) * 4 + (iota(some, 0) & 3)
    select = jnp.where((iota(some, 1) & 15) == cell, 1.0, 0.0)
    half = iota((8, 128), 0) >> 2

    def place(owner, tiles):
        got = got_ref[pl.ds(owner, 16, stride=8), :]
        slices = jnp.where(mask, jnp.concatenate([got] * 8, axis=0), 0.0)
        high, low = split(slices)
        left = turned(select, high) + turned(select, low)
        name = jnp.broadcast_to(across[owner : owner + 1], (8, 128))
        here = {
            (x, t): ((name >> 7) == x) & (((name >> 5) & 3) == 2 * t + half)
            for x in range(2)
            for t in tiles
        }
        places = [(x, t) for x in range(8) for t in tiles]
        values = jnp.concatenate(
            [jnp.where(here[x >> 2, t], left[8 * (x & 3) : 8 * (x & 3) + 8], 0.0) for x, t in places],
            axis=0,
        )
        marks = jnp.concatenate(
            [jnp.where(here[x >> 2, t], 1.0, 0.0) for x, t in places if x % 4 == 0], axis=0
        )
        put = right[:, 128 * owner : 128 * owner + 128]
        placed = dot(values, put).reshape(8, 8 * len(tiles), 128)
        covered = small(marks, put).reshape(2, 8 * len(tiles), 128) > 0.5
        return placed, covered

    for number in range(2):
        for part, (tiles, start) in enumerate((((1,), 0), ((0, 1), 8), ((0,), 24))):
            placed, covered = place(2 * part + number, tiles)
            lines = slice(start, start + 8 * len(tiles))
            old = chip_ref[number, 0, :, lines]
            for x in range(2):
                four = slice(4 * x, 4 * x + 4)
                source_ref[number, four, lines] = jnp.where(covered[x], placed[four], old[four])
    for number in range(2):
        pay_ref[number] = source_ref[number, pl.ds(first, 6)]


def pair_matrix(size):
    shape = (size, 128)
    return jnp.where((iota(shape, 0) >> 1) == iota(shape, 1), 1.0, 0.0)


def prepare(h, inside, depth):
    mid = h[1:-1]
    lane = iota(mid.shape, 2)
    hy = after(mid, 1)
    hz = jnp.where(lane < depth - 1, after(mid, 2), 0.0)
    diagonal = 6.0 * mid + h[:-2] + h[2:] + hy + before(mid, 1) + hz
    diagonal += jnp.where(lane > 0, before(mid, 2), 0.0)
    scale = jnp.where(inside & (lane < depth), DAMPING * inverse(diagonal), 0.0)
    wx = h[:-1] + h[1:]
    wy = mid + hy
    wz = jnp.where(lane < depth - 1, mid + hz, 0.0)
    return diagonal, scale, wx, wy, wz


def neighbours(u, wx, wy, wz):
    mid = u[1:-1]
    total = wx[1:] * u[2:] + wx[:-1] * u[:-2]
    total += wy * after(mid, 1) + before(wy * mid, 1)
    return total + wz * after(mid, 2) + before(wz * mid, 2)


def within(shape, start, first_layer, first_row, sizes):
    x = iota(shape, 0) + (start[0] + first_layer)
    y = iota(shape, 1) + (start[1] + first_row)
    return (x >= 0) & (x < sizes[0]) & (y >= 0) & (y < sizes[1])


def coarser(values, matrix, scale, rows_ref):
    layers, rows, depth = values.shape
    values = values.reshape(layers // 2, 2, rows, depth)
    values = values[:, 0] + values[:, 1]
    flat = dot(values.reshape(layers // 2 * rows, depth), matrix) * scale
    count = flat.shape[0]
    rows_ref[:count] = flat
    total = rows_ref[pl.ds(0, count // 2, stride=2), :] + rows_ref[pl.ds(1, count // 2, stride=2), :]
    return total.reshape(layers // 2, rows // 2, 128)


def weight_kernel(
    sizes, chip_ref, side_ref,
    wx_ref, wy_ref, wz_ref, diag_ref, scale_ref,
    mid_wx_ref, mid_wy_ref, mid_wz_ref, mid_diag_ref, mid_scale_ref, low_scale_ref, low_h_ref,
    h_ref, rows_ref,
):
    gx, gy = lax.axis_index("gx"), lax.axis_index("gy")
    for number in range(2):
        lanes = slice(128 * number, 128 * number + 128)
        for place, part in ((0, 0), (15, 1)):
            both = side_ref[part, number]
            upper = jnp.floor(both * (1.0 / PACK))
            h_ref[place : place + 4, :, lanes] = upper * (1.0 / 1024.0)
            h_ref[place + 3 : place + 7, :, lanes] = (both - upper * PACK) * (1.0 / 1024.0)
        h_ref[7:15, :, lanes] = chip_ref[number, 1]
    shape = (32, 256)
    lane = iota(shape, 1)
    y = iota(shape, 0) + (gy * 16 - 8)
    rows_in = (y >= 0) & (y < sizes[1])

    def weigh(layer, _):
        h = h_ref[layer + 1]
        below, above = h_ref[layer], h_ref[layer + 2]
        hy = after(h, 0)
        hz = jnp.where(lane < 255, after(h, 1), 0.0)
        diagonal = 6.0 * h + below + above + hy + before(h, 0) + hz
        diagonal += jnp.where(lane > 0, before(h, 1), 0.0)
        x = gx * 8 + layer - 6
        inside = rows_in & (x >= 0) & (x < sizes[0])
        diag_ref[layer] = diagonal
        scale_ref[layer] = jnp.where(inside, DAMPING * inverse(diagonal), 0.0)
        wx_ref[layer] = h + above
        wy_ref[layer] = h + hy
        wz_ref[layer] = jnp.where(lane < 255, h + hz, 0.0)
        return 0

    lax.fori_loop(0, 20, weigh, 0, unroll=True)
    h = coarser(h_ref[1:21], pair_matrix(256), 0.125, rows_ref)
    inside = within((8, 16, 128), (gx * 4, gy * 8), -2, -4, (sizes[0] // 2, sizes[1] // 2))
    diagonal, scale, wx, wy, wz = prepare(h, inside, 128)
    mid_wx_ref[...] = wx
    mid_wy_ref[...] = wy
    mid_wz_ref[...] = wz
    mid_diag_ref[...] = diagonal
    mid_scale_ref[...] = scale
    h = coarser(h[1:-1], pair_matrix(128), 0.125, rows_ref)
    _, scale, _, _, _ = prepare(h, jnp.full((2, 8, 128), True), 64)
    low_scale_ref[...] = scale
    low_h_ref[...] = h[1:3]


def base_kernel(
    source_ref, side_ref,
    wx_ref, wy_ref, wz_ref, diag_ref, scale_ref,
    mid_wx_ref, mid_wy_ref, mid_wz_ref, mid_diag_ref, mid_scale_ref, low_scale_ref, low_h_ref,
    out_ref, pay_ref, s_ref, first_ref, second_ref, res_ref, rows_ref,
):
    for number in range(2):
        lanes = slice(128 * number, 128 * number + 128)
        s_ref[0:6, :, lanes] = side_ref[0, number]
        s_ref[6:14, :, lanes] = source_ref[number]
        s_ref[14:20, :, lanes] = side_ref[1, number]

    def begin(layer, _):
        first_ref[layer] = s_ref[layer] * scale_ref[layer]
        return 0

    lax.fori_loop(0, 20, begin, 0, unroll=True)

    def sides(ref, layer):
        u, wy, wz = ref[layer], wy_ref[layer], wz_ref[layer]
        total = wx_ref[layer] * ref[layer + 1] + wx_ref[layer - 1] * ref[layer - 1]
        total += wy * after(u, 0) + before(wy * u, 0)
        return u, total + wz * after(u, 1) + before(wz * u, 1)

    def correct(layer, _):
        u, total = sides(first_ref, layer)
        second_ref[layer] = u + scale_ref[layer] * (REST * s_ref[layer] + total)
        return 0

    lax.fori_loop(1, 19, correct, 0, unroll=True)

    def leave(layer, _):
        u, total = sides(second_ref, layer)
        res_ref[layer - 2] = s_ref[layer] - diag_ref[layer] * u + total
        return 0

    lax.fori_loop(2, 18, leave, 0, unroll=True)
    own = second_ref[6:14, 8:24, :]
    out_ref[...] = jnp.where(lax.axis_index("gz") == 0, own[:, :, :128], own[:, :, 128:])

    source = coarser(res_ref[...], pair_matrix(256), 0.5, rows_ref)
    scale, wx, wy, wz = mid_scale_ref[...], mid_wx_ref[...], mid_wy_ref[...], mid_wz_ref[...]
    first = source * scale
    total = neighbours(first, wx[1:-1], wy[1:-1], wz[1:-1])
    second = first[1:-1] + scale[1:-1] * (REST * source[1:-1] + total)
    total = neighbours(second, wx[2:-2], wy[2:-2], wz[2:-2])
    residue = source[2:-2] - mid_diag_ref[2:-2] * second[1:-1] + total
    source = coarser(residue, pair_matrix(128), 0.5, rows_ref)
    pay_ref[0:2] = source[:, 2:6]
    pay_ref[2:4] = (source * low_scale_ref[...])[:, 2:6]
    pay_ref[4:6] = low_h_ref[:, 2:6]


def deep_kernel(sizes, mid_ref, side_ref, out_ref, win_ref, rows_ref):
    gx, gy, core = (lax.axis_index(name) for name in ("gx", "gy", "gz"))
    win_ref[...] = jnp.zeros(win_ref.shape, F32)
    for number in range(3):
        for part in range(3):
            blocks = [
                side_ref[0, 1, part], side_ref[0, 0, part], mid_ref[part],
                side_ref[1, 0, part], side_ref[1, 1, part],
            ]
            for place, block in enumerate(blocks):
                win_ref[number, 2 * place : 2 * place + 2, 4 * part : 4 * part + 4] = block[
                    2 * number : 2 * number + 2
                ]
    source, first, h = win_ref[0], win_ref[1], win_ref[2]
    shape = (8, 16, 128)
    inside = within(shape, (gx * 2, gy * 4), -3, -4, (sizes[0] // 4, sizes[1] // 4))
    inside &= iota(shape, 1) < 12
    diagonal, scale, wx, wy, wz = prepare(h, inside, 64)
    total = neighbours(first, wx, wy, wz)
    second = first[1:-1] + scale * (REST * source[1:-1] + total)
    total = neighbours(second, wx[1:-1], wy[1:-1], wz[1:-1])
    residue = source[2:-2] - diagonal[1:-1] * second[1:-1] + total

    zoom = pair_matrix(128)
    source = coarser(residue, zoom, 0.5, rows_ref)
    h = coarser(h, zoom, 0.125, rows_ref)
    inside = within(source.shape, (gx, gy * 2), -1, -2, (sizes[0] // 8, sizes[1] // 8))
    inside &= iota(source.shape, 1) < 6
    _, scale, wx, wy, wz = prepare(h, inside, 32)
    first = source * scale
    total = neighbours(first, wx[1:-1], wy[1:-1], wz[1:-1])
    second = first[1:-1] + scale[1:-1] * (REST * source[1:-1] + total)
    second = second[:, 2:4]
    out_ref[...] = jnp.where(core == 0, second[:, :, :16], second[:, :, 16:32])


def call(kernel, out_shape, in_specs, scratch=(), flops=100_000, outs=None, vmem=VMEM_BYTES):
    specs = {} if outs is None else {"out_specs": outs}
    return pl.pallas_call(
        kernel,
        out_shape=out_shape,
        scratch_shapes=list(scratch),
        compiler_params=pltpu.CompilerParams(vmem_limit_bytes=vmem),
        cost_estimate=pl.CostEstimate(flops=flops, bytes_accessed=flops, transcendentals=0),
        in_specs=in_specs,
        **specs,
    )


def split_send(values, axis, step):
    count = lax.axis_size(axis)
    pairs = []
    for place in range(count):
        if place + step < count:
            pairs.append((place * CORES, (place + step) * CORES))
        if place - step >= 0:
            pairs.append((place * CORES + 1, (place - step) * CORES + 1))
    return lax.ppermute(values, (axis, "gz"), pairs)


def exchanged(up, down, axis):
    count = lax.axis_size(axis)
    pairs = [(place, place + 1) for place in range(count - 1)]
    back = [(target, source) for source, target in pairs]
    return lax.ppermute(up, axis, pairs), lax.ppermute(down, axis, back)


def shared(values):
    return lax.all_gather(values, "gz")


def per_device(fine_rhs, fine_coef, coarse_rhs, coarse_coef, patch_count, patch_target):
    core = lax.axis_index("gz")
    sizes = (
        lax.axis_size("gx") * coarse_rhs.shape[0],
        lax.axis_size("gy") * coarse_rhs.shape[1],
    )
    vmem = pl.BlockSpec(memory_space=pltpu.VMEM)
    smem = pl.BlockSpec(memory_space=pltpu.SMEM)
    struct = jax.ShapeDtypeStruct
    hbm = pl.BlockSpec(memory_space=pltpu.HBM)
    own_block = struct((2, *coarse_rhs.shape), F32)
    second, send, away, own = call(
        fine_kernel,
        (struct((16, 8, 128), F32), struct((128, 128), F32), own_block, own_block),
        [smem, hbm, hbm, hbm, hbm, hbm],
        [
            pltpu.VMEM((1, 32), jnp.int32),
            pltpu.VMEM(fine_rhs.shape, F32),
            pltpu.VMEM(fine_coef.shape, fine_coef.dtype),
            pltpu.VMEM(coarse_rhs.shape, F32),
            pltpu.VMEM(coarse_coef.shape, coarse_coef.dtype),
            pltpu.SemaphoreType.DMA((5,)),
        ],
        outs=[vmem] * 4,
        vmem=MOST_VMEM,
    )(patch_count, patch_target.reshape(1, 32), fine_rhs, fine_coef, coarse_rhs, coarse_coef)
    fine_solution = call(store_kernel, struct(fine_rhs.shape, F32), [smem, vmem])(
        patch_count, second
    )
    got = lax.all_to_all(send.reshape(16, 8, 128), ("gy", "gz"), 0, 0).reshape(128, 128)
    below, above = exchanged(away, away, "gy")
    chip = shared(jnp.concatenate([below[:, :, 8:], own, above[:, :, :8]], axis=2))
    edge = jnp.where(core == 0, chip[:, 1, 1:], chip[:, 1, :7])
    edge = split_send(edge[:, :4] * (1024.0 * PACK) + edge[:, 3:] * 1024.0, "gx", 1)
    source, pay = call(
        place_kernel,
        (struct((2, 8, 32, 128), F32), struct((2, 6, 32, 128), F32)),
        [vmem, vmem],
        outs=[vmem] * 2,
    )(got, chip)
    grid = (32, 256)
    window = struct((20, *grid), F32)
    block = struct((8, 16, 128), F32)
    low = struct((2, 8, 128), F32)
    weights = call(
        functools.partial(weight_kernel, sizes),
        (window,) * 5 + (struct((9, 16, 128), F32),) + (block,) * 4 + (low,) * 2,
        [vmem, vmem],
        [pltpu.VMEM((22, *grid), F32), pltpu.VMEM((320, 128), F32)],
        flops=5_000_000,
        outs=[vmem] * 12,
    )(chip, shared(edge))
    moved, last = lax.optimization_barrier((split_send(pay, "gx", 1), weights[-1]))
    side = shared(moved)
    coarse_solution, pay = call(
        base_kernel,
        (block, struct((6, 4, 128), F32)),
        [vmem] * 14,
        [pltpu.VMEM((20, *grid), F32)] * 3
        + [pltpu.VMEM((16, *grid), F32), pltpu.VMEM((320, 128), F32)],
        flops=5_000_000,
        outs=[vmem] * 2,
    )(source, side, *weights[:-1], last)
    halo = shared(split_send(pay, "gy", 1))
    mid = jnp.stack([halo[0], pay, halo[1]])
    sides = shared(jnp.stack([split_send(mid, "gx", 1), split_send(mid, "gx", 2)]))
    deep_solution = call(
        functools.partial(deep_kernel, sizes),
        struct((1, 2, 16), F32),
        [vmem, vmem],
        [pltpu.VMEM((3, 10, 16, 128), F32), pltpu.VMEM((320, 128), F32)],
    )(mid, sides)
    return (fine_solution, coarse_solution, deep_solution)


def solution(mesh):
    return jax.shard_map(
        per_device,
        mesh=mesh,
        in_specs=(
            P(("gx", "gy", "gz"), None, None),
            P(("gx", "gy", "gz"), None, None),
            P("gx", "gy", "gz"),
            P("gx", "gy", "gz"),
            P(("gx", "gy", "gz")),
            P(("gx", "gy", "gz")),
        ),
        out_specs=(P(("gx", "gy", "gz"), None, None), P("gx", "gy", "gz"), P("gx", "gy", "gz")),
        check_vma=False,
    )
```

```python
import functools

import jax
import jax.numpy as jnp
from jax import lax
from jax.experimental import pallas as pl
from jax.experimental.pallas import tpu as pltpu
from jax.sharding import PartitionSpec as P

DAMPING = 6.0 / 7.0
REST = 1.0 - DAMPING
F32 = jnp.float32
BF16 = jnp.bfloat16
CORES = 2
PACK = 2048.0
VMEM_BYTES = 40 * 1024 * 1024
MOST_VMEM = 60 * 1024 * 1024


def iota(shape, dim):
    return lax.broadcasted_iota(jnp.int32, shape, dim)


def split(values):
    high = values.astype(BF16)
    return high, (values - high.astype(F32)).astype(BF16)


def small(a, b):
    return jnp.dot(a.astype(BF16), b.astype(BF16), preferred_element_type=F32)


def dot(a, picks):
    high, low = split(a)
    return small(high, picks) + small(low, picks)


def pick(picks, a):
    high, low = split(a)
    return small(picks, high) + small(picks, low)


def turned(a, b):
    return lax.dot_general(
        a.astype(BF16), b, (((1,), (1,)), ((), ())), preferred_element_type=F32
    )


def after(values, axis):
    return pltpu.roll(values, values.shape[axis] - 1, axis)


def before(values, axis):
    return pltpu.roll(values, 1, axis)


def inverse(values):
    guess = pl.reciprocal(values, approx=True)
    return guess * (2.0 - values * guess)


def fine_kernel(
    count_ref, target_hbm, rhs_hbm, coef_hbm, grid_hbm, cond_hbm, second_ref, send_ref, own_ref,
    target_ref, rhs_ref, coef_ref, grid_ref, cond_ref, sems
):
    live = count_ref[0]
    loads = [
        pltpu.make_async_copy(coef_hbm, coef_ref, sems.at[0]),
        pltpu.make_async_copy(rhs_hbm, rhs_ref, sems.at[1]),
        pltpu.make_async_copy(target_hbm, target_ref, sems.at[2]),
        pltpu.make_async_copy(grid_hbm, grid_ref, sems.at[3]),
        pltpu.make_async_copy(cond_hbm, cond_ref, sems.at[4]),
    ]
    for load in loads:
        load.start()
    half = rhs_ref.shape[0] // 2
    loads[0].wait()
    k = coef_ref[...].astype(F32) * 0.5
    h = jnp.concatenate([k[:half], k[half:]], axis=2)
    shape = h.shape
    x, lane = iota(shape, 1), iota(shape, 2)
    y, z = (lane >> 3) & 7, lane & 7

    def wrapped(values, amount):
        return pltpu.roll(values, amount % 128, 2)

    hx = jnp.where(x < 7, after(h, 1), 0.0)
    hy = jnp.where(y < 7, wrapped(h, -8), 0.0)
    hz = jnp.where(z < 7, wrapped(h, -1), 0.0)
    diagonal = 6.0 * h + hx + hy + hz
    diagonal += jnp.where(x > 0, before(h, 1), 0.0)
    diagonal += jnp.where(y > 0, wrapped(h, 8), 0.0)
    diagonal += jnp.where(z > 0, wrapped(h, 1), 0.0)
    wx = jnp.where(x < 7, h + hx, 0.0)
    wy = jnp.where(y < 7, h + hy, 0.0)
    wz = jnp.where(z < 7, h + hz, 0.0)

    def sides(u):
        total = wx * after(u, 1) + before(wx * u, 1)
        total += wy * wrapped(u, -8) + wrapped(wy * u, 8)
        return total + wz * wrapped(u, -1) + wrapped(wz * u, 1)

    scale = DAMPING * inverse(diagonal)
    loads[1].wait()
    source = jnp.concatenate([rhs_ref[:half], rhs_ref[half:]], axis=2)
    first = source * scale
    second = first + scale * (REST * source + sides(first))
    residue = source - diagonal * second + sides(second)
    second_ref[...] = second

    loads[2].wait()
    square = (128, 128)
    row, col = iota(square, 0), iota(square, 1)
    iz, ix, iy = (col >> 4) & 3, (col >> 2) & 3, col & 3
    match = (((row >> 4) & 3) == iy) & (((row >> 1) & 3) == iz)
    keep = ((row >> 1) & 3) == ix
    cells = residue.reshape(square)
    parts = []
    for number in range(2):
        gather = jnp.where(match & ((row >> 6) == number), 0.5, 0.0)
        parts.append(jnp.where(keep, dot(cells, gather), 0.0))

    wide = (32, 256)
    spread = jnp.where(iota(wide, 0) == (iota(wide, 1) >> 3), 1.0, 0.0)
    names = jnp.broadcast_to(target_ref[...].astype(F32), (8, 32))
    name = (dot(names, spread)[:1] + 0.5).astype(jnp.int32)
    names = jnp.broadcast_to(name, wide)
    row, col = iota(wide, 0), iota(wide, 1)
    own = jnp.sum(jnp.where(col == row * 8, names, 0).astype(F32), axis=1, keepdims=True)
    own = own.astype(jnp.int32)
    earlier = ((own >> 8) == (names >> 8)) & (row < (col >> 3))
    rank = jnp.sum(jnp.where(earlier, 1.0, 0.0), axis=0, keepdims=True).astype(jnp.int32)
    wide = (128, 256)
    row, col = iota(wide, 0), iota(wide, 1)
    chip = (row >> 4) + ((row >> 1) & 3) - 1
    owner = chip * 2 + (row & 1)
    wanted = ((row & 7) < 6) & (chip >= 0) & (chip < 8) & ((col >> 3) < live)
    chosen = wanted & (owner == (name >> 8))
    packed, tags = [], []
    for number in range(2):
        mine = chosen & (rank == number)
        picked = jnp.where(mine, 1.0, 0.0)
        packed.append(pick(picked[:, :128], parts[0]) + pick(picked[:, 128:], parts[1]))
        tag = jnp.where(mine & ((col & 7) == 0), (name & 255) + 1, 0).astype(F32)
        tags.append(jnp.sum(tag, axis=1, keepdims=True))
    row, col = iota(square, 0), iota(square, 1)
    place = (row & 7) * 2
    tags = jnp.where(col == place, tags[0], 0.0) + jnp.where(col == place + 1, tags[1], 0.0)
    lift = jnp.where(((row & 7) == 6) & ((row >> 3) == (col >> 3)), 1.0, 0.0)
    send_ref[...] = jnp.where(col < 64, packed[0], packed[1]) + small(lift, tags)
    loads[3].wait()
    loads[4].wait()
    own_ref[0] = grid_ref[...]
    own_ref[1] = cond_ref[...].astype(F32) * 0.5


def store_kernel(count_ref, second_ref, solved_ref):
    live = count_ref[0]
    second = second_ref[...]
    half = second.shape[0]
    slot = iota((half, 8, 64), 0)
    solved_ref[:half] = jnp.where(slot < live, second[:, :, :64], 0.0)
    solved_ref[half:] = jnp.where(slot + half < live, second[:, :, 64:], 0.0)


def place_kernel(got_ref, chip_ref, source_ref, pay_ref):
    first = jnp.where(lax.axis_index("gz") == 0, 2, 0)
    square = (128, 128)
    row, col = iota(square, 0), iota(square, 1)
    slot = (row >> 4) & 1
    tags = jnp.concatenate([got_ref[pl.ds(6, 16, stride=8), :]] * 8, axis=0)
    tags = jnp.where((col & 1) == slot, tags, 0.0).astype(BF16)
    some = (16, 128)
    across = turned(jnp.where((iota(some, 1) >> 1) == iota(some, 0), 1.0, 0.0), tags)
    across = (across + 0.5).astype(jnp.int32) - 1
    wide = (128, 768)
    spread = jnp.where((iota(wide, 0) >> 1) == (iota(wide, 1) >> 7), 1.0, 0.0)
    down = (small(tags, spread) + 0.5).astype(jnp.int32) - 1
    lane = iota(wide, 1)
    right = ((down & 31) == ((lane & 127) >> 2)) & ((lane & 3) == (iota(wide, 0) >> 5))
    right = jnp.where(right, 1.0, 0.0).astype(BF16)
    mask = (col >> 4) == slot * 4 + (row >> 5)
    some = (32, 128)
    cell = (iota(some, 0) >> 3) * 4 + (iota(some, 0) & 3)
    select = jnp.where((iota(some, 1) & 15) == cell, 1.0, 0.0)
    half = iota((8, 128), 0) >> 2

    def place(owner, tiles):
        got = got_ref[pl.ds(owner, 16, stride=8), :]
        slices = jnp.where(mask, jnp.concatenate([got] * 8, axis=0), 0.0)
        high, low = split(slices)
        left = turned(select, high) + turned(select, low)
        name = jnp.broadcast_to(across[owner : owner + 1], (8, 128))
        here = {
            (x, t): ((name >> 7) == x) & (((name >> 5) & 3) == 2 * t + half)
            for x in range(2)
            for t in tiles
        }
        places = [(x, t) for x in range(8) for t in tiles]
        values = jnp.concatenate(
            [jnp.where(here[x >> 2, t], left[8 * (x & 3) : 8 * (x & 3) + 8], 0.0) for x, t in places],
            axis=0,
        )
        marks = jnp.concatenate(
            [jnp.where(here[x >> 2, t], 1.0, 0.0) for x, t in places if x % 4 == 0], axis=0
        )
        put = right[:, 128 * owner : 128 * owner + 128]
        placed = dot(values, put).reshape(8, 8 * len(tiles), 128)
        covered = small(marks, put).reshape(2, 8 * len(tiles), 128) > 0.5
        return placed, covered

    for number in range(2):
        for part, (tiles, start) in enumerate((((1,), 0), ((0, 1), 8), ((0,), 24))):
            placed, covered = place(2 * part + number, tiles)
            lines = slice(start, start + 8 * len(tiles))
            old = chip_ref[number, 0, :, lines]
            for x in range(2):
                four = slice(4 * x, 4 * x + 4)
                source_ref[number, four, lines] = jnp.where(covered[x], placed[four], old[four])
    for number in range(2):
        pay_ref[number] = source_ref[number, pl.ds(first, 6)]


def pair_matrix(size):
    shape = (size, 128)
    return jnp.where((iota(shape, 0) >> 1) == iota(shape, 1), 1.0, 0.0)


def prepare(h, inside, depth):
    mid = h[1:-1]
    lane = iota(mid.shape, 2)
    hy = after(mid, 1)
    hz = jnp.where(lane < depth - 1, after(mid, 2), 0.0)
    diagonal = 6.0 * mid + h[:-2] + h[2:] + hy + before(mid, 1) + hz
    diagonal += jnp.where(lane > 0, before(mid, 2), 0.0)
    scale = jnp.where(inside & (lane < depth), DAMPING * inverse(diagonal), 0.0)
    wx = h[:-1] + h[1:]
    wy = mid + hy
    wz = jnp.where(lane < depth - 1, mid + hz, 0.0)
    return diagonal, scale, wx, wy, wz


def neighbours(u, wx, wy, wz):
    mid = u[1:-1]
    total = wx[1:] * u[2:] + wx[:-1] * u[:-2]
    total += wy * after(mid, 1) + before(wy * mid, 1)
    return total + wz * after(mid, 2) + before(wz * mid, 2)


def within(shape, start, first_layer, first_row, sizes):
    x = iota(shape, 0) + (start[0] + first_layer)
    y = iota(shape, 1) + (start[1] + first_row)
    return (x >= 0) & (x < sizes[0]) & (y >= 0) & (y < sizes[1])


def coarser(values, matrix, scale, rows_ref):
    layers, rows, depth = values.shape
    values = values.reshape(layers // 2, 2, rows, depth)
    values = values[:, 0] + values[:, 1]
    flat = dot(values.reshape(layers // 2 * rows, depth), matrix) * scale
    count = flat.shape[0]
    rows_ref[:count] = flat
    total = rows_ref[pl.ds(0, count // 2, stride=2), :] + rows_ref[pl.ds(1, count // 2, stride=2), :]
    return total.reshape(layers // 2, rows // 2, 128)


def weight_kernel(
    sizes, chip_ref, side_ref,
    wx_ref, wy_ref, wz_ref, diag_ref, scale_ref,
    mid_wx_ref, mid_wy_ref, mid_wz_ref, mid_diag_ref, mid_scale_ref, low_scale_ref, low_h_ref,
    h_ref, rows_ref,
):
    gx, gy = lax.axis_index("gx"), lax.axis_index("gy")
    for number in range(2):
        lanes = slice(128 * number, 128 * number + 128)
        for place, part in ((0, 0), (15, 1)):
            both = side_ref[part, number]
            upper = jnp.floor(both * (1.0 / PACK))
            h_ref[place : place + 4, :, lanes] = upper * (1.0 / 1024.0)
            h_ref[place + 3 : place + 7, :, lanes] = (both - upper * PACK) * (1.0 / 1024.0)
        h_ref[7:15, :, lanes] = chip_ref[number, 1]
    shape = (32, 256)
    lane = iota(shape, 1)
    y = iota(shape, 0) + (gy * 16 - 8)
    rows_in = (y >= 0) & (y < sizes[1])

    def weigh(layer, _):
        h = h_ref[layer + 1]
        below, above = h_ref[layer], h_ref[layer + 2]
        hy = after(h, 0)
        hz = jnp.where(lane < 255, after(h, 1), 0.0)
        diagonal = 6.0 * h + below + above + hy + before(h, 0) + hz
        diagonal += jnp.where(lane > 0, before(h, 1), 0.0)
        x = gx * 8 + layer - 6
        inside = rows_in & (x >= 0) & (x < sizes[0])
        diag_ref[layer] = diagonal
        scale_ref[layer] = jnp.where(inside, DAMPING * inverse(diagonal), 0.0)
        wx_ref[layer] = h + above
        wy_ref[layer] = h + hy
        wz_ref[layer] = jnp.where(lane < 255, h + hz, 0.0)
        return 0

    lax.fori_loop(0, 20, weigh, 0, unroll=True)
    h = coarser(h_ref[1:21], pair_matrix(256), 0.125, rows_ref)
    inside = within((8, 16, 128), (gx * 4, gy * 8), -2, -4, (sizes[0] // 2, sizes[1] // 2))
    diagonal, scale, wx, wy, wz = prepare(h, inside, 128)
    mid_wx_ref[...] = wx
    mid_wy_ref[...] = wy
    mid_wz_ref[...] = wz
    mid_diag_ref[...] = diagonal
    mid_scale_ref[...] = scale
    h = coarser(h[1:-1], pair_matrix(128), 0.125, rows_ref)
    _, scale, _, _, _ = prepare(h, jnp.full((2, 8, 128), True), 64)
    low_scale_ref[...] = scale
    low_h_ref[...] = h[1:3]


def base_kernel(
    source_ref, side_ref,
    wx_ref, wy_ref, wz_ref, diag_ref, scale_ref,
    mid_wx_ref, mid_wy_ref, mid_wz_ref, mid_diag_ref, mid_scale_ref, low_scale_ref, low_h_ref,
    out_ref, pay_ref, s_ref, first_ref, second_ref, res_ref, rows_ref,
):
    for number in range(2):
        lanes = slice(128 * number, 128 * number + 128)
        s_ref[0:6, :, lanes] = side_ref[0, number]
        s_ref[6:14, :, lanes] = source_ref[number]
        s_ref[14:20, :, lanes] = side_ref[1, number]

    def begin(layer, _):
        first_ref[layer] = s_ref[layer] * scale_ref[layer]
        return 0

    lax.fori_loop(0, 20, begin, 0, unroll=True)

    def sides(ref, layer):
        u, wy, wz = ref[layer], wy_ref[layer], wz_ref[layer]
        total = wx_ref[layer] * ref[layer + 1] + wx_ref[layer - 1] * ref[layer - 1]
        total += wy * after(u, 0) + before(wy * u, 0)
        return u, total + wz * after(u, 1) + before(wz * u, 1)

    def correct(layer, _):
        u, total = sides(first_ref, layer)
        second_ref[layer] = u + scale_ref[layer] * (REST * s_ref[layer] + total)
        return 0

    lax.fori_loop(1, 19, correct, 0, unroll=True)

    def leave(layer, _):
        u, total = sides(second_ref, layer)
        res_ref[layer - 2] = s_ref[layer] - diag_ref[layer] * u + total
        return 0

    lax.fori_loop(2, 18, leave, 0, unroll=True)
    own = second_ref[6:14, 8:24, :]
    out_ref[...] = jnp.where(lax.axis_index("gz") == 0, own[:, :, :128], own[:, :, 128:])

    source = coarser(res_ref[...], pair_matrix(256), 0.5, rows_ref)
    scale, wx, wy, wz = mid_scale_ref[...], mid_wx_ref[...], mid_wy_ref[...], mid_wz_ref[...]
    first = source * scale
    total = neighbours(first, wx[1:-1], wy[1:-1], wz[1:-1])
    second = first[1:-1] + scale[1:-1] * (REST * source[1:-1] + total)
    total = neighbours(second, wx[2:-2], wy[2:-2], wz[2:-2])
    residue = source[2:-2] - mid_diag_ref[2:-2] * second[1:-1] + total
    source = coarser(residue, pair_matrix(128), 0.5, rows_ref)
    pay_ref[0:2] = source[:, 2:6]
    pay_ref[2:4] = (source * low_scale_ref[...])[:, 2:6]
    pay_ref[4:6] = low_h_ref[:, 2:6]


def deep_kernel(sizes, mid_ref, side_ref, out_ref, win_ref, rows_ref):
    gx, gy, core = (lax.axis_index(name) for name in ("gx", "gy", "gz"))
    win_ref[...] = jnp.zeros(win_ref.shape, F32)
    for number in range(3):
        for part in range(3):
            blocks = [
                side_ref[0, 1, part], side_ref[0, 0, part], mid_ref[part],
                side_ref[1, 0, part], side_ref[1, 1, part],
            ]
            for place, block in enumerate(blocks):
                win_ref[number, 2 * place : 2 * place + 2, 4 * part : 4 * part + 4] = block[
                    2 * number : 2 * number + 2
                ]
    source, first, h = win_ref[0], win_ref[1], win_ref[2]
    shape = (8, 16, 128)
    inside = within(shape, (gx * 2, gy * 4), -3, -4, (sizes[0] // 4, sizes[1] // 4))
    inside &= iota(shape, 1) < 12
    diagonal, scale, wx, wy, wz = prepare(h, inside, 64)
    total = neighbours(first, wx, wy, wz)
    second = first[1:-1] + scale * (REST * source[1:-1] + total)
    total = neighbours(second, wx[1:-1], wy[1:-1], wz[1:-1])
    residue = source[2:-2] - diagonal[1:-1] * second[1:-1] + total

    zoom = pair_matrix(128)
    source = coarser(residue, zoom, 0.5, rows_ref)
    h = coarser(h, zoom, 0.125, rows_ref)
    inside = within(source.shape, (gx, gy * 2), -1, -2, (sizes[0] // 8, sizes[1] // 8))
    inside &= iota(source.shape, 1) < 6
    _, scale, wx, wy, wz = prepare(h, inside, 32)
    first = source * scale
    total = neighbours(first, wx[1:-1], wy[1:-1], wz[1:-1])
    second = first[1:-1] + scale[1:-1] * (REST * source[1:-1] + total)
    second = second[:, 2:4]
    out_ref[...] = jnp.where(core == 0, second[:, :, :16], second[:, :, 16:32])


def call(kernel, out_shape, in_specs, scratch=(), flops=100_000, outs=None, vmem=VMEM_BYTES):
    specs = {} if outs is None else {"out_specs": outs}
    return pl.pallas_call(
        kernel,
        out_shape=out_shape,
        scratch_shapes=list(scratch),
        compiler_params=pltpu.CompilerParams(vmem_limit_bytes=vmem),
        cost_estimate=pl.CostEstimate(flops=flops, bytes_accessed=flops, transcendentals=0),
        in_specs=in_specs,
        **specs,
    )


def split_send(values, axis, step):
    count = lax.axis_size(axis)
    pairs = []
    for place in range(count):
        if place + step < count:
            pairs.append((place * CORES, (place + step) * CORES))
        if place - step >= 0:
            pairs.append((place * CORES + 1, (place - step) * CORES + 1))
    return lax.ppermute(values, (axis, "gz"), pairs)


def shared(values):
    return lax.all_gather(values, "gz")


def per_device(fine_rhs, fine_coef, coarse_rhs, coarse_coef, patch_count, patch_target):
    core = lax.axis_index("gz")
    sizes = (
        lax.axis_size("gx") * coarse_rhs.shape[0],
        lax.axis_size("gy") * coarse_rhs.shape[1],
    )
    vmem = pl.BlockSpec(memory_space=pltpu.VMEM)
    smem = pl.BlockSpec(memory_space=pltpu.SMEM)
    struct = jax.ShapeDtypeStruct
    hbm = pl.BlockSpec(memory_space=pltpu.HBM)
    own_block = struct((2, *coarse_rhs.shape), F32)
    second, send, own = call(
        fine_kernel,
        (struct((16, 8, 128), F32), struct((128, 128), F32), own_block),
        [smem, hbm, hbm, hbm, hbm, hbm],
        [
            pltpu.VMEM((1, 32), jnp.int32),
            pltpu.VMEM(fine_rhs.shape, F32),
            pltpu.VMEM(fine_coef.shape, fine_coef.dtype),
            pltpu.VMEM(coarse_rhs.shape, F32),
            pltpu.VMEM(coarse_coef.shape, coarse_coef.dtype),
            pltpu.SemaphoreType.DMA((5,)),
        ],
        outs=[vmem] * 3,
        vmem=MOST_VMEM,
    )(patch_count, patch_target.reshape(1, 32), fine_rhs, fine_coef, coarse_rhs, coarse_coef)
    fine_solution = call(store_kernel, struct(fine_rhs.shape, F32), [smem, vmem])(
        patch_count, second
    )
    got = lax.all_to_all(send.reshape(16, 8, 128), ("gy", "gz"), 0, 0).reshape(128, 128)
    chip = shared(own)
    halo = shared(split_send(jnp.where(core == 0, chip[:, :, :, 8:], chip[:, :, :, :8]), "gy", 1))
    chip = jnp.concatenate([halo[0], chip, halo[1]], axis=3)
    edge = jnp.where(core == 0, chip[:, 1, 1:], chip[:, 1, :7])
    edge = split_send(edge[:, :4] * (1024.0 * PACK) + edge[:, 3:] * 1024.0, "gx", 1)
    source, pay = call(
        place_kernel,
        (struct((2, 8, 32, 128), F32), struct((2, 6, 32, 128), F32)),
        [vmem, vmem],
        outs=[vmem] * 2,
    )(got, chip)
    grid = (32, 256)
    window = struct((20, *grid), F32)
    block = struct((8, 16, 128), F32)
    low = struct((2, 8, 128), F32)
    weights = call(
        functools.partial(weight_kernel, sizes),
        (window,) * 5 + (struct((9, 16, 128), F32),) + (block,) * 4 + (low,) * 2,
        [vmem, vmem],
        [pltpu.VMEM((22, *grid), F32), pltpu.VMEM((320, 128), F32)],
        flops=5_000_000,
        outs=[vmem] * 12,
    )(chip, shared(edge))
    moved, last = lax.optimization_barrier((split_send(pay, "gx", 1), weights[-1]))
    side = shared(moved)
    coarse_solution, pay = call(
        base_kernel,
        (block, struct((6, 4, 128), F32)),
        [vmem] * 14,
        [pltpu.VMEM((20, *grid), F32)] * 3
        + [pltpu.VMEM((16, *grid), F32), pltpu.VMEM((320, 128), F32)],
        flops=5_000_000,
        outs=[vmem] * 2,
    )(source, side, *weights[:-1], last)
    halo = shared(split_send(pay, "gy", 1))
    mid = jnp.stack([halo[0], pay, halo[1]])
    sides = shared(jnp.stack([split_send(mid, "gx", 1), split_send(mid, "gx", 2)]))
    deep_solution = call(
        functools.partial(deep_kernel, sizes),
        struct((1, 2, 16), F32),
        [vmem, vmem],
        [pltpu.VMEM((3, 10, 16, 128), F32), pltpu.VMEM((320, 128), F32)],
    )(mid, sides)
    return (fine_solution, coarse_solution, deep_solution)


def solution(mesh):
    return jax.shard_map(
        per_device,
        mesh=mesh,
        in_specs=(
            P(("gx", "gy", "gz"), None, None),
            P(("gx", "gy", "gz"), None, None),
            P("gx", "gy", "gz"),
            P("gx", "gy", "gz"),
            P(("gx", "gy", "gz")),
            P(("gx", "gy", "gz")),
        ),
        out_specs=(P(("gx", "gy", "gz"), None, None), P("gx", "gy", "gz"), P("gx", "gy", "gz")),
        check_vma=False,
    )
```

```python
import functools

import jax
import jax.numpy as jnp
from jax import lax
from jax.experimental import pallas as pl
from jax.experimental.pallas import tpu as pltpu
from jax.sharding import PartitionSpec as P

DAMPING = 6.0 / 7.0
REST = 1.0 - DAMPING
F32 = jnp.float32
BF16 = jnp.bfloat16
CORES = 2
PACK = 2048.0
VMEM_BYTES = 40 * 1024 * 1024
MOST_VMEM = 60 * 1024 * 1024


def iota(shape, dim):
    return lax.broadcasted_iota(jnp.int32, shape, dim)


def split(values):
    high = values.astype(BF16)
    return high, (values - high.astype(F32)).astype(BF16)


def small(a, b):
    return jnp.dot(a.astype(BF16), b.astype(BF16), preferred_element_type=F32)


def dot(a, picks):
    high, low = split(a)
    return small(high, picks) + small(low, picks)


def pick(picks, a):
    high, low = split(a)
    return small(picks, high) + small(picks, low)


def turned(a, b):
    return lax.dot_general(
        a.astype(BF16), b, (((1,), (1,)), ((), ())), preferred_element_type=F32
    )


def after(values, axis):
    return pltpu.roll(values, values.shape[axis] - 1, axis)


def before(values, axis):
    return pltpu.roll(values, 1, axis)


def inverse(values):
    guess = pl.reciprocal(values, approx=True)
    return guess * (2.0 - values * guess)


def fine_kernel(
    count_ref, target_hbm, rhs_hbm, coef_hbm, grid_hbm, cond_hbm, second_ref, send_ref, own_ref,
    target_ref, rhs_ref, coef_ref, grid_ref, cond_ref, sems
):
    live = count_ref[0]
    loads = [
        pltpu.make_async_copy(coef_hbm, coef_ref, sems.at[0]),
        pltpu.make_async_copy(rhs_hbm, rhs_ref, sems.at[1]),
        pltpu.make_async_copy(target_hbm, target_ref, sems.at[2]),
        pltpu.make_async_copy(grid_hbm, grid_ref, sems.at[3]),
        pltpu.make_async_copy(cond_hbm, cond_ref, sems.at[4]),
    ]
    for load in loads:
        load.start()
    half = rhs_ref.shape[0] // 2
    loads[0].wait()
    k = coef_ref[...].astype(F32) * 0.5
    h = jnp.concatenate([k[:half], k[half:]], axis=2)
    shape = h.shape
    x, lane = iota(shape, 1), iota(shape, 2)
    y, z = (lane >> 3) & 7, lane & 7

    def wrapped(values, amount):
        return pltpu.roll(values, amount % 128, 2)

    hx = jnp.where(x < 7, after(h, 1), 0.0)
    hy = jnp.where(y < 7, wrapped(h, -8), 0.0)
    hz = jnp.where(z < 7, wrapped(h, -1), 0.0)
    diagonal = 6.0 * h + hx + hy + hz
    diagonal += jnp.where(x > 0, before(h, 1), 0.0)
    diagonal += jnp.where(y > 0, wrapped(h, 8), 0.0)
    diagonal += jnp.where(z > 0, wrapped(h, 1), 0.0)
    wx = jnp.where(x < 7, h + hx, 0.0)
    wy = jnp.where(y < 7, h + hy, 0.0)
    wz = jnp.where(z < 7, h + hz, 0.0)

    def sides(u):
        total = wx * after(u, 1) + before(wx * u, 1)
        total += wy * wrapped(u, -8) + wrapped(wy * u, 8)
        return total + wz * wrapped(u, -1) + wrapped(wz * u, 1)

    scale = DAMPING * inverse(diagonal)
    loads[1].wait()
    source = jnp.concatenate([rhs_ref[:half], rhs_ref[half:]], axis=2)
    first = source * scale
    second = first + scale * (REST * source + sides(first))
    residue = source - diagonal * second + sides(second)
    second_ref[...] = second

    loads[2].wait()
    square = (128, 128)
    row, col = iota(square, 0), iota(square, 1)
    iz, ix, iy = (col >> 4) & 3, (col >> 2) & 3, col & 3
    match = (((row >> 4) & 3) == iy) & (((row >> 1) & 3) == iz)
    keep = ((row >> 1) & 3) == ix
    cells = residue.reshape(square)
    parts = []
    for number in range(2):
        gather = jnp.where(match & ((row >> 6) == number), 0.5, 0.0)
        parts.append(jnp.where(keep, dot(cells, gather), 0.0))

    wide = (32, 256)
    spread = jnp.where(iota(wide, 0) == (iota(wide, 1) >> 3), 1.0, 0.0)
    names = jnp.broadcast_to(target_ref[...].astype(F32), (8, 32))
    name = (dot(names, spread)[:1] + 0.5).astype(jnp.int32)
    names = jnp.broadcast_to(name, wide)
    row, col = iota(wide, 0), iota(wide, 1)
    own = jnp.sum(jnp.where(col == row * 8, names, 0).astype(F32), axis=1, keepdims=True)
    own = own.astype(jnp.int32)
    earlier = ((own >> 8) == (names >> 8)) & (row < (col >> 3))
    rank = jnp.sum(jnp.where(earlier, 1.0, 0.0), axis=0, keepdims=True).astype(jnp.int32)
    wide = (128, 256)
    row, col = iota(wide, 0), iota(wide, 1)
    chip = (row >> 4) + ((row >> 1) & 3) - 1
    owner = chip * 2 + (row & 1)
    wanted = ((row & 7) < 6) & (chip >= 0) & (chip < 8) & ((col >> 3) < live)
    chosen = wanted & (owner == (name >> 8))
    packed, tags = [], []
    for number in range(2):
        mine = chosen & (rank == number)
        picked = jnp.where(mine, 1.0, 0.0)
        packed.append(pick(picked[:, :128], parts[0]) + pick(picked[:, 128:], parts[1]))
        tag = jnp.where(mine & ((col & 7) == 0), (name & 255) + 1, 0).astype(F32)
        tags.append(jnp.sum(tag, axis=1, keepdims=True))
    row, col = iota(square, 0), iota(square, 1)
    place = (row & 7) * 2
    tags = jnp.where(col == place, tags[0], 0.0) + jnp.where(col == place + 1, tags[1], 0.0)
    lift = jnp.where(((row & 7) == 6) & ((row >> 3) == (col >> 3)), 1.0, 0.0)
    send_ref[...] = jnp.where(col < 64, packed[0], packed[1]) + small(lift, tags)
    loads[3].wait()
    loads[4].wait()
    own_ref[0] = grid_ref[...]
    own_ref[1] = cond_ref[...].astype(F32) * 0.5


def store_kernel(count_ref, second_ref, solved_ref):
    live = count_ref[0]
    second = second_ref[...]
    half = second.shape[0]
    slot = iota((half, 8, 64), 0)
    solved_ref[:half] = jnp.where(slot < live, second[:, :, :64], 0.0)
    solved_ref[half:] = jnp.where(slot + half < live, second[:, :, 64:], 0.0)


def place_kernel(got_ref, chip_ref, source_ref, pay_ref):
    first = jnp.where(lax.axis_index("gz") == 0, 2, 0)
    square = (128, 128)
    row, col = iota(square, 0), iota(square, 1)
    slot = (row >> 4) & 1
    tags = jnp.concatenate([got_ref[pl.ds(6, 16, stride=8), :]] * 8, axis=0)
    tags = jnp.where((col & 1) == slot, tags, 0.0).astype(BF16)
    some = (16, 128)
    across = turned(jnp.where((iota(some, 1) >> 1) == iota(some, 0), 1.0, 0.0), tags)
    across = (across + 0.5).astype(jnp.int32) - 1
    wide = (128, 768)
    spread = jnp.where((iota(wide, 0) >> 1) == (iota(wide, 1) >> 7), 1.0, 0.0)
    down = (small(tags, spread) + 0.5).astype(jnp.int32) - 1
    lane = iota(wide, 1)
    right = ((down & 31) == ((lane & 127) >> 2)) & ((lane & 3) == (iota(wide, 0) >> 5))
    right = jnp.where(right, 1.0, 0.0).astype(BF16)
    mask = (col >> 4) == slot * 4 + (row >> 5)
    some = (32, 128)
    cell = (iota(some, 0) >> 3) * 4 + (iota(some, 0) & 3)
    select = jnp.where((iota(some, 1) & 15) == cell, 1.0, 0.0)
    half = iota((8, 128), 0) >> 2

    def place(owner, tiles):
        got = got_ref[pl.ds(owner, 16, stride=8), :]
        slices = jnp.where(mask, jnp.concatenate([got] * 8, axis=0), 0.0)
        high, low = split(slices)
        left = turned(select, high) + turned(select, low)
        name = jnp.broadcast_to(across[owner : owner + 1], (8, 128))
        here = {
            (x, t): ((name >> 7) == x) & (((name >> 5) & 3) == 2 * t + half)
            for x in range(2)
            for t in tiles
        }
        places = [(x, t) for x in range(8) for t in tiles]
        values = jnp.concatenate(
            [jnp.where(here[x >> 2, t], left[8 * (x & 3) : 8 * (x & 3) + 8], 0.0) for x, t in places],
            axis=0,
        )
        marks = jnp.concatenate(
            [jnp.where(here[x >> 2, t], 1.0, 0.0) for x, t in places if x % 4 == 0], axis=0
        )
        put = right[:, 128 * owner : 128 * owner + 128]
        placed = dot(values, put).reshape(8, 8 * len(tiles), 128)
        covered = small(marks, put).reshape(2, 8 * len(tiles), 128) > 0.5
        return placed, covered

    for number in range(2):
        for part, (tiles, start) in enumerate((((1,), 0), ((0, 1), 8), ((0,), 24))):
            placed, covered = place(2 * part + number, tiles)
            lines = slice(start, start + 8 * len(tiles))
            old = chip_ref[number, 0, :, lines]
            for x in range(2):
                four = slice(4 * x, 4 * x + 4)
                source_ref[number, four, lines] = jnp.where(covered[x], placed[four], old[four])
    for number in range(2):
        pay_ref[number] = source_ref[number, pl.ds(first, 6)]


def pair_matrix(size):
    shape = (size, 128)
    return jnp.where((iota(shape, 0) >> 1) == iota(shape, 1), 1.0, 0.0)


def prepare(h, inside, depth):
    mid = h[1:-1]
    lane = iota(mid.shape, 2)
    hy = after(mid, 1)
    hz = jnp.where(lane < depth - 1, after(mid, 2), 0.0)
    diagonal = 6.0 * mid + h[:-2] + h[2:] + hy + before(mid, 1) + hz
    diagonal += jnp.where(lane > 0, before(mid, 2), 0.0)
    scale = jnp.where(inside & (lane < depth), DAMPING * inverse(diagonal), 0.0)
    wx = h[:-1] + h[1:]
    wy = mid + hy
    wz = jnp.where(lane < depth - 1, mid + hz, 0.0)
    return diagonal, scale, wx, wy, wz


def neighbours(u, wx, wy, wz):
    mid = u[1:-1]
    total = wx[1:] * u[2:] + wx[:-1] * u[:-2]
    total += wy * after(mid, 1) + before(wy * mid, 1)
    return total + wz * after(mid, 2) + before(wz * mid, 2)


def within(shape, start, first_layer, first_row, sizes):
    x = iota(shape, 0) + (start[0] + first_layer)
    y = iota(shape, 1) + (start[1] + first_row)
    return (x >= 0) & (x < sizes[0]) & (y >= 0) & (y < sizes[1])


def coarser(values, matrix, scale, rows_ref):
    layers, rows, depth = values.shape
    values = values.reshape(layers // 2, 2, rows, depth)
    values = values[:, 0] + values[:, 1]
    flat = dot(values.reshape(layers // 2 * rows, depth), matrix) * scale
    count = flat.shape[0]
    rows_ref[:count] = flat
    total = rows_ref[pl.ds(0, count // 2, stride=2), :] + rows_ref[pl.ds(1, count // 2, stride=2), :]
    return total.reshape(layers // 2, rows // 2, 128)


def weight_kernel(
    sizes, chip_ref, side_ref,
    wx_ref, wy_ref, wz_ref, diag_ref, scale_ref,
    mid_wx_ref, mid_wy_ref, mid_wz_ref, mid_diag_ref, mid_scale_ref, low_scale_ref, low_h_ref,
    h_ref, rows_ref,
):
    gx, gy = lax.axis_index("gx"), lax.axis_index("gy")
    for number in range(2):
        lanes = slice(128 * number, 128 * number + 128)
        for place, part in ((0, 0), (15, 1)):
            both = side_ref[part, number]
            upper = jnp.floor(both * (1.0 / PACK))
            h_ref[place : place + 4, :, lanes] = upper * (1.0 / 1024.0)
            h_ref[place + 3 : place + 7, :, lanes] = (both - upper * PACK) * (1.0 / 1024.0)
        h_ref[7:15, :, lanes] = chip_ref[number, 1]
    shape = (32, 256)
    lane = iota(shape, 1)
    y = iota(shape, 0) + (gy * 16 - 8)
    rows_in = (y >= 0) & (y < sizes[1])

    def weigh(layer, _):
        h = h_ref[layer + 1]
        below, above = h_ref[layer], h_ref[layer + 2]
        hy = after(h, 0)
        hz = jnp.where(lane < 255, after(h, 1), 0.0)
        diagonal = 6.0 * h + below + above + hy + before(h, 0) + hz
        diagonal += jnp.where(lane > 0, before(h, 1), 0.0)
        x = gx * 8 + layer - 6
        inside = rows_in & (x >= 0) & (x < sizes[0])
        diag_ref[layer] = diagonal
        scale_ref[layer] = jnp.where(inside, DAMPING * inverse(diagonal), 0.0)
        wx_ref[layer] = h + above
        wy_ref[layer] = h + hy
        wz_ref[layer] = jnp.where(lane < 255, h + hz, 0.0)
        return 0

    lax.fori_loop(0, 20, weigh, 0, unroll=True)
    h = coarser(h_ref[1:21], pair_matrix(256), 0.125, rows_ref)
    inside = within((8, 16, 128), (gx * 4, gy * 8), -2, -4, (sizes[0] // 2, sizes[1] // 2))
    diagonal, scale, wx, wy, wz = prepare(h, inside, 128)
    mid_wx_ref[...] = wx
    mid_wy_ref[...] = wy
    mid_wz_ref[...] = wz
    mid_diag_ref[...] = diagonal
    mid_scale_ref[...] = scale
    h = coarser(h[1:-1], pair_matrix(128), 0.125, rows_ref)
    _, scale, _, _, _ = prepare(h, jnp.full((2, 8, 128), True), 64)
    low_scale_ref[...] = scale
    low_h_ref[...] = h[1:3]


def base_kernel(
    source_ref, side_ref,
    wx_ref, wy_ref, wz_ref, diag_ref, scale_ref,
    mid_wx_ref, mid_wy_ref, mid_wz_ref, mid_diag_ref, mid_scale_ref, low_scale_ref, low_h_ref,
    out_hbm, pay_ref, s_ref, first_ref, second_ref, res_ref, rows_ref, out_ref, sem,
):
    for number in range(2):
        lanes = slice(128 * number, 128 * number + 128)
        s_ref[0:6, :, lanes] = side_ref[0, number]
        s_ref[6:14, :, lanes] = source_ref[number]
        s_ref[14:20, :, lanes] = side_ref[1, number]

    def begin(layer, _):
        first_ref[layer] = s_ref[layer] * scale_ref[layer]
        return 0

    lax.fori_loop(0, 20, begin, 0, unroll=True)

    def sides(ref, layer):
        u, wy, wz = ref[layer], wy_ref[layer], wz_ref[layer]
        total = wx_ref[layer] * ref[layer + 1] + wx_ref[layer - 1] * ref[layer - 1]
        total += wy * after(u, 0) + before(wy * u, 0)
        return u, total + wz * after(u, 1) + before(wz * u, 1)

    def correct(layer, _):
        u, total = sides(first_ref, layer)
        second_ref[layer] = u + scale_ref[layer] * (REST * s_ref[layer] + total)
        return 0

    lax.fori_loop(1, 19, correct, 0, unroll=True)

    own = second_ref[6:14, 8:24, :]
    out_ref[...] = jnp.where(lax.axis_index("gz") == 0, own[:, :, :128], own[:, :, 128:])
    store = pltpu.make_async_copy(out_ref, out_hbm, sem)
    store.start()

    def leave(layer, _):
        u, total = sides(second_ref, layer)
        res_ref[layer - 2] = s_ref[layer] - diag_ref[layer] * u + total
        return 0

    lax.fori_loop(2, 18, leave, 0, unroll=True)
    source = coarser(res_ref[...], pair_matrix(256), 0.5, rows_ref)
    scale, wx, wy, wz = mid_scale_ref[...], mid_wx_ref[...], mid_wy_ref[...], mid_wz_ref[...]
    first = source * scale
    total = neighbours(first, wx[1:-1], wy[1:-1], wz[1:-1])
    second = first[1:-1] + scale[1:-1] * (REST * source[1:-1] + total)
    total = neighbours(second, wx[2:-2], wy[2:-2], wz[2:-2])
    residue = source[2:-2] - mid_diag_ref[2:-2] * second[1:-1] + total
    source = coarser(residue, pair_matrix(128), 0.5, rows_ref)
    pay_ref[0:2] = source[:, 2:6]
    pay_ref[2:4] = (source * low_scale_ref[...])[:, 2:6]
    pay_ref[4:6] = low_h_ref[:, 2:6]
    store.wait()


def deep_kernel(sizes, mid_ref, side_ref, out_ref, win_ref, rows_ref):
    gx, gy, core = (lax.axis_index(name) for name in ("gx", "gy", "gz"))
    win_ref[...] = jnp.zeros(win_ref.shape, F32)
    for number in range(3):
        for part in range(3):
            blocks = [
                side_ref[0, 1, part], side_ref[0, 0, part], mid_ref[part],
                side_ref[1, 0, part], side_ref[1, 1, part],
            ]
            for place, block in enumerate(blocks):
                win_ref[number, 2 * place : 2 * place + 2, 4 * part : 4 * part + 4] = block[
                    2 * number : 2 * number + 2
                ]
    source, first, h = win_ref[0], win_ref[1], win_ref[2]
    shape = (8, 16, 128)
    inside = within(shape, (gx * 2, gy * 4), -3, -4, (sizes[0] // 4, sizes[1] // 4))
    inside &= iota(shape, 1) < 12
    diagonal, scale, wx, wy, wz = prepare(h, inside, 64)
    total = neighbours(first, wx, wy, wz)
    second = first[1:-1] + scale * (REST * source[1:-1] + total)
    total = neighbours(second, wx[1:-1], wy[1:-1], wz[1:-1])
    residue = source[2:-2] - diagonal[1:-1] * second[1:-1] + total

    zoom = pair_matrix(128)
    source = coarser(residue, zoom, 0.5, rows_ref)
    h = coarser(h, zoom, 0.125, rows_ref)
    inside = within(source.shape, (gx, gy * 2), -1, -2, (sizes[0] // 8, sizes[1] // 8))
    inside &= iota(source.shape, 1) < 6
    _, scale, wx, wy, wz = prepare(h, inside, 32)
    first = source * scale
    total = neighbours(first, wx[1:-1], wy[1:-1], wz[1:-1])
    second = first[1:-1] + scale[1:-1] * (REST * source[1:-1] + total)
    second = second[:, 2:4]
    out_ref[...] = jnp.where(core == 0, second[:, :, :16], second[:, :, 16:32])


def call(kernel, out_shape, in_specs, scratch=(), flops=100_000, outs=None, vmem=VMEM_BYTES):
    specs = {} if outs is None else {"out_specs": outs}
    return pl.pallas_call(
        kernel,
        out_shape=out_shape,
        scratch_shapes=list(scratch),
        compiler_params=pltpu.CompilerParams(vmem_limit_bytes=vmem),
        cost_estimate=pl.CostEstimate(flops=flops, bytes_accessed=flops, transcendentals=0),
        in_specs=in_specs,
        **specs,
    )


def split_send(values, axis, step):
    count = lax.axis_size(axis)
    pairs = []
    for place in range(count):
        if place + step < count:
            pairs.append((place * CORES, (place + step) * CORES))
        if place - step >= 0:
            pairs.append((place * CORES + 1, (place - step) * CORES + 1))
    return lax.ppermute(values, (axis, "gz"), pairs)


def shared(values):
    return lax.all_gather(values, "gz")


def per_device(fine_rhs, fine_coef, coarse_rhs, coarse_coef, patch_count, patch_target):
    core = lax.axis_index("gz")
    sizes = (
        lax.axis_size("gx") * coarse_rhs.shape[0],
        lax.axis_size("gy") * coarse_rhs.shape[1],
    )
    vmem = pl.BlockSpec(memory_space=pltpu.VMEM)
    smem = pl.BlockSpec(memory_space=pltpu.SMEM)
    struct = jax.ShapeDtypeStruct
    hbm = pl.BlockSpec(memory_space=pltpu.HBM)
    own_block = struct((2, *coarse_rhs.shape), F32)
    second, send, own = call(
        fine_kernel,
        (struct((16, 8, 128), F32), struct((128, 128), F32), own_block),
        [smem, hbm, hbm, hbm, hbm, hbm],
        [
            pltpu.VMEM((1, 32), jnp.int32),
            pltpu.VMEM(fine_rhs.shape, F32),
            pltpu.VMEM(fine_coef.shape, fine_coef.dtype),
            pltpu.VMEM(coarse_rhs.shape, F32),
            pltpu.VMEM(coarse_coef.shape, coarse_coef.dtype),
            pltpu.SemaphoreType.DMA((5,)),
        ],
        outs=[vmem] * 3,
        vmem=MOST_VMEM,
    )(patch_count, patch_target.reshape(1, 32), fine_rhs, fine_coef, coarse_rhs, coarse_coef)
    fine_solution = call(store_kernel, struct(fine_rhs.shape, F32), [smem, vmem])(
        patch_count, second
    )
    got = lax.all_to_all(send.reshape(16, 8, 128), ("gy", "gz"), 0, 0).reshape(128, 128)
    chip = shared(own)
    halo = shared(split_send(jnp.where(core == 0, chip[:, :, :, 8:], chip[:, :, :, :8]), "gy", 1))
    chip = jnp.concatenate([halo[0], chip, halo[1]], axis=3)
    edge = jnp.where(core == 0, chip[:, 1, 1:], chip[:, 1, :7])
    edge = split_send(edge[:, :4] * (1024.0 * PACK) + edge[:, 3:] * 1024.0, "gx", 1)
    source, pay = call(
        place_kernel,
        (struct((2, 8, 32, 128), F32), struct((2, 6, 32, 128), F32)),
        [vmem, vmem],
        outs=[vmem] * 2,
    )(got, chip)
    grid = (32, 256)
    window = struct((20, *grid), F32)
    block = struct((8, 16, 128), F32)
    low = struct((2, 8, 128), F32)
    weights = call(
        functools.partial(weight_kernel, sizes),
        (window,) * 5 + (struct((9, 16, 128), F32),) + (block,) * 4 + (low,) * 2,
        [vmem, vmem],
        [pltpu.VMEM((22, *grid), F32), pltpu.VMEM((320, 128), F32)],
        flops=5_000_000,
        outs=[vmem] * 12,
    )(chip, shared(edge))
    moved, last = lax.optimization_barrier((split_send(pay, "gx", 1), weights[-1]))
    side = shared(moved)
    coarse_solution, pay = call(
        base_kernel,
        (block, struct((6, 4, 128), F32)),
        [vmem] * 14,
        [pltpu.VMEM((20, *grid), F32)] * 3
        + [pltpu.VMEM((16, *grid), F32), pltpu.VMEM((320, 128), F32)]
        + [pltpu.VMEM((8, 16, 128), F32), pltpu.SemaphoreType.DMA],
        flops=5_000_000,
        outs=[hbm, vmem],
    )(source, side, *weights[:-1], last)
    halo = shared(split_send(pay, "gy", 1))
    mid = jnp.stack([halo[0], pay, halo[1]])
    sides = shared(jnp.stack([split_send(mid, "gx", 1), split_send(mid, "gx", 2)]))
    deep_solution = call(
        functools.partial(deep_kernel, sizes),
        struct((1, 2, 16), F32),
        [vmem, vmem],
        [pltpu.VMEM((3, 10, 16, 128), F32), pltpu.VMEM((320, 128), F32)],
    )(mid, sides)
    return (fine_solution, coarse_solution, deep_solution)


def solution(mesh):
    return jax.shard_map(
        per_device,
        mesh=mesh,
        in_specs=(
            P(("gx", "gy", "gz"), None, None),
            P(("gx", "gy", "gz"), None, None),
            P("gx", "gy", "gz"),
            P("gx", "gy", "gz"),
            P(("gx", "gy", "gz")),
            P(("gx", "gy", "gz")),
        ),
        out_specs=(P(("gx", "gy", "gz"), None, None), P("gx", "gy", "gz"), P("gx", "gy", "gz")),
        check_vma=False,
    )
```

```python
import functools

import jax
import jax.numpy as jnp
from jax import lax
from jax.experimental import pallas as pl
from jax.experimental.pallas import tpu as pltpu
from jax.sharding import PartitionSpec as P

DAMPING = 6.0 / 7.0
REST = 1.0 - DAMPING
F32 = jnp.float32
BF16 = jnp.bfloat16
CORES = 2
PACK = 2048.0
VMEM_BYTES = 40 * 1024 * 1024
MOST_VMEM = 60 * 1024 * 1024


def iota(shape, dim):
    return lax.broadcasted_iota(jnp.int32, shape, dim)


def split(values):
    high = values.astype(BF16)
    return high, (values - high.astype(F32)).astype(BF16)


def small(a, b):
    return jnp.dot(a.astype(BF16), b.astype(BF16), preferred_element_type=F32)


def dot(a, picks):
    high, low = split(a)
    return small(high, picks) + small(low, picks)


def pick(picks, a):
    high, low = split(a)
    return small(picks, high) + small(picks, low)


def turned(a, b):
    return lax.dot_general(
        a.astype(BF16), b, (((1,), (1,)), ((), ())), preferred_element_type=F32
    )


def after(values, axis):
    return pltpu.roll(values, values.shape[axis] - 1, axis)


def before(values, axis):
    return pltpu.roll(values, 1, axis)


def inverse(values):
    guess = pl.reciprocal(values, approx=True)
    return guess * (2.0 - values * guess)


def fine_kernel(
    count_ref, target_hbm, rhs_hbm, coef_hbm, grid_hbm, cond_hbm, second_ref, send_ref, own_ref,
    target_ref, rhs_ref, coef_ref, grid_ref, cond_ref, sems
):
    live = count_ref[0]
    loads = [
        pltpu.make_async_copy(coef_hbm, coef_ref, sems.at[0]),
        pltpu.make_async_copy(rhs_hbm, rhs_ref, sems.at[1]),
        pltpu.make_async_copy(target_hbm, target_ref, sems.at[2]),
        pltpu.make_async_copy(grid_hbm, grid_ref, sems.at[3]),
        pltpu.make_async_copy(cond_hbm, cond_ref, sems.at[4]),
    ]
    for load in loads:
        load.start()
    half = rhs_ref.shape[0] // 2
    loads[0].wait()
    k = coef_ref[...].astype(F32) * 0.5
    h = jnp.concatenate([k[:half], k[half:]], axis=2)
    shape = h.shape
    x, lane = iota(shape, 1), iota(shape, 2)
    y, z = (lane >> 3) & 7, lane & 7

    def wrapped(values, amount):
        return pltpu.roll(values, amount % 128, 2)

    hx = jnp.where(x < 7, after(h, 1), 0.0)
    hy = jnp.where(y < 7, wrapped(h, -8), 0.0)
    hz = jnp.where(z < 7, wrapped(h, -1), 0.0)
    diagonal = 6.0 * h + hx + hy + hz
    diagonal += jnp.where(x > 0, before(h, 1), 0.0)
    diagonal += jnp.where(y > 0, wrapped(h, 8), 0.0)
    diagonal += jnp.where(z > 0, wrapped(h, 1), 0.0)
    wx = jnp.where(x < 7, h + hx, 0.0)
    wy = jnp.where(y < 7, h + hy, 0.0)
    wz = jnp.where(z < 7, h + hz, 0.0)

    def sides(u):
        total = wx * after(u, 1) + before(wx * u, 1)
        total += wy * wrapped(u, -8) + wrapped(wy * u, 8)
        return total + wz * wrapped(u, -1) + wrapped(wz * u, 1)

    scale = DAMPING * inverse(diagonal)
    loads[1].wait()
    source = jnp.concatenate([rhs_ref[:half], rhs_ref[half:]], axis=2)
    first = source * scale
    second = first + scale * (REST * source + sides(first))
    residue = source - diagonal * second + sides(second)
    second_ref[...] = second

    loads[2].wait()
    square = (128, 128)
    row, col = iota(square, 0), iota(square, 1)
    iz, ix, iy = (col >> 4) & 3, (col >> 2) & 3, col & 3
    match = (((row >> 4) & 3) == iy) & (((row >> 1) & 3) == iz)
    keep = ((row >> 1) & 3) == ix
    cells = residue.reshape(square)
    parts = []
    for number in range(2):
        gather = jnp.where(match & ((row >> 6) == number), 0.5, 0.0)
        parts.append(jnp.where(keep, dot(cells, gather), 0.0))

    wide = (32, 256)
    spread = jnp.where(iota(wide, 0) == (iota(wide, 1) >> 3), 1.0, 0.0)
    names = jnp.broadcast_to(target_ref[...].astype(F32), (8, 32))
    name = (dot(names, spread)[:1] + 0.5).astype(jnp.int32)
    names = jnp.broadcast_to(name, wide)
    row, col = iota(wide, 0), iota(wide, 1)
    own = jnp.sum(jnp.where(col == row * 8, names, 0).astype(F32), axis=1, keepdims=True)
    own = own.astype(jnp.int32)
    earlier = ((own >> 8) == (names >> 8)) & (row < (col >> 3))
    rank = jnp.sum(jnp.where(earlier, 1.0, 0.0), axis=0, keepdims=True).astype(jnp.int32)
    wide = (128, 256)
    row, col = iota(wide, 0), iota(wide, 1)
    chip = (row >> 4) + ((row >> 1) & 3) - 1
    owner = chip * 2 + (row & 1)
    wanted = ((row & 7) < 6) & (chip >= 0) & (chip < 8) & ((col >> 3) < live)
    chosen = wanted & (owner == (name >> 8))
    packed, tags = [], []
    for number in range(2):
        mine = chosen & (rank == number)
        picked = jnp.where(mine, 1.0, 0.0)
        packed.append(pick(picked[:, :128], parts[0]) + pick(picked[:, 128:], parts[1]))
        tag = jnp.where(mine & ((col & 7) == 0), (name & 255) + 1, 0).astype(F32)
        tags.append(jnp.sum(tag, axis=1, keepdims=True))
    row, col = iota(square, 0), iota(square, 1)
    place = (row & 7) * 2
    tags = jnp.where(col == place, tags[0], 0.0) + jnp.where(col == place + 1, tags[1], 0.0)
    lift = jnp.where(((row & 7) == 6) & ((row >> 3) == (col >> 3)), 1.0, 0.0)
    send_ref[...] = jnp.where(col < 64, packed[0], packed[1]) + small(lift, tags)
    loads[3].wait()
    loads[4].wait()
    own_ref[0] = grid_ref[...]
    own_ref[1] = cond_ref[...].astype(F32) * 0.5


def store_kernel(count_ref, second_ref, solved_ref):
    live = count_ref[0]
    second = second_ref[...]
    half = second.shape[0]
    slot = iota((half, 8, 64), 0)
    solved_ref[:half] = jnp.where(slot < live, second[:, :, :64], 0.0)
    solved_ref[half:] = jnp.where(slot + half < live, second[:, :, 64:], 0.0)


def place_kernel(got_ref, chip_ref, source_ref, pay_ref):
    first = jnp.where(lax.axis_index("gz") == 0, 2, 0)
    square = (128, 128)
    row, col = iota(square, 0), iota(square, 1)
    slot = (row >> 4) & 1
    tags = jnp.concatenate([got_ref[pl.ds(6, 16, stride=8), :]] * 8, axis=0)
    tags = jnp.where((col & 1) == slot, tags, 0.0).astype(BF16)
    some = (16, 128)
    across = turned(jnp.where((iota(some, 1) >> 1) == iota(some, 0), 1.0, 0.0), tags)
    across = (across + 0.5).astype(jnp.int32) - 1
    wide = (128, 768)
    spread = jnp.where((iota(wide, 0) >> 1) == (iota(wide, 1) >> 7), 1.0, 0.0)
    down = (small(tags, spread) + 0.5).astype(jnp.int32) - 1
    lane = iota(wide, 1)
    right = ((down & 31) == ((lane & 127) >> 2)) & ((lane & 3) == (iota(wide, 0) >> 5))
    right = jnp.where(right, 1.0, 0.0).astype(BF16)
    mask = (col >> 4) == slot * 4 + (row >> 5)
    some = (32, 128)
    cell = (iota(some, 0) >> 3) * 4 + (iota(some, 0) & 3)
    select = jnp.where((iota(some, 1) & 15) == cell, 1.0, 0.0)
    half = iota((8, 128), 0) >> 2

    def place(owner, tiles):
        got = got_ref[pl.ds(owner, 16, stride=8), :]
        slices = jnp.where(mask, jnp.concatenate([got] * 8, axis=0), 0.0)
        high, low = split(slices)
        left = turned(select, high) + turned(select, low)
        name = jnp.broadcast_to(across[owner : owner + 1], (8, 128))
        here = {
            (x, t): ((name >> 7) == x) & (((name >> 5) & 3) == 2 * t + half)
            for x in range(2)
            for t in tiles
        }
        places = [(x, t) for x in range(8) for t in tiles]
        values = jnp.concatenate(
            [jnp.where(here[x >> 2, t], left[8 * (x & 3) : 8 * (x & 3) + 8], 0.0) for x, t in places],
            axis=0,
        )
        marks = jnp.concatenate(
            [jnp.where(here[x >> 2, t], 1.0, 0.0) for x, t in places if x % 4 == 0], axis=0
        )
        put = right[:, 128 * owner : 128 * owner + 128]
        placed = dot(values, put).reshape(8, 8 * len(tiles), 128)
        covered = small(marks, put).reshape(2, 8 * len(tiles), 128) > 0.5
        return placed, covered

    for number in range(2):
        for part, (tiles, start) in enumerate((((1,), 0), ((0, 1), 8), ((0,), 24))):
            placed, covered = place(2 * part + number, tiles)
            lines = slice(start, start + 8 * len(tiles))
            old = chip_ref[number, 0, :, lines]
            for x in range(2):
                four = slice(4 * x, 4 * x + 4)
                source_ref[number, four, lines] = jnp.where(covered[x], placed[four], old[four])
    for number in range(2):
        pay_ref[number] = source_ref[number, pl.ds(first, 6)]


def pair_matrix(size):
    shape = (size, 128)
    return jnp.where((iota(shape, 0) >> 1) == iota(shape, 1), 1.0, 0.0)


def prepare(h, inside, depth):
    mid = h[1:-1]
    lane = iota(mid.shape, 2)
    hy = after(mid, 1)
    hz = jnp.where(lane < depth - 1, after(mid, 2), 0.0)
    diagonal = 6.0 * mid + h[:-2] + h[2:] + hy + before(mid, 1) + hz
    diagonal += jnp.where(lane > 0, before(mid, 2), 0.0)
    scale = jnp.where(inside & (lane < depth), DAMPING * inverse(diagonal), 0.0)
    wx = h[:-1] + h[1:]
    wy = mid + hy
    wz = jnp.where(lane < depth - 1, mid + hz, 0.0)
    return diagonal, scale, wx, wy, wz


def neighbours(u, wx, wy, wz):
    mid = u[1:-1]
    total = wx[1:] * u[2:] + wx[:-1] * u[:-2]
    total += wy * after(mid, 1) + before(wy * mid, 1)
    return total + wz * after(mid, 2) + before(wz * mid, 2)


def within(shape, start, first_layer, first_row, sizes):
    x = iota(shape, 0) + (start[0] + first_layer)
    y = iota(shape, 1) + (start[1] + first_row)
    return (x >= 0) & (x < sizes[0]) & (y >= 0) & (y < sizes[1])


def coarser(values, matrix, scale, rows_ref):
    layers, rows, depth = values.shape
    values = values.reshape(layers // 2, 2, rows, depth)
    values = values[:, 0] + values[:, 1]
    flat = dot(values.reshape(layers // 2 * rows, depth), matrix) * scale
    count = flat.shape[0]
    rows_ref[:count] = flat
    total = rows_ref[pl.ds(0, count // 2, stride=2), :] + rows_ref[pl.ds(1, count // 2, stride=2), :]
    return total.reshape(layers // 2, rows // 2, 128)


def weight_kernel(
    sizes, chip_ref, side_ref,
    wx_ref, wy_ref, wz_ref, diag_ref, scale_ref,
    mid_wx_ref, mid_wy_ref, mid_wz_ref, mid_diag_ref, mid_scale_ref, low_scale_ref, low_h_ref,
    h_ref, rows_ref,
):
    gx, gy = lax.axis_index("gx"), lax.axis_index("gy")
    for number in range(2):
        lanes = slice(128 * number, 128 * number + 128)
        for place, part in ((0, 0), (15, 1)):
            both = side_ref[part, number]
            upper = jnp.floor(both * (1.0 / PACK))
            h_ref[place : place + 4, :, lanes] = upper * (1.0 / 1024.0)
            h_ref[place + 3 : place + 7, :, lanes] = (both - upper * PACK) * (1.0 / 1024.0)
        h_ref[7:15, :, lanes] = chip_ref[number, 1]
    shape = (32, 256)
    lane = iota(shape, 1)
    y = iota(shape, 0) + (gy * 16 - 8)
    rows_in = (y >= 0) & (y < sizes[1])

    def weigh(layer, _):
        h = h_ref[layer + 1]
        below, above = h_ref[layer], h_ref[layer + 2]
        hy = after(h, 0)
        hz = jnp.where(lane < 255, after(h, 1), 0.0)
        diagonal = 6.0 * h + below + above + hy + before(h, 0) + hz
        diagonal += jnp.where(lane > 0, before(h, 1), 0.0)
        x = gx * 8 + layer - 6
        inside = rows_in & (x >= 0) & (x < sizes[0])
        diag_ref[layer] = diagonal
        scale_ref[layer] = jnp.where(inside, DAMPING * inverse(diagonal), 0.0)
        wx_ref[layer] = h + above
        wy_ref[layer] = h + hy
        wz_ref[layer] = jnp.where(lane < 255, h + hz, 0.0)
        return 0

    lax.fori_loop(0, 20, weigh, 0, unroll=True)
    h = coarser(h_ref[1:21], pair_matrix(256), 0.125, rows_ref)
    inside = within((8, 16, 128), (gx * 4, gy * 8), -2, -4, (sizes[0] // 2, sizes[1] // 2))
    diagonal, scale, wx, wy, wz = prepare(h, inside, 128)
    mid_wx_ref[...] = wx
    mid_wy_ref[...] = wy
    mid_wz_ref[...] = wz
    mid_diag_ref[...] = diagonal
    mid_scale_ref[...] = scale
    h = coarser(h[1:-1], pair_matrix(128), 0.125, rows_ref)
    _, scale, _, _, _ = prepare(h, jnp.full((2, 8, 128), True), 64)
    low_scale_ref[...] = scale
    low_h_ref[...] = h[1:3]


def base_kernel(
    source_ref, side_ref,
    wx_ref, wy_ref, wz_ref, diag_ref, scale_ref,
    mid_wx_ref, mid_wy_ref, mid_wz_ref, mid_diag_ref, mid_scale_ref, low_scale_ref, low_h_ref,
    out_ref, pay_ref, s_ref, first_ref, second_ref, res_ref, rows_ref,
):
    for number in range(2):
        lanes = slice(128 * number, 128 * number + 128)
        s_ref[0:6, :, lanes] = side_ref[0, number]
        s_ref[6:14, :, lanes] = source_ref[number]
        s_ref[14:20, :, lanes] = side_ref[1, number]

    def begin(layer, _):
        first_ref[layer] = s_ref[layer] * scale_ref[layer]
        return 0

    lax.fori_loop(0, 20, begin, 0, unroll=True)

    def sides(ref, layer):
        u, wy, wz = ref[layer], wy_ref[layer], wz_ref[layer]
        total = wx_ref[layer] * ref[layer + 1] + wx_ref[layer - 1] * ref[layer - 1]
        total += wy * after(u, 0) + before(wy * u, 0)
        return u, total + wz * after(u, 1) + before(wz * u, 1)

    def correct(layer, _):
        u, total = sides(first_ref, layer)
        second_ref[layer] = u + scale_ref[layer] * (REST * s_ref[layer] + total)
        return 0

    lax.fori_loop(1, 19, correct, 0, unroll=True)

    def leave(layer, _):
        u, total = sides(second_ref, layer)
        res_ref[layer - 2] = s_ref[layer] - diag_ref[layer] * u + total
        return 0

    lax.fori_loop(2, 18, leave, 0, unroll=True)
    own = second_ref[6:14, 8:24, :]
    out_ref[...] = jnp.where(lax.axis_index("gz") == 0, own[:, :, :128], own[:, :, 128:])

    source = coarser(res_ref[...], pair_matrix(256), 0.5, rows_ref)
    scale, wx, wy, wz = mid_scale_ref[...], mid_wx_ref[...], mid_wy_ref[...], mid_wz_ref[...]
    first = source * scale
    total = neighbours(first, wx[1:-1], wy[1:-1], wz[1:-1])
    second = first[1:-1] + scale[1:-1] * (REST * source[1:-1] + total)
    total = neighbours(second, wx[2:-2], wy[2:-2], wz[2:-2])
    residue = source[2:-2] - mid_diag_ref[2:-2] * second[1:-1] + total
    source = coarser(residue, pair_matrix(128), 0.5, rows_ref)
    pay_ref[0:2] = source[:, 2:6]
    pay_ref[2:4] = (source * low_scale_ref[...])[:, 2:6]
    pay_ref[4:6] = low_h_ref[:, 2:6]


def deep_kernel(sizes, mid_ref, side_ref, out_ref, win_ref, rows_ref):
    gx, gy, core = (lax.axis_index(name) for name in ("gx", "gy", "gz"))
    win_ref[...] = jnp.zeros(win_ref.shape, F32)
    for number in range(3):
        for part in range(3):
            for place in range(5):
                block = (side_ref[0, place], mid_ref[place], side_ref[1, place])[part]
                win_ref[number, 2 * place : 2 * place + 2, 4 * part : 4 * part + 4] = block[
                    2 * number : 2 * number + 2
                ]
    source, first, h = win_ref[0], win_ref[1], win_ref[2]
    shape = (8, 16, 128)
    inside = within(shape, (gx * 2, gy * 4), -3, -4, (sizes[0] // 4, sizes[1] // 4))
    inside &= iota(shape, 1) < 12
    diagonal, scale, wx, wy, wz = prepare(h, inside, 64)
    total = neighbours(first, wx, wy, wz)
    second = first[1:-1] + scale * (REST * source[1:-1] + total)
    total = neighbours(second, wx[1:-1], wy[1:-1], wz[1:-1])
    residue = source[2:-2] - diagonal[1:-1] * second[1:-1] + total

    zoom = pair_matrix(128)
    source = coarser(residue, zoom, 0.5, rows_ref)
    h = coarser(h, zoom, 0.125, rows_ref)
    inside = within(source.shape, (gx, gy * 2), -1, -2, (sizes[0] // 8, sizes[1] // 8))
    inside &= iota(source.shape, 1) < 6
    _, scale, wx, wy, wz = prepare(h, inside, 32)
    first = source * scale
    total = neighbours(first, wx[1:-1], wy[1:-1], wz[1:-1])
    second = first[1:-1] + scale[1:-1] * (REST * source[1:-1] + total)
    second = second[:, 2:4]
    out_ref[...] = jnp.where(core == 0, second[:, :, :16], second[:, :, 16:32])


def call(kernel, out_shape, in_specs, scratch=(), flops=100_000, outs=None, vmem=VMEM_BYTES):
    specs = {} if outs is None else {"out_specs": outs}
    return pl.pallas_call(
        kernel,
        out_shape=out_shape,
        scratch_shapes=list(scratch),
        compiler_params=pltpu.CompilerParams(vmem_limit_bytes=vmem),
        cost_estimate=pl.CostEstimate(flops=flops, bytes_accessed=flops, transcendentals=0),
        in_specs=in_specs,
        **specs,
    )


def split_send(values, axis, step):
    count = lax.axis_size(axis)
    pairs = []
    for place in range(count):
        if place + step < count:
            pairs.append((place * CORES, (place + step) * CORES))
        if place - step >= 0:
            pairs.append((place * CORES + 1, (place - step) * CORES + 1))
    return lax.ppermute(values, (axis, "gz"), pairs)


def shared(values):
    return lax.all_gather(values, "gz")


def per_device(fine_rhs, fine_coef, coarse_rhs, coarse_coef, patch_count, patch_target):
    core = lax.axis_index("gz")
    sizes = (
        lax.axis_size("gx") * coarse_rhs.shape[0],
        lax.axis_size("gy") * coarse_rhs.shape[1],
    )
    vmem = pl.BlockSpec(memory_space=pltpu.VMEM)
    smem = pl.BlockSpec(memory_space=pltpu.SMEM)
    struct = jax.ShapeDtypeStruct
    hbm = pl.BlockSpec(memory_space=pltpu.HBM)
    own_block = struct((2, *coarse_rhs.shape), F32)
    second, send, own = call(
        fine_kernel,
        (struct((16, 8, 128), F32), struct((128, 128), F32), own_block),
        [smem, hbm, hbm, hbm, hbm, hbm],
        [
            pltpu.VMEM((1, 32), jnp.int32),
            pltpu.VMEM(fine_rhs.shape, F32),
            pltpu.VMEM(fine_coef.shape, fine_coef.dtype),
            pltpu.VMEM(coarse_rhs.shape, F32),
            pltpu.VMEM(coarse_coef.shape, coarse_coef.dtype),
            pltpu.SemaphoreType.DMA((5,)),
        ],
        outs=[vmem] * 3,
        vmem=MOST_VMEM,
    )(patch_count, patch_target.reshape(1, 32), fine_rhs, fine_coef, coarse_rhs, coarse_coef)
    fine_solution = call(store_kernel, struct(fine_rhs.shape, F32), [smem, vmem])(
        patch_count, second
    )
    got = lax.all_to_all(send.reshape(16, 8, 128), ("gy", "gz"), 0, 0).reshape(128, 128)
    chip = shared(own)
    halo = shared(split_send(jnp.where(core == 0, chip[:, :, :, 8:], chip[:, :, :, :8]), "gy", 1))
    chip = jnp.concatenate([halo[0], chip, halo[1]], axis=3)
    edge = jnp.where(core == 0, chip[:, 1, 1:], chip[:, 1, :7])
    edge = split_send(edge[:, :4] * (1024.0 * PACK) + edge[:, 3:] * 1024.0, "gx", 1)
    source, pay = call(
        place_kernel,
        (struct((2, 8, 32, 128), F32), struct((2, 6, 32, 128), F32)),
        [vmem, vmem],
        outs=[vmem] * 2,
    )(got, chip)
    grid = (32, 256)
    window = struct((20, *grid), F32)
    block = struct((8, 16, 128), F32)
    low = struct((2, 8, 128), F32)
    weights = call(
        functools.partial(weight_kernel, sizes),
        (window,) * 5 + (struct((9, 16, 128), F32),) + (block,) * 4 + (low,) * 2,
        [vmem, vmem],
        [pltpu.VMEM((22, *grid), F32), pltpu.VMEM((320, 128), F32)],
        flops=5_000_000,
        outs=[vmem] * 12,
    )(chip, shared(edge))
    moved, last = lax.optimization_barrier((split_send(pay, "gx", 1), weights[-1]))
    side = shared(moved)
    coarse_solution, pay = call(
        base_kernel,
        (block, struct((6, 4, 128), F32)),
        [vmem] * 14,
        [pltpu.VMEM((20, *grid), F32)] * 3
        + [pltpu.VMEM((16, *grid), F32), pltpu.VMEM((320, 128), F32)],
        flops=5_000_000,
        outs=[vmem] * 2,
    )(source, side, *weights[:-1], last)
    far = shared(jnp.stack([split_send(pay, "gx", 1), split_send(pay, "gx", 2)]))
    mid = jnp.stack([far[0, 1], far[0, 0], pay, far[1, 0], far[1, 1]])
    sides = shared(split_send(mid, "gy", 1))
    deep_solution = call(
        functools.partial(deep_kernel, sizes),
        struct((1, 2, 16), F32),
        [vmem, vmem],
        [pltpu.VMEM((3, 10, 16, 128), F32), pltpu.VMEM((320, 128), F32)],
    )(mid, sides)
    return (fine_solution, coarse_solution, deep_solution)


def solution(mesh):
    return jax.shard_map(
        per_device,
        mesh=mesh,
        in_specs=(
            P(("gx", "gy", "gz"), None, None),
            P(("gx", "gy", "gz"), None, None),
            P("gx", "gy", "gz"),
            P("gx", "gy", "gz"),
            P(("gx", "gy", "gz")),
            P(("gx", "gy", "gz")),
        ),
        out_specs=(P(("gx", "gy", "gz"), None, None), P("gx", "gy", "gz"), P("gx", "gy", "gz")),
        check_vma=False,
    )
```

```python
import functools

import jax
import jax.numpy as jnp
from jax import lax
from jax.experimental import pallas as pl
from jax.experimental.pallas import tpu as pltpu
from jax.sharding import PartitionSpec as P

DAMPING = 6.0 / 7.0
REST = 1.0 - DAMPING
F32 = jnp.float32
BF16 = jnp.bfloat16
CORES = 2
PACK = 2048.0
VMEM_BYTES = 40 * 1024 * 1024
MOST_VMEM = 60 * 1024 * 1024


def iota(shape, dim):
    return lax.broadcasted_iota(jnp.int32, shape, dim)


def split(values):
    high = values.astype(BF16)
    return high, (values - high.astype(F32)).astype(BF16)


def small(a, b):
    return jnp.dot(a.astype(BF16), b.astype(BF16), preferred_element_type=F32)


def dot(a, picks):
    high, low = split(a)
    return small(high, picks) + small(low, picks)


def pick(picks, a):
    high, low = split(a)
    return small(picks, high) + small(picks, low)


def turned(a, b):
    return lax.dot_general(
        a.astype(BF16), b, (((1,), (1,)), ((), ())), preferred_element_type=F32
    )


def after(values, axis):
    return pltpu.roll(values, values.shape[axis] - 1, axis)


def before(values, axis):
    return pltpu.roll(values, 1, axis)


def inverse(values):
    guess = pl.reciprocal(values, approx=True)
    return guess * (2.0 - values * guess)


def fine_kernel(
    count_ref, target_hbm, rhs_hbm, coef_hbm, grid_hbm, cond_hbm, second_ref, send_ref, own_ref,
    target_ref, rhs_ref, coef_ref, grid_ref, cond_ref, sems
):
    live = count_ref[0]
    loads = [
        pltpu.make_async_copy(coef_hbm, coef_ref, sems.at[0]),
        pltpu.make_async_copy(rhs_hbm, rhs_ref, sems.at[1]),
        pltpu.make_async_copy(target_hbm, target_ref, sems.at[2]),
        pltpu.make_async_copy(grid_hbm, grid_ref, sems.at[3]),
        pltpu.make_async_copy(cond_hbm, cond_ref, sems.at[4]),
    ]
    for load in (loads[2], *loads[:2], *loads[3:]):
        load.start()
    loads[2].wait()
    wide = (32, 256)
    spread = jnp.where(iota(wide, 0) == (iota(wide, 1) >> 3), 1.0, 0.0)
    names = jnp.broadcast_to(target_ref[...].astype(F32), (8, 32))
    name = (dot(names, spread)[:1] + 0.5).astype(jnp.int32)
    names = jnp.broadcast_to(name, wide)
    row, col = iota(wide, 0), iota(wide, 1)
    own = jnp.sum(jnp.where(col == row * 8, names, 0).astype(F32), axis=1, keepdims=True)
    own = own.astype(jnp.int32)
    earlier = ((own >> 8) == (names >> 8)) & (row < (col >> 3))
    rank = jnp.sum(jnp.where(earlier, 1.0, 0.0), axis=0, keepdims=True).astype(jnp.int32)
    wide = (128, 256)
    row, col = iota(wide, 0), iota(wide, 1)
    chip = (row >> 4) + ((row >> 1) & 3) - 1
    owner = chip * 2 + (row & 1)
    wanted = ((row & 7) < 6) & (chip >= 0) & (chip < 8) & ((col >> 3) < live)
    chosen = wanted & (owner == (name >> 8))
    picked, tags = [], []
    for number in range(2):
        mine = chosen & (rank == number)
        picked.append(jnp.where(mine, 1.0, 0.0))
        tag = jnp.where(mine & ((col & 7) == 0), (name & 255) + 1, 0).astype(F32)
        tags.append(jnp.sum(tag, axis=1, keepdims=True))
    half = rhs_ref.shape[0] // 2
    loads[0].wait()
    k = coef_ref[...].astype(F32) * 0.5
    h = jnp.concatenate([k[:half], k[half:]], axis=2)
    shape = h.shape
    x, lane = iota(shape, 1), iota(shape, 2)
    y, z = (lane >> 3) & 7, lane & 7

    def wrapped(values, amount):
        return pltpu.roll(values, amount % 128, 2)

    hx = jnp.where(x < 7, after(h, 1), 0.0)
    hy = jnp.where(y < 7, wrapped(h, -8), 0.0)
    hz = jnp.where(z < 7, wrapped(h, -1), 0.0)
    diagonal = 6.0 * h + hx + hy + hz
    diagonal += jnp.where(x > 0, before(h, 1), 0.0)
    diagonal += jnp.where(y > 0, wrapped(h, 8), 0.0)
    diagonal += jnp.where(z > 0, wrapped(h, 1), 0.0)
    wx = jnp.where(x < 7, h + hx, 0.0)
    wy = jnp.where(y < 7, h + hy, 0.0)
    wz = jnp.where(z < 7, h + hz, 0.0)

    def sides(u):
        total = wx * after(u, 1) + before(wx * u, 1)
        total += wy * wrapped(u, -8) + wrapped(wy * u, 8)
        return total + wz * wrapped(u, -1) + wrapped(wz * u, 1)

    scale = DAMPING * inverse(diagonal)
    loads[1].wait()
    source = jnp.concatenate([rhs_ref[:half], rhs_ref[half:]], axis=2)
    first = source * scale
    second = first + scale * (REST * source + sides(first))
    residue = source - diagonal * second + sides(second)
    second_ref[...] = second

    square = (128, 128)
    row, col = iota(square, 0), iota(square, 1)
    iz, ix, iy = (col >> 4) & 3, (col >> 2) & 3, col & 3
    match = (((row >> 4) & 3) == iy) & (((row >> 1) & 3) == iz)
    keep = ((row >> 1) & 3) == ix
    cells = residue.reshape(square)
    parts = []
    for number in range(2):
        gather = jnp.where(match & ((row >> 6) == number), 0.5, 0.0)
        parts.append(jnp.where(keep, dot(cells, gather), 0.0))

    packed = [pick(mine[:, :128], parts[0]) + pick(mine[:, 128:], parts[1]) for mine in picked]
    row, col = iota(square, 0), iota(square, 1)
    place = (row & 7) * 2
    tags = jnp.where(col == place, tags[0], 0.0) + jnp.where(col == place + 1, tags[1], 0.0)
    lift = jnp.where(((row & 7) == 6) & ((row >> 3) == (col >> 3)), 1.0, 0.0)
    send_ref[...] = jnp.where(col < 64, packed[0], packed[1]) + small(lift, tags)
    loads[3].wait()
    loads[4].wait()
    own_ref[0] = grid_ref[...]
    own_ref[1] = cond_ref[...].astype(F32) * 0.5


def store_kernel(count_ref, second_ref, solved_ref):
    live = count_ref[0]
    second = second_ref[...]
    half = second.shape[0]
    slot = iota((half, 8, 64), 0)
    solved_ref[:half] = jnp.where(slot < live, second[:, :, :64], 0.0)
    solved_ref[half:] = jnp.where(slot + half < live, second[:, :, 64:], 0.0)


def place_kernel(got_ref, chip_ref, source_ref, pay_ref):
    first = jnp.where(lax.axis_index("gz") == 0, 2, 0)
    square = (128, 128)
    row, col = iota(square, 0), iota(square, 1)
    slot = (row >> 4) & 1
    tags = jnp.concatenate([got_ref[pl.ds(6, 16, stride=8), :]] * 8, axis=0)
    tags = jnp.where((col & 1) == slot, tags, 0.0).astype(BF16)
    some = (16, 128)
    across = turned(jnp.where((iota(some, 1) >> 1) == iota(some, 0), 1.0, 0.0), tags)
    across = (across + 0.5).astype(jnp.int32) - 1
    wide = (128, 768)
    spread = jnp.where((iota(wide, 0) >> 1) == (iota(wide, 1) >> 7), 1.0, 0.0)
    down = (small(tags, spread) + 0.5).astype(jnp.int32) - 1
    lane = iota(wide, 1)
    right = ((down & 31) == ((lane & 127) >> 2)) & ((lane & 3) == (iota(wide, 0) >> 5))
    right = jnp.where(right, 1.0, 0.0).astype(BF16)
    mask = (col >> 4) == slot * 4 + (row >> 5)
    some = (32, 128)
    cell = (iota(some, 0) >> 3) * 4 + (iota(some, 0) & 3)
    select = jnp.where((iota(some, 1) & 15) == cell, 1.0, 0.0)
    half = iota((8, 128), 0) >> 2

    def place(owner, tiles):
        got = got_ref[pl.ds(owner, 16, stride=8), :]
        slices = jnp.where(mask, jnp.concatenate([got] * 8, axis=0), 0.0)
        high, low = split(slices)
        left = turned(select, high) + turned(select, low)
        name = jnp.broadcast_to(across[owner : owner + 1], (8, 128))
        here = {
            (x, t): ((name >> 7) == x) & (((name >> 5) & 3) == 2 * t + half)
            for x in range(2)
            for t in tiles
        }
        places = [(x, t) for x in range(8) for t in tiles]
        values = jnp.concatenate(
            [jnp.where(here[x >> 2, t], left[8 * (x & 3) : 8 * (x & 3) + 8], 0.0) for x, t in places],
            axis=0,
        )
        marks = jnp.concatenate(
            [jnp.where(here[x >> 2, t], 1.0, 0.0) for x, t in places if x % 4 == 0], axis=0
        )
        put = right[:, 128 * owner : 128 * owner + 128]
        placed = dot(values, put).reshape(8, 8 * len(tiles), 128)
        covered = small(marks, put).reshape(2, 8 * len(tiles), 128) > 0.5
        return placed, covered

    for number in range(2):
        for part, (tiles, start) in enumerate((((1,), 0), ((0, 1), 8), ((0,), 24))):
            placed, covered = place(2 * part + number, tiles)
            lines = slice(start, start + 8 * len(tiles))
            old = chip_ref[number, 0, :, lines]
            for x in range(2):
                four = slice(4 * x, 4 * x + 4)
                source_ref[number, four, lines] = jnp.where(covered[x], placed[four], old[four])
    for number in range(2):
        pay_ref[number] = source_ref[number, pl.ds(first, 6)]


def pair_matrix(size):
    shape = (size, 128)
    return jnp.where((iota(shape, 0) >> 1) == iota(shape, 1), 1.0, 0.0)


def prepare(h, inside, depth):
    mid = h[1:-1]
    lane = iota(mid.shape, 2)
    hy = after(mid, 1)
    hz = jnp.where(lane < depth - 1, after(mid, 2), 0.0)
    diagonal = 6.0 * mid + h[:-2] + h[2:] + hy + before(mid, 1) + hz
    diagonal += jnp.where(lane > 0, before(mid, 2), 0.0)
    scale = jnp.where(inside & (lane < depth), DAMPING * inverse(diagonal), 0.0)
    wx = h[:-1] + h[1:]
    wy = mid + hy
    wz = jnp.where(lane < depth - 1, mid + hz, 0.0)
    return diagonal, scale, wx, wy, wz


def neighbours(u, wx, wy, wz):
    mid = u[1:-1]
    total = wx[1:] * u[2:] + wx[:-1] * u[:-2]
    total += wy * after(mid, 1) + before(wy * mid, 1)
    return total + wz * after(mid, 2) + before(wz * mid, 2)


def within(shape, start, first_layer, first_row, sizes):
    x = iota(shape, 0) + (start[0] + first_layer)
    y = iota(shape, 1) + (start[1] + first_row)
    return (x >= 0) & (x < sizes[0]) & (y >= 0) & (y < sizes[1])


def coarser(values, matrix, scale, rows_ref):
    layers, rows, depth = values.shape
    values = values.reshape(layers // 2, 2, rows, depth)
    values = values[:, 0] + values[:, 1]
    flat = dot(values.reshape(layers // 2 * rows, depth), matrix) * scale
    count = flat.shape[0]
    rows_ref[:count] = flat
    total = rows_ref[pl.ds(0, count // 2, stride=2), :] + rows_ref[pl.ds(1, count // 2, stride=2), :]
    return total.reshape(layers // 2, rows // 2, 128)


def weight_kernel(
    sizes, chip_ref, side_ref,
    wx_ref, wy_ref, wz_ref, diag_ref, scale_ref,
    mid_wx_ref, mid_wy_ref, mid_wz_ref, mid_diag_ref, mid_scale_ref, low_scale_ref, low_h_ref,
    h_ref, rows_ref,
):
    gx, gy = lax.axis_index("gx"), lax.axis_index("gy")
    for number in range(2):
        lanes = slice(128 * number, 128 * number + 128)
        for place, part in ((0, 0), (15, 1)):
            both = side_ref[part, number]
            upper = jnp.floor(both * (1.0 / PACK))
            h_ref[place : place + 4, :, lanes] = upper * (1.0 / 1024.0)
            h_ref[place + 3 : place + 7, :, lanes] = (both - upper * PACK) * (1.0 / 1024.0)
        h_ref[7:15, :, lanes] = chip_ref[number, 1]
    shape = (32, 256)
    lane = iota(shape, 1)
    y = iota(shape, 0) + (gy * 16 - 8)
    rows_in = (y >= 0) & (y < sizes[1])

    def weigh(layer, _):
        h = h_ref[layer + 1]
        below, above = h_ref[layer], h_ref[layer + 2]
        hy = after(h, 0)
        hz = jnp.where(lane < 255, after(h, 1), 0.0)
        diagonal = 6.0 * h + below + above + hy + before(h, 0) + hz
        diagonal += jnp.where(lane > 0, before(h, 1), 0.0)
        x = gx * 8 + layer - 6
        inside = rows_in & (x >= 0) & (x < sizes[0])
        diag_ref[layer] = diagonal
        scale_ref[layer] = jnp.where(inside, DAMPING * inverse(diagonal), 0.0)
        wx_ref[layer] = h + above
        wy_ref[layer] = h + hy
        wz_ref[layer] = jnp.where(lane < 255, h + hz, 0.0)
        return 0

    lax.fori_loop(0, 20, weigh, 0, unroll=True)
    h = coarser(h_ref[1:21], pair_matrix(256), 0.125, rows_ref)
    inside = within((8, 16, 128), (gx * 4, gy * 8), -2, -4, (sizes[0] // 2, sizes[1] // 2))
    diagonal, scale, wx, wy, wz = prepare(h, inside, 128)
    mid_wx_ref[...] = wx
    mid_wy_ref[...] = wy
    mid_wz_ref[...] = wz
    mid_diag_ref[...] = diagonal
    mid_scale_ref[...] = scale
    h = coarser(h[1:-1], pair_matrix(128), 0.125, rows_ref)
    _, scale, _, _, _ = prepare(h, jnp.full((2, 8, 128), True), 64)
    low_scale_ref[...] = scale
    low_h_ref[...] = h[1:3]


def base_kernel(
    source_ref, side_ref,
    wx_ref, wy_ref, wz_ref, diag_ref, scale_ref,
    mid_wx_ref, mid_wy_ref, mid_wz_ref, mid_diag_ref, mid_scale_ref, low_scale_ref, low_h_ref,
    out_ref, pay_ref, s_ref, first_ref, second_ref, res_ref, rows_ref,
):
    for number in range(2):
        lanes = slice(128 * number, 128 * number + 128)
        s_ref[0:6, :, lanes] = side_ref[0, number]
        s_ref[6:14, :, lanes] = source_ref[number]
        s_ref[14:20, :, lanes] = side_ref[1, number]

    def begin(layer, _):
        first_ref[layer] = s_ref[layer] * scale_ref[layer]
        return 0

    lax.fori_loop(0, 20, begin, 0, unroll=True)

    def sides(ref, layer):
        u, wy, wz = ref[layer], wy_ref[layer], wz_ref[layer]
        total = wx_ref[layer] * ref[layer + 1] + wx_ref[layer - 1] * ref[layer - 1]
        total += wy * after(u, 0) + before(wy * u, 0)
        return u, total + wz * after(u, 1) + before(wz * u, 1)

    def correct(layer, _):
        u, total = sides(first_ref, layer)
        second_ref[layer] = u + scale_ref[layer] * (REST * s_ref[layer] + total)
        return 0

    lax.fori_loop(1, 19, correct, 0, unroll=True)

    def leave(layer, _):
        u, total = sides(second_ref, layer)
        res_ref[layer - 2] = s_ref[layer] - diag_ref[layer] * u + total
        return 0

    lax.fori_loop(2, 18, leave, 0, unroll=True)
    own = second_ref[6:14, 8:24, :]
    out_ref[...] = jnp.where(lax.axis_index("gz") == 0, own[:, :, :128], own[:, :, 128:])

    source = coarser(res_ref[...], pair_matrix(256), 0.5, rows_ref)
    scale, wx, wy, wz = mid_scale_ref[...], mid_wx_ref[...], mid_wy_ref[...], mid_wz_ref[...]
    first = source * scale
    total = neighbours(first, wx[1:-1], wy[1:-1], wz[1:-1])
    second = first[1:-1] + scale[1:-1] * (REST * source[1:-1] + total)
    total = neighbours(second, wx[2:-2], wy[2:-2], wz[2:-2])
    residue = source[2:-2] - mid_diag_ref[2:-2] * second[1:-1] + total
    source = coarser(residue, pair_matrix(128), 0.5, rows_ref)
    pay_ref[0:2] = source[:, 2:6]
    pay_ref[2:4] = (source * low_scale_ref[...])[:, 2:6]
    pay_ref[4:6] = low_h_ref[:, 2:6]


def deep_kernel(sizes, mid_ref, side_ref, out_ref, win_ref, rows_ref):
    gx, gy, core = (lax.axis_index(name) for name in ("gx", "gy", "gz"))
    win_ref[...] = jnp.zeros(win_ref.shape, F32)
    for number in range(3):
        for part in range(3):
            blocks = [
                side_ref[0, 1, part], side_ref[0, 0, part], mid_ref[part],
                side_ref[1, 0, part], side_ref[1, 1, part],
            ]
            for place, block in enumerate(blocks):
                win_ref[number, 2 * place : 2 * place + 2, 4 * part : 4 * part + 4] = block[
                    2 * number : 2 * number + 2
                ]
    source, first, h = win_ref[0], win_ref[1], win_ref[2]
    shape = (8, 16, 128)
    inside = within(shape, (gx * 2, gy * 4), -3, -4, (sizes[0] // 4, sizes[1] // 4))
    inside &= iota(shape, 1) < 12
    diagonal, scale, wx, wy, wz = prepare(h, inside, 64)
    total = neighbours(first, wx, wy, wz)
    second = first[1:-1] + scale * (REST * source[1:-1] + total)
    total = neighbours(second, wx[1:-1], wy[1:-1], wz[1:-1])
    residue = source[2:-2] - diagonal[1:-1] * second[1:-1] + total

    zoom = pair_matrix(128)
    source = coarser(residue, zoom, 0.5, rows_ref)
    h = coarser(h, zoom, 0.125, rows_ref)
    inside = within(source.shape, (gx, gy * 2), -1, -2, (sizes[0] // 8, sizes[1] // 8))
    inside &= iota(source.shape, 1) < 6
    _, scale, wx, wy, wz = prepare(h, inside, 32)
    first = source * scale
    total = neighbours(first, wx[1:-1], wy[1:-1], wz[1:-1])
    second = first[1:-1] + scale[1:-1] * (REST * source[1:-1] + total)
    second = second[:, 2:4]
    out_ref[...] = jnp.where(core == 0, second[:, :, :16], second[:, :, 16:32])


def call(kernel, out_shape, in_specs, scratch=(), flops=100_000, outs=None, vmem=VMEM_BYTES):
    specs = {} if outs is None else {"out_specs": outs}
    return pl.pallas_call(
        kernel,
        out_shape=out_shape,
        scratch_shapes=list(scratch),
        compiler_params=pltpu.CompilerParams(vmem_limit_bytes=vmem),
        cost_estimate=pl.CostEstimate(flops=flops, bytes_accessed=flops, transcendentals=0),
        in_specs=in_specs,
        **specs,
    )


def split_send(values, axis, step):
    count = lax.axis_size(axis)
    pairs = []
    for place in range(count):
        if place + step < count:
            pairs.append((place * CORES, (place + step) * CORES))
        if place - step >= 0:
            pairs.append((place * CORES + 1, (place - step) * CORES + 1))
    return lax.ppermute(values, (axis, "gz"), pairs)


def shared(values):
    return lax.all_gather(values, "gz")


def per_device(fine_rhs, fine_coef, coarse_rhs, coarse_coef, patch_count, patch_target):
    core = lax.axis_index("gz")
    sizes = (
        lax.axis_size("gx") * coarse_rhs.shape[0],
        lax.axis_size("gy") * coarse_rhs.shape[1],
    )
    vmem = pl.BlockSpec(memory_space=pltpu.VMEM)
    smem = pl.BlockSpec(memory_space=pltpu.SMEM)
    struct = jax.ShapeDtypeStruct
    hbm = pl.BlockSpec(memory_space=pltpu.HBM)
    own_block = struct((2, *coarse_rhs.shape), F32)
    second, send, own = call(
        fine_kernel,
        (struct((16, 8, 128), F32), struct((128, 128), F32), own_block),
        [smem, hbm, hbm, hbm, hbm, hbm],
        [
            pltpu.VMEM((1, 32), jnp.int32),
            pltpu.VMEM(fine_rhs.shape, F32),
            pltpu.VMEM(fine_coef.shape, fine_coef.dtype),
            pltpu.VMEM(coarse_rhs.shape, F32),
            pltpu.VMEM(coarse_coef.shape, coarse_coef.dtype),
            pltpu.SemaphoreType.DMA((5,)),
        ],
        outs=[vmem] * 3,
        vmem=MOST_VMEM,
    )(patch_count, patch_target.reshape(1, 32), fine_rhs, fine_coef, coarse_rhs, coarse_coef)
    fine_solution = call(store_kernel, struct(fine_rhs.shape, F32), [smem, vmem])(
        patch_count, second
    )
    got = lax.all_to_all(send.reshape(16, 8, 128), ("gy", "gz"), 0, 0).reshape(128, 128)
    chip = shared(own)
    halo = shared(split_send(jnp.where(core == 0, chip[:, :, :, 8:], chip[:, :, :, :8]), "gy", 1))
    chip = jnp.concatenate([halo[0], chip, halo[1]], axis=3)
    edge = jnp.where(core == 0, chip[:, 1, 1:], chip[:, 1, :7])
    edge = split_send(edge[:, :4] * (1024.0 * PACK) + edge[:, 3:] * 1024.0, "gx", 1)
    source, pay = call(
        place_kernel,
        (struct((2, 8, 32, 128), F32), struct((2, 6, 32, 128), F32)),
        [vmem, vmem],
        outs=[vmem] * 2,
    )(got, chip)
    grid = (32, 256)
    window = struct((20, *grid), F32)
    block = struct((8, 16, 128), F32)
    low = struct((2, 8, 128), F32)
    weights = call(
        functools.partial(weight_kernel, sizes),
        (window,) * 5 + (struct((9, 16, 128), F32),) + (block,) * 4 + (low,) * 2,
        [vmem, vmem],
        [pltpu.VMEM((22, *grid), F32), pltpu.VMEM((320, 128), F32)],
        flops=5_000_000,
        outs=[vmem] * 12,
    )(chip, shared(edge))
    moved, last = lax.optimization_barrier((split_send(pay, "gx", 1), weights[-1]))
    side = shared(moved)
    coarse_solution, pay = call(
        base_kernel,
        (block, struct((6, 4, 128), F32)),
        [vmem] * 14,
        [pltpu.VMEM((20, *grid), F32)] * 3
        + [pltpu.VMEM((16, *grid), F32), pltpu.VMEM((320, 128), F32)],
        flops=5_000_000,
        outs=[vmem] * 2,
    )(source, side, *weights[:-1], last)
    halo = shared(split_send(pay, "gy", 1))
    mid = jnp.stack([halo[0], pay, halo[1]])
    sides = shared(jnp.stack([split_send(mid, "gx", 1), split_send(mid, "gx", 2)]))
    deep_solution = call(
        functools.partial(deep_kernel, sizes),
        struct((1, 2, 16), F32),
        [vmem, vmem],
        [pltpu.VMEM((3, 10, 16, 128), F32), pltpu.VMEM((320, 128), F32)],
    )(mid, sides)
    return (fine_solution, coarse_solution, deep_solution)


def solution(mesh):
    return jax.shard_map(
        per_device,
        mesh=mesh,
        in_specs=(
            P(("gx", "gy", "gz"), None, None),
            P(("gx", "gy", "gz"), None, None),
            P("gx", "gy", "gz"),
            P("gx", "gy", "gz"),
            P(("gx", "gy", "gz")),
            P(("gx", "gy", "gz")),
        ),
        out_specs=(P(("gx", "gy", "gz"), None, None), P("gx", "gy", "gz"), P("gx", "gy", "gz")),
        check_vma=False,
    )
```
